512 devices in a mesh: row: 4 (over z_lo, core), col: 16 (over x, z_hi), depth: 8 (over y).
Axes of the slice: x: 4, y: 8, z: 8 (z_hi: 4, z_lo: 2; z = z_hi * 2 + z_lo), core: 2. Of those that a mesh axis runs over, the one named last changes fastest.
Arguments:
- matrix: bfloat16 [8192, 8192], P('row', 'col'), may hold values from -6 to 6
- occupancy: int32 [128, 128], P('row', 'col'), may hold values 0 or 1
- filtering: int32 [128, 128], replicated, may hold values 0 or 1
Outputs:
- updated: bfloat16 [8192, 8192], P('row', ('col', 'depth'))
The draws below stay inside these ranges and needn't reach their ends.
All inputs are finite; a program needn't handle non-finite values. No bound on the sum of `occupancy` on one device may be relied on, other than what follows from the above.
Results may differ from the reference program's by a relative error of at most 0.0095.
Values may be sent and summed in bfloat16 or wider, within the bound.
No kernel may reach another device: no remote copies, remote signals or barrier semaphores. Data moves between devices by JAX's collectives and lax.ppermute only.
A program may use at most 64 MiB of HBM per device.

```python
import jax
import jax.numpy as jnp

BLK = 64
SUB = 64
ORDER = 8192
NB = 128
N_COL = 16
N_DEPTH = 8


def plant(values, key, low, high):
    longest = values.shape.index(max(values.shape))
    spots = []
    for shift in (0, 1):
        where = [jax.random.randint(jax.random.fold_in(key, axis), (), 0, length) for axis, length in enumerate(values.shape)]
        where[longest] = (where[longest] + shift) % values.shape[longest]
        spots.append(tuple(where))
    return values.at[spots[0]].set(low).at[spots[1]].set(high)


def block_scale(own_key, extent, cuts, low, high):
    gain = 1.0
    for dim, blocks in cuts:
        draws = jax.random.uniform(jax.random.fold_in(jax.random.fold_in(own_key, 6), dim), (blocks,), jnp.float32, low / len(cuts), high / len(cuts))
        gain = gain * jnp.repeat(jnp.exp(draws), extent[dim] // blocks).reshape((-1,) + (1,) * (len(extent) - 1 - dim))
    return gain


def gaussian(own_key, extent, scale, limit, split=(), kind=jnp.bfloat16):
    values = jax.random.normal(own_key, extent, jnp.float32) * scale
    if len(split) > 0:
        values = block_scale(own_key, extent, split, -0.22, 0.18) * values
    return jnp.clip(values, min=-limit, max=limit).astype(kind)


def setup_inputs(seed: int = 0) -> dict:
    arg_keys = jax.random.split(jax.random.key(seed), 4)
    matrix = gaussian(arg_keys[0], (ORDER, ORDER), 1.0, 6.0, ((0, 4), (1, 16)))
    occupancy = plant((jax.random.randint(arg_keys[1], (NB, NB), 0, 2) < 1).astype(jnp.int32), jax.random.fold_in(arg_keys[1], 1), 0, 1)
    filtering = plant((jax.random.randint(arg_keys[2], (NB, NB), 0, 4) < 3).astype(jnp.int32), jax.random.fold_in(arg_keys[2], 1), 0, 1)
    return {"matrix": matrix, "occupancy": occupancy, "filtering": filtering}


def expand(tile_table):
    tile_rows, tile_cols = tile_table.shape
    broadcasted = jnp.broadcast_to(tile_table[:, None, :, None], (tile_rows, BLK, tile_cols, BLK))
    return broadcasted.reshape(tile_rows * BLK, tile_cols * BLK)


def grouped_product(left_panel, right_panel, scale_factor):
    running_sum = jnp.zeros((ORDER, ORDER), jnp.float32)
    for group_index in range(N_DEPTH):
        left_part = left_panel.reshape(ORDER, N_COL, N_DEPTH, SUB)[:, :, group_index, :].reshape(ORDER, N_COL * SUB)
        right_part = right_panel.reshape(N_COL, N_DEPTH, SUB, ORDER)[:, group_index].reshape(N_COL * SUB, ORDER)
        group_term = (scale_factor * jnp.dot(left_part, right_part, preferred_element_type=jnp.float32)).astype(jnp.bfloat16)
        running_sum = running_sum + group_term.astype(jnp.float32)
    return running_sum


def reference(matrix, occupancy, filtering):
    scale_factor = (ORDER / 2.0) ** -0.5
    sparse = matrix * expand(occupancy.astype(matrix.dtype))
    square_sum = grouped_product(sparse, sparse, scale_factor)
    square = (square_sum * expand(filtering.astype(jnp.float32))).astype(jnp.bfloat16)
    cube_sum = grouped_product(sparse, square, scale_factor)
    return (1.5 * sparse.astype(jnp.float32) - 0.5 * cube_sum).astype(jnp.bfloat16)
```

```python
import functools

import jax
import jax.numpy as jnp
from jax import lax
from jax.experimental import pallas as pl
from jax.experimental.pallas import tpu as pltpu
from jax.sharding import PartitionSpec as P

BLK = 64
LANES = 128
HALVES = 2
RING = 4
BF16 = jnp.bfloat16
F32 = jnp.float32


def call(kernel, flops=0, moved=1 << 20, **kwargs):
    return pl.pallas_call(
        kernel,
        compiler_params=pltpu.CompilerParams(vmem_limit_bytes=40 << 20),
        cost_estimate=pl.CostEstimate(flops=flops, bytes_accessed=moved, transcendentals=0),
        **kwargs,
    )


def tile_mask(scalars):
    shape = (1, BLK * len(scalars))
    tile = lax.broadcasted_iota(jnp.int32, shape, 1) // BLK
    mask = jnp.zeros(shape, F32)
    for t, value in enumerate(scalars):
        mask = jnp.where(tile == t, value.astype(F32), mask)
    return mask


def prepare_kernel(depths, cycles, width, where, occ_t, rows, columns, right, *lefts):
    depth = where[0]
    tile_cols = rows.shape[3] // BLK
    for a in range(cycles):
        mask = tile_mask([occ_t[t, a * depths + depth] for t in range(tile_cols)])
        right[a * width : (a + 1) * width, :] = (rows[a, 0].astype(F32) * mask).astype(BF16)
    half = lax.rem(depth * width, LANES)
    pick = (
        lax.broadcasted_iota(jnp.int32, (width, LANES), 0) + half
        == lax.broadcasted_iota(jnp.int32, (width, LANES), 1)
    ).astype(BF16)
    per = cycles // HALVES
    for h, left in enumerate(lefts):
        order = [a * depths + d for d in range(depths) for a in range(h * per, (h + 1) * per)]
        stacked = jnp.concatenate([columns[t * width : (t + 1) * width, :] for t in order], axis=0)
        turned = lax.dot_general(
            pick, stacked, (((1,), (1,)), ((), ())), preferred_element_type=F32
        )
        left[...] = (turned * tile_mask([occ_t[depth, t] for t in order])).astype(BF16)


def prepare(matrix, occupancy, depths, depth):
    local_rows, local_cols = matrix.shape
    width = local_cols // depths
    cycles = local_rows // (depths * width)
    cut = matrix.reshape(cycles, depths, width, local_cols)
    piece = (width, local_rows // HALVES)
    return call(
        functools.partial(prepare_kernel, depths, cycles, width),
        out_shape=[jax.ShapeDtypeStruct((cycles * width, local_cols), BF16)]
        + [jax.ShapeDtypeStruct(piece, BF16)] * HALVES,
        grid_spec=pltpu.PrefetchScalarGridSpec(
            num_scalar_prefetch=2,
            grid=(1,),
            in_specs=[
                pl.BlockSpec((cycles, 1, width, local_cols), lambda i, where, occ: (0, where[0], 0, 0)),
                pl.BlockSpec((local_rows, LANES), lambda i, where, occ: (0, where[0] * width // LANES)),
            ],
            out_specs=[pl.BlockSpec((cycles * width, local_cols), lambda i, where, occ: (0, 0))]
            + [pl.BlockSpec(piece, lambda i, where, occ: (0, 0))] * HALVES,
        ),
    )(depth[None], occupancy.T, cut, matrix)


def product_kernel(n_right, parts, sources, scale, grouped, where, *refs):
    rights, lefts = refs[:n_right], refs[n_right:-3]
    out, whole, turned = refs[-3:]
    n_rows = n_right // parts
    row, x, z = where[1], where[2] // RING, lax.rem(where[2], RING)

    @pl.when(pl.program_id(0) == 0)
    def _():
        for q in range(n_rows):
            at = 0
            for part in rights[q * parts : (q + 1) * parts]:
                whole[row ^ q, at : at + part.shape[0], :] = part[...]
                at += part.shape[0]
        per = whole.shape[1] // BLK

        def chunk(n):
            dx, dz = sources[n]
            which = ((x + dx) & (RING - 1)) * RING + ((z + dz) & (RING - 1))
            start = pl.multiple_of(lax.rem(which, per) * BLK, BLK)
            return whole[which // per, pl.ds(start, BLK), :]

        for n in range(0, len(lefts), 2):
            pair = jnp.concatenate([chunk(n), chunk(n + 1)], axis=0)
            turned[:, n * BLK : (n + 2) * BLK] = pair.T

    left = jnp.concatenate([ref[...] for ref in lefts], axis=0)
    total = scale * jnp.dot(turned[...], left, preferred_element_type=F32)
    if grouped:
        lanes = out.shape[2]
        for s in range(out.shape[0]):
            out[s] = total[:, s * lanes : (s + 1) * lanes].astype(BF16)
    else:
        out[...] = total.astype(BF16)


def product(rights, pieces, where, scale, groups, grouped):
    sources, lefts = zip(*pieces)
    parts = len(rights[0])
    flat = [part for row in rights for part in row]
    cols = flat[0].shape[1]
    row_depth = sum(part.shape[0] for part in rights[0])
    width, lanes = lefts[0].shape
    block = 2 * (lanes // groups)
    depth = width * len(lefts)
    if grouped:
        out_shape, out_block = (groups, cols, lanes // groups), (2, cols, lanes // groups)
        place = lambda i, where: (i, 0, 0)
    else:
        out_shape, out_block = (cols, lanes), (cols, block)
        place = lambda i, where: (0, i)
    return call(
        functools.partial(product_kernel, len(flat), parts, sources, scale, grouped),
        flops=2 * cols * lanes * depth,
        moved=2 * (cols * depth + lanes * depth + cols * lanes),
        out_shape=jax.ShapeDtypeStruct(out_shape, BF16),
        grid_spec=pltpu.PrefetchScalarGridSpec(
            num_scalar_prefetch=1,
            grid=(lanes // block,),
            in_specs=[pl.BlockSpec(part.shape, lambda i, where: (0, 0)) for part in flat]
            + [pl.BlockSpec((width, block), lambda i, where: (0, i)) for _ in lefts],
            out_specs=pl.BlockSpec(out_block, place),
            scratch_shapes=[
                pltpu.VMEM((len(rights), row_depth, cols), BF16),
                pltpu.VMEM((cols, depth), BF16),
            ],
        ),
    )(where, *flat, *lefts)


def filter_kernel(depths, tile_rows, tile_cols, where, filtering, mask):
    lanes = mask.shape[1]
    spread = (
        lax.broadcasted_iota(jnp.int32, (filtering.shape[1], lanes), 0)
        == lax.broadcasted_iota(jnp.int32, (filtering.shape[1], lanes), 1) // BLK
        + where[2] * tile_cols
    ).astype(F32)
    for a in range(tile_rows // depths):
        row = filtering[pl.ds(where[1] * tile_rows + a * depths + where[0], 1), :].astype(F32)
        mask[pl.ds(a, 1), :] = jnp.dot(
            jnp.broadcast_to(row, (8, row.shape[1])), spread, preferred_element_type=F32
        )[:1]


def filter_rows(filtering, where, depths, tile_rows, tile_cols):
    return call(
        functools.partial(filter_kernel, depths, tile_rows, tile_cols),
        out_shape=jax.ShapeDtypeStruct((8, tile_cols * BLK), F32),
        grid_spec=pltpu.PrefetchScalarGridSpec(
            num_scalar_prefetch=1,
            grid=(1,),
            in_specs=[pl.BlockSpec(filtering.shape, lambda i, where: (0, 0))],
            out_specs=pl.BlockSpec((8, tile_cols * BLK), lambda i, where: (0, 0)),
        ),
    )(where, filtering)


def square_kernel(first, n_got, where, own, *refs):
    got, mask, out = refs[:n_got], refs[n_got], refs[n_got + 1]
    total = own[0].astype(F32)
    for ref in got:
        total = total + ref[...].astype(F32)
    turned = total.astype(BF16).T
    for a in range(turned.shape[0] // BLK):
        rows = turned[a * BLK : (a + 1) * BLK, :].astype(F32)
        out[a * BLK : (a + 1) * BLK, :] = (rows * mask[first + a : first + a + 1, :]).astype(BF16)


def square_rows(terms, got, mask, where, first):
    _, cols, rows = terms.shape
    return call(
        functools.partial(square_kernel, first, len(got)),
        out_shape=jax.ShapeDtypeStruct((rows, cols), BF16),
        grid_spec=pltpu.PrefetchScalarGridSpec(
            num_scalar_prefetch=1,
            grid=(1,),
            in_specs=[pl.BlockSpec((1, cols, rows), lambda i, where: (where[0], 0, 0))]
            + [pl.BlockSpec((cols, rows), lambda i, where: (0, 0)) for _ in got]
            + [pl.BlockSpec(mask.shape, lambda i, where: (0, 0))],
            out_specs=pl.BlockSpec((rows, cols), lambda i, where: (0, 0)),
        ),
    )(where, terms, *got, mask)


def update_kernel(depths, n_got, where, *refs):
    out = refs[-1]
    each = n_got + 2
    for h in range(HALVES):
        own, left, *got = refs[h * each : (h + 1) * each]
        cube = own[0].astype(F32)
        for ref in got:
            cube = cube + ref[...].astype(F32)
        new = 1.5 * left[...].astype(F32) - 0.5 * cube
        low = lax.broadcasted_iota(jnp.int32, (new.shape[0], LANES), 1) < BLK
        for d in range(0, depths, 2):
            one, two = (new[:, (d + s) * LANES : (d + s + 1) * LANES] for s in (0, 1))
            first = jnp.where(low, one, pltpu.roll(two, BLK, 1))
            second = jnp.where(low, pltpu.roll(one, BLK, 1), two)
            for a, value in enumerate((first, second)):
                at = ((h * 2 + a) * depths + d) * BLK
                out[:, at : at + LANES] = value.astype(BF16)


def update(halves, where, depths):
    _, width, lanes = halves[0][0].shape
    n_got = len(halves[0]) - 2
    specs = [pl.BlockSpec((1, width, lanes), lambda i, where: (where[0], 0, 0))]
    specs += [pl.BlockSpec((width, lanes), lambda i, where: (0, 0))] * (1 + n_got)
    return call(
        functools.partial(update_kernel, depths, n_got),
        out_shape=jax.ShapeDtypeStruct((width, lanes * HALVES), BF16),
        grid_spec=pltpu.PrefetchScalarGridSpec(
            num_scalar_prefetch=1,
            grid=(1,),
            in_specs=specs * HALVES,
            out_specs=pl.BlockSpec((width, lanes * HALVES), lambda i, where: (0, 0)),
        ),
    )(where, *[value for half in halves for value in half])


def shift_col(value, dx, dz):
    pairs = [
        (x * RING + z, (x + dx) % RING * RING + (z + dz) % RING)
        for x in range(RING)
        for z in range(RING)
    ]
    return lax.ppermute(value, "col", pairs)


def gather_pieces(piece, way):
    def ring(value, move):
        up, down = move(value, 1), move(value, -1)
        return up, down, move(up if way > 0 else down, way)

    along_z = ring(piece, lambda value, step: shift_col(value, 0, step))
    held = [(0, piece)] + list(zip((-1, 1, 2), along_z))
    pieces = []
    for dz, value in held:
        along_x = ring(value, lambda value, step: shift_col(value, step, 0))
        pieces += [((dx, dz), got) for dx, got in zip((0, -1, 1, 2), (value,) + along_x)]
    return pieces


def gather_rows(value):
    def swap(value, bit):
        return lax.ppermute(value, "row", [(r, r ^ bit) for r in range(4)])

    across = swap(value, 2)
    return [value, swap(value, 1), across, swap(across, 1)]


def ring_reduce(terms, depth, way):
    depths = terms.shape[0]
    long = depths // 2
    got = []
    for step, hops in ((way, long), (-way, depths - 1 - long)):
        if hops == 0:
            continue
        pairs = [(d, (d + step) % depths) for d in range(depths)]

        def term(ahead):
            place = (depth + step * ahead + depths).astype(jnp.uint32) & (depths - 1)
            zero = jnp.uint32(0)
            return lax.dynamic_slice(terms, (place, zero, zero), (1,) + terms.shape[1:])[0]

        value = term(hops)
        for left in range(hops - 1, -1, -1):
            value = lax.ppermute(value, "depth", pairs)
            if left:
                value = (value.astype(F32) + term(left).astype(F32)).astype(BF16)
        got.append(value)
    return got


def shards(matrix, occupancy, filtering):
    rows = lax.axis_size("row")
    depths = lax.axis_size("depth")
    row, col, depth = (lax.axis_index(name) for name in ("row", "col", "depth"))
    local_rows, local_cols = matrix.shape
    scale = (local_rows * rows / 2.0) ** (-0.5)
    width = local_cols // depths
    where = jnp.stack([depth, row, col]).astype(jnp.int32)

    right, *lefts = prepare(matrix, occupancy, depths, depth)
    gathered = [gather_pieces(left, way) for left, way in zip(lefts, (1, -1))]
    mask = filter_rows(filtering, where, depths, local_rows // BLK, local_cols // BLK)

    rights = [[value] for value in gather_rows(right)]
    per = local_rows // (depths * width * HALVES)
    squares = []
    for h, way in enumerate((1, -1)):
        terms = product(rights, gathered[h], where, scale, depths, True)
        got = ring_reduce(terms, depth, way)
        squares.append(square_rows(terms, got, mask, where, h * per))

    rights = list(zip(*[gather_rows(square) for square in squares]))
    halves = []
    for h, way in enumerate((1, -1)):
        terms = product(rights, gathered[h], where, scale, depths, False)
        terms = terms.reshape(depths, width, -1)
        halves.append([terms, lefts[h]] + ring_reduce(terms, depth, way))
    return update(halves, where, depths).T


def solution(mesh):
    placed = (P("row", "col"), P("row", "col"), P())
    return jax.shard_map(
        shards, mesh=mesh, in_specs=placed, out_specs=P("row", ("col", "depth")), check_vma=False
    )
```

```python
import functools

import jax
import jax.numpy as jnp
from jax import lax
from jax.experimental import pallas as pl
from jax.experimental.pallas import tpu as pltpu
from jax.sharding import PartitionSpec as P

BLK = 64
LANES = 128
HALVES = 2
RING = 4
ALONG_Z = [[x * RING + z for z in range(RING)] for x in range(RING)]
ALONG_X = [[x * RING + z for x in range(RING)] for z in range(RING)]
BF16 = jnp.bfloat16
F32 = jnp.float32
F16 = jnp.float16


def call(kernel, flops=0, moved=1 << 20, **kwargs):
    return pl.pallas_call(
        kernel,
        compiler_params=pltpu.CompilerParams(vmem_limit_bytes=40 << 20),
        cost_estimate=pl.CostEstimate(flops=flops, bytes_accessed=moved, transcendentals=0),
        **kwargs,
    )


def tile_mask(scalars):
    shape = (1, BLK * len(scalars))
    tile = lax.broadcasted_iota(jnp.int32, shape, 1) // BLK
    mask = jnp.zeros(shape, F32)
    for t, value in enumerate(scalars):
        mask = jnp.where(tile == t, value.astype(F32), mask)
    return mask


def prepare_kernel(depths, cycles, width, where, occ_t, rows, columns, right, *lefts):
    depth = where[0]
    tile_cols = rows.shape[3] // BLK
    parts = []
    for a in range(cycles):
        mask = tile_mask([occ_t[t, a * depths + depth] for t in range(tile_cols)])
        parts.append((rows[a, 0].astype(F32) * mask).astype(BF16))
    right[...] = jnp.concatenate(parts, axis=0).T
    half = lax.rem(depth * width, LANES)
    pick = (
        lax.broadcasted_iota(jnp.int32, (width, LANES), 0) + half
        == lax.broadcasted_iota(jnp.int32, (width, LANES), 1)
    ).astype(BF16)
    per = cycles // HALVES
    for h, left in enumerate(lefts):
        order = [a * depths + d for d in range(depths) for a in range(h * per, (h + 1) * per)]
        stacked = jnp.concatenate([columns[t * width : (t + 1) * width, :] for t in order], axis=0)
        turned = lax.dot_general(
            pick, stacked, (((1,), (1,)), ((), ())), preferred_element_type=F32
        )
        left[...] = (turned * tile_mask([occ_t[depth, t] for t in order])).astype(BF16)


def prepare(matrix, occupancy, depths, where):
    local_rows, local_cols = matrix.shape
    width = local_cols // depths
    cycles = local_rows // (depths * width)
    cut = matrix.reshape(cycles, depths, width, local_cols)
    piece = (width, local_rows // HALVES)
    return call(
        functools.partial(prepare_kernel, depths, cycles, width),
        out_shape=[jax.ShapeDtypeStruct((local_cols, cycles * width), BF16)]
        + [jax.ShapeDtypeStruct(piece, BF16)] * HALVES,
        grid_spec=pltpu.PrefetchScalarGridSpec(
            num_scalar_prefetch=2,
            grid=(1,),
            in_specs=[
                pl.BlockSpec((cycles, 1, width, local_cols), lambda i, where, occ: (0, where[0], 0, 0)),
                pl.BlockSpec((local_rows, LANES), lambda i, where, occ: (0, where[0] * width // LANES)),
            ],
            out_specs=[pl.BlockSpec((local_cols, cycles * width), lambda i, where, occ: (0, 0))]
            + [pl.BlockSpec(piece, lambda i, where, occ: (0, 0))] * HALVES,
        ),
    )(where, occupancy.T, cut, matrix)


def product_kernel(n_right, scale, cuts, *refs):
    rights, left, outs, whole = refs[:n_right], refs[n_right], refs[n_right + 1 : -1], refs[-1]

    @pl.when(pl.program_id(0) == 0)
    def _():
        at = 0
        for row in range(rights[0].shape[0]):
            for part in rights:
                whole[:, at : at + part.shape[2]] = part[row]
                at += part.shape[2]

    total = scale * jnp.dot(whole[...], left[...], preferred_element_type=F32)
    if cuts is None:
        outs[0][...] = total.astype(BF16)
    else:
        for out, (low, high) in zip(outs, cuts):
            lanes = out.shape[2]
            for s in range(out.shape[0]):
                out[s] = total[low:high, s * lanes : (s + 1) * lanes].astype(BF16)


def product(rights, left, scale, groups, cuts):
    cols = rights[0].shape[1]
    depth, lanes = left.shape
    each = lanes // groups
    if cuts is None:
        out_shape = [jax.ShapeDtypeStruct((cols, lanes), BF16)]
        out_specs = [pl.BlockSpec((cols, 2 * each), lambda i: (0, i))]
    else:
        out_shape = [jax.ShapeDtypeStruct((groups, high - low, each), BF16) for low, high in cuts]
        out_specs = [pl.BlockSpec((2, high - low, each), lambda i: (i, 0, 0)) for low, high in cuts]
    return call(
        functools.partial(product_kernel, len(rights), scale, cuts),
        flops=2 * cols * lanes * depth,
        moved=2 * (cols * depth + lanes * depth + cols * lanes),
        out_shape=out_shape,
        grid=(groups // 2,),
        in_specs=[pl.BlockSpec(part.shape, lambda i: (0, 0, 0)) for part in rights]
        + [pl.BlockSpec((depth, 2 * each), lambda i: (0, i))],
        out_specs=out_specs,
        scratch_shapes=[pltpu.VMEM((cols, depth), BF16)],
    )(*rights, left)


def filter_kernel(depths, tile_rows, tile_cols, where, filtering, mask):
    cols, lanes = mask.shape
    tiles = filtering.shape[0]
    row = lax.broadcasted_iota(jnp.int32, (tiles, lanes), 1) // BLK * depths
    rows = lax.broadcasted_iota(jnp.int32, (tiles, lanes), 0) == (
        row + where[1] * tile_rows + where[0]
    )
    col = lax.broadcasted_iota(jnp.int32, (cols, tiles), 0) // BLK + where[2] * tile_cols
    cols_of = lax.broadcasted_iota(jnp.int32, (cols, tiles), 1) == col
    spread = lax.dot_general(
        filtering[...].astype(F32), rows.astype(F32), (((0,), (0,)), ((), ())),
        preferred_element_type=F32,
    )
    mask[...] = jnp.dot(cols_of.astype(F32), spread, preferred_element_type=F32).astype(BF16)


def filter_mask(filtering, where, depths, tile_rows, tile_cols):
    shape = (tile_cols * BLK, tile_rows // depths * BLK)
    return call(
        functools.partial(filter_kernel, depths, tile_rows, tile_cols),
        out_shape=jax.ShapeDtypeStruct(shape, BF16),
        grid_spec=pltpu.PrefetchScalarGridSpec(
            num_scalar_prefetch=1,
            grid=(1,),
            in_specs=[pl.BlockSpec(filtering.shape, lambda i, where: (0, 0))],
            out_specs=pl.BlockSpec(shape, lambda i, where: (0, 0)),
        ),
    )(where, filtering)


def sum_of(ref):
    if len(ref.shape) == 2:
        return ref[...].astype(F32)
    total = ref[0].astype(F32)
    for i in range(1, ref.shape[0]):
        total = total + ref[i].astype(F32)
    return total


def square_kernel(*refs):
    *parts, mask, out = refs
    low = 0
    for part in parts:
        high = low + part.shape[-2]
        keep = mask[low:high, :].astype(F32)
        out[low:high, :] = (sum_of(part) * keep).astype(BF16)
        low = high


def square_part(parts, mask, h):
    cols, lanes = mask.shape
    lanes //= HALVES

    def whole(part):
        return pl.BlockSpec(part.shape, lambda i: (0,) * part.ndim)

    return call(
        square_kernel,
        out_shape=jax.ShapeDtypeStruct((cols, lanes), BF16),
        grid=(1,),
        in_specs=[whole(part) for part in parts] + [pl.BlockSpec((cols, lanes), lambda i: (0, h))],
        out_specs=pl.BlockSpec((cols, lanes), lambda i: (0, 0)),
    )(*parts, mask)


def update_kernel(depths, *refs):
    out = refs[-1]
    for h in range(HALVES):
        left, terms = refs[2 * h : 2 * h + 2]
        new = 1.5 * left[...].astype(F32) - 0.5 * sum_of(terms)
        low = lax.broadcasted_iota(jnp.int32, (new.shape[0], LANES), 1) < BLK
        for d in range(0, depths, 2):
            one, two = (new[:, (d + s) * LANES : (d + s + 1) * LANES] for s in (0, 1))
            first = jnp.where(low, one, pltpu.roll(two, BLK, 1))
            second = jnp.where(low, pltpu.roll(one, BLK, 1), two)
            for a, value in enumerate((first, second)):
                at = ((h * 2 + a) * depths + d) * BLK
                out[:, at : at + LANES] = value.astype(BF16)


def update(values, depths):
    width, lanes = values[0].shape
    return call(
        functools.partial(update_kernel, depths),
        out_shape=jax.ShapeDtypeStruct((width, lanes * HALVES), BF16),
    )(*values)


def gather_col(piece):
    piece = lax.all_gather(piece.astype(F16), "col", axis=0, tiled=True, axis_index_groups=ALONG_Z)
    piece = lax.all_gather(piece, "col", axis=0, tiled=True, axis_index_groups=ALONG_X)
    return piece.astype(BF16)


def add_over_depth(terms):
    return lax.psum_scatter(terms, "depth", scatter_dimension=0, tiled=False)


def trade_over_depth(terms):
    return lax.all_to_all(terms, "depth", 0, 0, tiled=True)


def shards(matrix, occupancy, filtering):
    rows = lax.axis_size("row")
    depths = lax.axis_size("depth")
    row, col, depth = (lax.axis_index(name) for name in ("row", "col", "depth"))
    local_rows, local_cols = matrix.shape
    scale = (local_rows * rows / 2.0) ** (-0.5)
    width = local_cols // depths
    where = jnp.stack([depth, row, col]).astype(jnp.int32)

    right, one, two = prepare(matrix, occupancy, depths, where)
    mask = filter_mask(filtering, where, depths, local_rows // BLK, local_cols // BLK)
    rights = [lax.all_gather(right, "row", axis=0)]
    middle = local_cols // 2

    left_one = gather_col(one)
    [terms_one] = product(rights, left_one, scale, depths, ((0, local_cols),))
    sum_one = add_over_depth(terms_one)
    two, terms_one = lax.optimization_barrier((two, terms_one))
    sum_one, left_two = lax.optimization_barrier((sum_one, gather_col(two)))
    terms_two = product(rights, left_two, scale, depths, ((0, middle), (middle, local_cols)))
    sum_two = add_over_depth(terms_two[0])
    sum_one, parts_two = lax.optimization_barrier((sum_one, trade_over_depth(terms_two[1])))
    squares = [
        lax.all_gather(square_part(parts, mask, h).astype(F16), "row", axis=0).astype(BF16)
        for h, parts in enumerate(([sum_one], [sum_two, parts_two]))
    ]

    [cube_one] = product(squares, left_one, scale, depths, None)
    [cube_two] = product(squares, left_two, scale, depths, None)
    cube_one = add_over_depth(cube_one.reshape(depths, width, -1))
    cube_two = trade_over_depth(cube_two.reshape(depths, width, -1))
    return update((one, cube_one, two, cube_two), depths).T


def solution(mesh):
    placed = (P("row", "col"), P("row", "col"), P())
    return jax.shard_map(
        shards, mesh=mesh, in_specs=placed, out_specs=P("row", ("col", "depth")), check_vma=False
    )
```

```python
import functools

import jax
import jax.numpy as jnp
from jax import lax
from jax.experimental import pallas as pl
from jax.experimental.pallas import tpu as pltpu
from jax.sharding import PartitionSpec as P

BLK = 64
LANES = 128
RING = 4
ALONG_Z = [[x * RING + z for z in range(RING)] for x in range(RING)]
ALONG_X = [[x * RING + z for x in range(RING)] for z in range(RING)]
BF16 = jnp.bfloat16
F32 = jnp.float32
F16 = jnp.float16


def call(kernel, flops=0, moved=1 << 20, **kwargs):
    return pl.pallas_call(
        kernel,
        compiler_params=pltpu.CompilerParams(vmem_limit_bytes=40 << 20),
        cost_estimate=pl.CostEstimate(flops=flops, bytes_accessed=moved, transcendentals=0),
        **kwargs,
    )


def tile_mask(scalars):
    shape = (1, BLK * len(scalars))
    tile = lax.broadcasted_iota(jnp.int32, shape, 1) // BLK
    mask = jnp.zeros(shape, F32)
    for t, value in enumerate(scalars):
        mask = jnp.where(tile == t, value.astype(F32), mask)
    return mask


def prepare_kernel(pairs, cycles, where, occ_t, rows, columns, right, left):
    pair, side = where[0] // 2, lax.rem(where[0], 2)
    tile_cols = rows.shape[3] // BLK
    parts = []
    for s in range(2):
        for a in range(cycles):
            tile_row = (a * pairs + pair) * 2 + s
            mask = tile_mask([occ_t[t, tile_row] for t in range(tile_cols)])
            part = rows[a, 0, s * BLK : (s + 1) * BLK, :].astype(F32)
            parts.append((part * mask).astype(BF16))
    right[...] = jnp.concatenate(parts, axis=0).T
    order = [a * pairs + q for q in range(pairs) for a in range(cycles)]
    stacked = jnp.concatenate([columns[t, 0] for t in order], axis=0)
    turned = stacked.T
    for s in range(2):
        mask = tile_mask([occ_t[pair * 2 + s, t * 2 + side] for t in order])
        part = turned[s * BLK : (s + 1) * BLK, :].astype(F32)
        left[s * BLK : (s + 1) * BLK, :] = (part * mask).astype(BF16)


def prepare(matrix, occupancy, pairs, where):
    local_rows, local_cols = matrix.shape
    cycles = local_rows // (pairs * 2 * BLK)
    right = (local_cols, cycles * 2 * BLK)
    left = (2 * BLK, local_rows // 2)
    return call(
        functools.partial(prepare_kernel, pairs, cycles),
        out_shape=[jax.ShapeDtypeStruct(right, BF16), jax.ShapeDtypeStruct(left, BF16)],
        grid_spec=pltpu.PrefetchScalarGridSpec(
            num_scalar_prefetch=2,
            grid=(1,),
            in_specs=[
                pl.BlockSpec(
                    (cycles, 1, 2 * BLK, local_cols), lambda i, where, occ: (0, where[0] // 2, 0, 0)
                ),
                pl.BlockSpec(
                    (cycles * pairs, 1, BLK, LANES),
                    lambda i, where, occ: (0, lax.rem(where[0], 2), 0, where[0] // 2),
                ),
            ],
            out_specs=[
                pl.BlockSpec(right, lambda i, where, occ: (0, 0)),
                pl.BlockSpec(left, lambda i, where, occ: (0, 0)),
            ],
        ),
    )(
        where,
        occupancy.T,
        matrix.reshape(cycles, pairs, 2 * BLK, local_cols),
        matrix.reshape(cycles * pairs, 2, BLK, local_cols),
    )


def product_kernel(n_right, scale, where, *refs):
    rights, left, out, whole = refs[:n_right], refs[n_right], refs[-2], refs[-1]
    n_rows = rights[0].shape[0]
    cycles = whole.shape[1] // (n_rows * 2 * BLK)

    @pl.when(pl.program_id(0) == 0)
    def _():
        span = 2 * cycles * BLK
        for row in range(n_rows):
            if n_right == 1:
                whole[:, row * span : (row + 1) * span] = rights[0][row]
            else:
                for n, part in enumerate(rights):
                    side = lax.rem(where[0] + n, 2)
                    at = pl.multiple_of(row * span + side * (span // 2), LANES)
                    whole[:, pl.ds(at, span // 2)] = part[row]

    chunks = [
        ((row * cycles + a) * 2 + s) * BLK for row in range(n_rows) for s in range(2) for a in range(cycles)
    ]
    ordered = jnp.concatenate([left[at : at + BLK, :] for at in chunks], axis=0)
    total = scale * jnp.dot(whole[...], ordered, preferred_element_type=F32)
    out[...] = total.astype(BF16).reshape(out.shape)


def product(rights, left, where, scale, pairs, grouped):
    cols = rights[0].shape[1]
    depth, lanes = left.shape
    each = lanes // pairs
    if grouped:
        out_shape, block, place = (pairs, cols, each), (1, cols, each), lambda i, where: (i, 0, 0)
    else:
        out_shape, block, place = (cols, lanes), (cols, each), lambda i, where: (0, i)
    return call(
        functools.partial(product_kernel, len(rights), scale),
        flops=2 * cols * lanes * depth,
        moved=2 * (cols * depth + lanes * depth + cols * lanes),
        out_shape=jax.ShapeDtypeStruct(out_shape, BF16),
        grid_spec=pltpu.PrefetchScalarGridSpec(
            num_scalar_prefetch=1,
            grid=(pairs,),
            in_specs=[pl.BlockSpec(part.shape, lambda i, where: (0, 0, 0)) for part in rights]
            + [pl.BlockSpec((depth, each), lambda i, where: (0, i))],
            out_specs=pl.BlockSpec(block, place),
            scratch_shapes=[pltpu.VMEM((cols, depth), BF16)],
        ),
    )(where, *rights, left)


def filter_kernel(depths, tile_rows, tile_cols, where, filtering, mask):
    cols, lanes = mask.shape
    tiles = filtering.shape[0]
    row = lax.broadcasted_iota(jnp.int32, (tiles, lanes), 1) // BLK * depths
    rows = lax.broadcasted_iota(jnp.int32, (tiles, lanes), 0) == (
        row + where[1] * tile_rows + where[0]
    )
    col = lax.broadcasted_iota(jnp.int32, (cols, tiles), 0) // BLK + where[2] * tile_cols
    cols_of = lax.broadcasted_iota(jnp.int32, (cols, tiles), 1) == col
    spread = lax.dot_general(
        filtering[...].astype(F32), rows.astype(F32), (((0,), (0,)), ((), ())),
        preferred_element_type=F32,
    )
    mask[...] = jnp.dot(cols_of.astype(F32), spread, preferred_element_type=F32).astype(BF16)


def filter_mask(filtering, where, depths, tile_rows, tile_cols):
    shape = (tile_cols * BLK, tile_rows // depths * BLK)
    return call(
        functools.partial(filter_kernel, depths, tile_rows, tile_cols),
        out_shape=jax.ShapeDtypeStruct(shape, BF16),
        grid_spec=pltpu.PrefetchScalarGridSpec(
            num_scalar_prefetch=1,
            grid=(1,),
            in_specs=[pl.BlockSpec(filtering.shape, lambda i, where: (0, 0))],
            out_specs=pl.BlockSpec(shape, lambda i, where: (0, 0)),
        ),
    )(where, filtering)


def update_kernel(where, left, cube, keep, send):
    new = 1.5 * left[...].astype(F32) - 0.5 * cube[...].astype(F32)
    first = lax.rem(where[0], 2) == 0
    low, high = new[:BLK, :], new[BLK:, :]
    keep[...] = jnp.where(first, low, high).astype(BF16)
    send[...] = jnp.where(first, high, low).astype(BF16)


def update(left, cube, where):
    shape = (BLK, left.shape[1])
    whole = pl.BlockSpec(left.shape, lambda i, where: (0, 0))
    half = pl.BlockSpec(shape, lambda i, where: (0, 0))
    return call(
        update_kernel,
        out_shape=[jax.ShapeDtypeStruct(shape, BF16)] * 2,
        grid_spec=pltpu.PrefetchScalarGridSpec(
            num_scalar_prefetch=1, grid=(1,), in_specs=[whole, whole], out_specs=[half, half]
        ),
    )(where, left, cube)


def join_kernel(pairs, cycles, where, keep, got, out):
    first = lax.rem(where[0], 2) == 0
    low = lax.broadcasted_iota(jnp.int32, (BLK, LANES), 1) < BLK
    for q in range(pairs):
        for a in range(0, cycles, 2):
            at = (q * cycles + a) * BLK
            mine = keep[:, at : at + LANES].astype(F32)
            other = got[:, at : at + LANES].astype(F32)
            one, two = jnp.where(first, mine, other), jnp.where(first, other, mine)
            even = jnp.where(low, one, pltpu.roll(two, BLK, 1))
            odd = jnp.where(low, pltpu.roll(one, BLK, 1), two)
            for b, value in ((a, even), (a + 1, odd)):
                to = (b * pairs + q) * LANES
                out[:, to : to + LANES] = value.astype(BF16)


def join(keep, got, where, pairs):
    width, lanes = keep.shape
    half = pl.BlockSpec(keep.shape, lambda i, where: (0, 0))
    return call(
        functools.partial(join_kernel, pairs, lanes // (pairs * BLK)),
        out_shape=jax.ShapeDtypeStruct((width, 2 * lanes), BF16),
        grid_spec=pltpu.PrefetchScalarGridSpec(
            num_scalar_prefetch=1,
            grid=(1,),
            in_specs=[half, half],
            out_specs=pl.BlockSpec((width, 2 * lanes), lambda i, where: (0, 0)),
        ),
    )(where, keep, got)


def shards(matrix, occupancy, filtering):
    rows = lax.axis_size("row")
    depths = lax.axis_size("depth")
    pairs = depths // 2
    row, col, depth = (lax.axis_index(name) for name in ("row", "col", "depth"))
    local_rows, local_cols = matrix.shape
    scale = (local_rows * rows / 2.0) ** (-0.5)
    where = jnp.stack([depth, row, col]).astype(jnp.int32)
    sides = [[2 * q + s for q in range(pairs)] for s in range(2)]

    def add_over_pairs(terms):
        return lax.psum_scatter(
            terms, "depth", scatter_dimension=0, tiled=False, axis_index_groups=sides
        )

    def to_other_side(value):
        return lax.ppermute(value, "depth", [(d, d ^ 1) for d in range(depths)])

    def gather_row(value):
        return lax.all_gather(value, "row", axis=0).astype(BF16)

    right, left = prepare(matrix, occupancy, pairs, where)
    mask = filter_mask(filtering, where, depths, local_rows // BLK, local_cols // BLK)
    along_z = lax.all_gather(left, "col", axis=0, tiled=True, axis_index_groups=ALONG_Z)
    right, along_z = lax.optimization_barrier((gather_row(right.astype(F16)), along_z))
    panel = lax.all_gather(
        along_z.astype(F16), "col", axis=0, tiled=True, axis_index_groups=ALONG_X
    ).astype(BF16)

    terms = product([right], panel, where, scale, pairs, True)
    square = (add_over_pairs(terms) * mask).astype(F16)
    other = to_other_side(square)
    squares = [gather_row(square), gather_row(other)]

    terms = product(squares, panel, where, scale, pairs, False)
    cube = add_over_pairs(terms.reshape(pairs, 2 * BLK, -1))
    keep, send = update(left, cube, where)
    return join(keep, to_other_side(send), where, pairs).T


def solution(mesh):
    placed = (P("row", "col"), P("row", "col"), P())
    return jax.shard_map(
        shards, mesh=mesh, in_specs=placed, out_specs=P("row", ("col", "depth")), check_vma=False
    )
```

```python
import functools

import jax
import jax.numpy as jnp
from jax import lax
from jax.experimental import pallas as pl
from jax.experimental.pallas import tpu as pltpu
from jax.sharding import PartitionSpec as P

BLK = 64
LANES = 128
HALVES = 2
RING = 4
ALONG_Z = [[x * RING + z for z in range(RING)] for x in range(RING)]
ALONG_X = [[x * RING + z for x in range(RING)] for z in range(RING)]
BF16 = jnp.bfloat16
F32 = jnp.float32
F16 = jnp.float16


def call(kernel, flops=0, moved=1 << 20, **kwargs):
    return pl.pallas_call(
        kernel,
        compiler_params=pltpu.CompilerParams(vmem_limit_bytes=40 << 20),
        cost_estimate=pl.CostEstimate(flops=flops, bytes_accessed=moved, transcendentals=0),
        **kwargs,
    )


def tile_mask(scalars):
    shape = (1, BLK * len(scalars))
    tile = lax.broadcasted_iota(jnp.int32, shape, 1) // BLK
    mask = jnp.zeros(shape, F32)
    for t, value in enumerate(scalars):
        mask = jnp.where(tile == t, value.astype(F32), mask)
    return mask


def prepare_kernel(pairs, cycles, where, occ_t, rows, columns, right, left):
    per = cycles // HALVES
    pair, side = where[0] // 2, lax.rem(where[0], 2)
    tile_cols = rows.shape[3] // BLK
    parts = []
    for s in range(2):
        for a in range(cycles):
            tile_row = (a * pairs + pair) * 2 + s
            mask = tile_mask([occ_t[t, tile_row] for t in range(tile_cols)])
            part = rows[a, 0, s * BLK : (s + 1) * BLK, :].astype(F32)
            parts.append((part * mask).astype(BF16))
    right[...] = jnp.concatenate(parts, axis=0).T
    for h in range(HALVES):
        order = [a * pairs + q for q in range(pairs) for a in range(h * per, (h + 1) * per)]
        turned = jnp.concatenate([columns[t, 0] for t in order], axis=0).T
        for s in range(2):
            mask = tile_mask([occ_t[pair * 2 + s, t * 2 + side] for t in order])
            part = turned[s * BLK : (s + 1) * BLK, :].astype(F32)
            left[h, s * BLK : (s + 1) * BLK, :] = (part * mask).astype(BF16)


def prepare(matrix, occupancy, pairs, where):
    local_rows, local_cols = matrix.shape
    cycles = local_rows // (pairs * 2 * BLK)
    right = (local_cols, cycles * 2 * BLK)
    left = (HALVES, 2 * BLK, local_rows // 2 // HALVES)
    return call(
        functools.partial(prepare_kernel, pairs, cycles),
        out_shape=[jax.ShapeDtypeStruct(right, BF16), jax.ShapeDtypeStruct(left, BF16)],
        grid_spec=pltpu.PrefetchScalarGridSpec(
            num_scalar_prefetch=2,
            grid=(1,),
            in_specs=[
                pl.BlockSpec(
                    (cycles, 1, 2 * BLK, local_cols), lambda i, where, occ: (0, where[0] // 2, 0, 0)
                ),
                pl.BlockSpec(
                    (cycles * pairs, 1, BLK, LANES),
                    lambda i, where, occ: (0, lax.rem(where[0], 2), 0, where[0] // 2),
                ),
            ],
            out_specs=[
                pl.BlockSpec(right, lambda i, where, occ: (0, 0)),
                pl.BlockSpec(left, lambda i, where, occ: (0, 0, 0)),
            ],
        ),
    )(
        where,
        occupancy.T,
        matrix.reshape(cycles, pairs, 2 * BLK, local_cols),
        matrix.reshape(cycles * pairs, 2, BLK, local_cols),
    )


def product_kernel(n_right, scale, where, *refs):
    rights, lefts, out, whole = refs[:n_right], refs[n_right:-2], refs[-2], refs[-1]
    n_rows = rights[0].shape[0]
    cycles = whole.shape[1] // (n_rows * 2 * BLK)
    span = cycles * BLK

    @pl.when(pl.program_id(0) == 0)
    def _():
        for row in range(n_rows):
            for h, part in enumerate(rights):
                if n_right == 1:
                    whole[:, row * 2 * span : (row + 1) * 2 * span] = part[row]
                    continue
                for n in range(2):
                    side = lax.rem(where[0] + n, 2)
                    at = pl.multiple_of((row * 2 + side) * span + h * part.shape[3], LANES)
                    whole[:, pl.ds(at, part.shape[3])] = part[row, n]

    chunks = [
        ((row * cycles + a) * 2 + s) * BLK for row in range(n_rows) for s in range(2) for a in range(cycles)
    ]
    steps = pl.num_programs(0) // len(lefts)
    for n, left in enumerate(lefts):

        @pl.when(pl.program_id(0) // steps == n)
        def _(left=left):
            ordered = jnp.concatenate([left[at : at + BLK, :] for at in chunks], axis=0)
            total = scale * jnp.dot(whole[...], ordered, preferred_element_type=F32)
            if len(out.shape) == 2:
                out[...] = total.astype(BF16)
            else:
                for q in range(out.shape[0]):
                    lanes = out.shape[2]
                    out[q] = total[:, q * lanes : (q + 1) * lanes].astype(BF16)


def product(rights, lefts, where, scale, pairs, grouped):
    cols = rights[0].shape[-2]
    depth, lanes = lefts[0].shape
    each = lanes // pairs
    block = 2 * each
    steps = lanes // block

    def left_place(n):
        return lambda i, where: (0, jnp.clip(i - n * steps, 0, steps - 1))

    if grouped:
        out_shape, out_block = (pairs, cols, each), (2, cols, each)
        place = lambda i, where: (i, 0, 0)
    else:
        out_shape, out_block = (cols, lanes * len(lefts)), (cols, block)
        place = lambda i, where: (0, i)

    def whole(part):
        return pl.BlockSpec(part.shape, lambda i, where: (0,) * part.ndim)

    return call(
        functools.partial(product_kernel, len(rights), scale),
        flops=2 * cols * lanes * len(lefts) * depth,
        moved=2 * (cols * depth + (lanes * depth + cols * lanes) * len(lefts)),
        out_shape=jax.ShapeDtypeStruct(out_shape, BF16),
        grid_spec=pltpu.PrefetchScalarGridSpec(
            num_scalar_prefetch=1,
            grid=(steps * len(lefts),),
            in_specs=[whole(part) for part in rights]
            + [pl.BlockSpec((depth, block), left_place(n)) for n in range(len(lefts))],
            out_specs=pl.BlockSpec(out_block, place),
            scratch_shapes=[pltpu.VMEM((cols, depth), BF16)],
        ),
    )(where, *rights, *lefts)


def filter_kernel(depths, tile_rows, tile_cols, where, filtering, mask):
    cols, lanes = mask.shape
    tiles = filtering.shape[0]
    row = lax.broadcasted_iota(jnp.int32, (tiles, lanes), 1) // BLK * depths
    rows = lax.broadcasted_iota(jnp.int32, (tiles, lanes), 0) == (
        row + where[1] * tile_rows + where[0]
    )
    col = lax.broadcasted_iota(jnp.int32, (cols, tiles), 0) // BLK + where[2] * tile_cols
    cols_of = lax.broadcasted_iota(jnp.int32, (cols, tiles), 1) == col
    spread = lax.dot_general(
        filtering[...].astype(F32), rows.astype(F32), (((0,), (0,)), ((), ())),
        preferred_element_type=F32,
    )
    mask[...] = jnp.dot(cols_of.astype(F32), spread, preferred_element_type=F32).astype(BF16)


def filter_mask(filtering, where, depths, tile_rows, tile_cols):
    shape = (tile_cols * BLK, tile_rows // depths * BLK)
    return call(
        functools.partial(filter_kernel, depths, tile_rows, tile_cols),
        out_shape=jax.ShapeDtypeStruct(shape, BF16),
        grid_spec=pltpu.PrefetchScalarGridSpec(
            num_scalar_prefetch=1,
            grid=(1,),
            in_specs=[pl.BlockSpec(filtering.shape, lambda i, where: (0, 0))],
            out_specs=pl.BlockSpec(shape, lambda i, where: (0, 0)),
        ),
    )(where, filtering)


def square_kernel(terms, mask, out):
    total = terms[0].astype(F32)
    for q in range(1, terms.shape[0]):
        total = total + terms[q].astype(F32)
    out[...] = (total * mask[...].astype(F32)).astype(BF16)


def square_part(terms, mask, h):
    _, cols, lanes = terms.shape
    return call(
        square_kernel,
        out_shape=jax.ShapeDtypeStruct((cols, lanes), BF16),
        grid=(1,),
        in_specs=[
            pl.BlockSpec(terms.shape, lambda i: (0, 0, 0)),
            pl.BlockSpec((cols, lanes), lambda i: (0, h)),
        ],
        out_specs=pl.BlockSpec((cols, lanes), lambda i: (0, 0)),
    )(terms, mask)


def update_kernel(where, left, terms, keep, send):
    first = lax.rem(where[0], 2) == 0
    lanes = left.shape[2]
    for h in range(HALVES):
        cube = terms[0, :, h * lanes : (h + 1) * lanes].astype(F32)
        for q in range(1, terms.shape[0]):
            cube = cube + terms[q, :, h * lanes : (h + 1) * lanes].astype(F32)
        new = 1.5 * left[h].astype(F32) - 0.5 * cube
        low, high = new[:BLK, :], new[BLK:, :]
        keep[:, h * lanes : (h + 1) * lanes] = jnp.where(first, low, high).astype(BF16)
        send[:, h * lanes : (h + 1) * lanes] = jnp.where(first, high, low).astype(BF16)


def update(left, terms, where):
    shape = (BLK, terms.shape[2])

    def whole(shape):
        return pl.BlockSpec(shape, lambda i, where: (0,) * len(shape))

    return call(
        update_kernel,
        out_shape=[jax.ShapeDtypeStruct(shape, BF16)] * 2,
        grid_spec=pltpu.PrefetchScalarGridSpec(
            num_scalar_prefetch=1,
            grid=(1,),
            in_specs=[whole(left.shape), whole(terms.shape)],
            out_specs=[whole(shape), whole(shape)],
        ),
    )(where, left, terms)


def join_kernel(pairs, where, keep, got, out):
    first = lax.rem(where[0], 2) == 0
    low = lax.broadcasted_iota(jnp.int32, (BLK, LANES), 1) < BLK
    for h in range(HALVES):
        for q in range(pairs):
            at = (h * pairs + q) * LANES
            mine = keep[:, at : at + LANES].astype(F32)
            other = got[:, at : at + LANES].astype(F32)
            one, two = jnp.where(first, mine, other), jnp.where(first, other, mine)
            even = jnp.where(low, one, pltpu.roll(two, BLK, 1))
            odd = jnp.where(low, pltpu.roll(one, BLK, 1), two)
            for a, value in ((2 * h, even), (2 * h + 1, odd)):
                to = (a * pairs + q) * LANES
                out[:, to : to + LANES] = value.astype(BF16)


def join(keep, got, where, pairs):
    width, lanes = keep.shape
    half = pl.BlockSpec(keep.shape, lambda i, where: (0, 0))
    return call(
        functools.partial(join_kernel, pairs),
        out_shape=jax.ShapeDtypeStruct((width, 2 * lanes), BF16),
        grid_spec=pltpu.PrefetchScalarGridSpec(
            num_scalar_prefetch=1,
            grid=(1,),
            in_specs=[half, half],
            out_specs=pl.BlockSpec((width, 2 * lanes), lambda i, where: (0, 0)),
        ),
    )(where, keep, got)


def shards(matrix, occupancy, filtering):
    rows = lax.axis_size("row")
    depths = lax.axis_size("depth")
    pairs = depths // 2
    row, col, depth = (lax.axis_index(name) for name in ("row", "col", "depth"))
    local_rows, local_cols = matrix.shape
    scale = (local_rows * rows / 2.0) ** (-0.5)
    where = jnp.stack([depth, row, col]).astype(jnp.int32)
    sides = [[2 * q + s for q in range(pairs)] for s in range(2)]

    def trade_over_pairs(terms):
        return lax.all_to_all(terms, "depth", 0, 0, tiled=True, axis_index_groups=sides)

    def to_other_side(value):
        return lax.ppermute(value, "depth", [(d, d ^ 1) for d in range(depths)])

    def gather_col(value, axis, groups):
        return lax.all_gather(value, "col", axis=axis, tiled=True, axis_index_groups=groups)

    right, left = prepare(matrix, occupancy, pairs, where)
    mask = filter_mask(filtering, where, depths, local_rows // BLK, local_cols // BLK)
    rights = [lax.all_gather(right, "row", axis=0)]
    along_z = gather_col(left.astype(F16), 1, ALONG_Z)

    one = gather_col(along_z[0], 0, ALONG_X).astype(BF16)
    terms_one = product(rights, [one], where, scale, pairs, True)
    terms_one, along_two = lax.optimization_barrier((terms_one, along_z[1]))
    got_one = trade_over_pairs(terms_one)
    two = gather_col(along_two, 0, ALONG_X).astype(BF16)
    got_one, two = lax.optimization_barrier((got_one, two))
    got_two = trade_over_pairs(product(rights, [two], where, scale, pairs, True))

    squares = []
    for h, got in enumerate((got_one, got_two)):
        square = square_part(got, mask, h).astype(F16)
        both = jnp.stack([square, to_other_side(square)])
        squares.append(lax.all_gather(both, "row", axis=0).astype(BF16))

    terms = product(squares, [one, two], where, scale, pairs, False)
    got = trade_over_pairs(terms.reshape(pairs, 2 * BLK, -1))
    keep, send = update(left, got, where)
    return join(keep, to_other_side(send), where, pairs).T


def solution(mesh):
    placed = (P("row", "col"), P("row", "col"), P())
    return jax.shard_map(
        shards, mesh=mesh, in_specs=placed, out_specs=P("row", ("col", "depth")), check_vma=False
    )
```

```python
import functools

import jax
import jax.numpy as jnp
from jax import lax
from jax.experimental import pallas as pl
from jax.experimental.pallas import tpu as pltpu
from jax.sharding import PartitionSpec as P

BLK = 64
LANES = 128
HALVES = 2
RING = 4
ALONG_Z = [[x * RING + z for z in range(RING)] for x in range(RING)]
ALONG_X = [[x * RING + z for x in range(RING)] for z in range(RING)]
BF16 = jnp.bfloat16
F32 = jnp.float32
F16 = jnp.float16


def call(kernel, flops=0, moved=1 << 20, vmem=40 << 20, **kwargs):
    return pl.pallas_call(
        kernel,
        compiler_params=pltpu.CompilerParams(vmem_limit_bytes=vmem),
        cost_estimate=pl.CostEstimate(flops=flops, bytes_accessed=moved, transcendentals=0),
        **kwargs,
    )


def tile_mask(scalars):
    shape = (1, BLK * len(scalars))
    tile = lax.broadcasted_iota(jnp.int32, shape, 1) // BLK
    mask = jnp.zeros(shape, F32)
    for t, value in enumerate(scalars):
        mask = jnp.where(tile == t, value.astype(F32), mask)
    return mask


def prepare_kernel(pairs, cycles, where, occ_t, rows, columns, right, left):
    per = cycles // HALVES
    pair, side = where[0] // 2, lax.rem(where[0], 2)
    tile_cols = rows.shape[3] // BLK
    parts = []
    for a in range(cycles):
        for s in range(2):
            tile_row = (a * pairs + pair) * 2 + s
            mask = tile_mask([occ_t[t, tile_row] for t in range(tile_cols)])
            part = rows[a, 0, s * BLK : (s + 1) * BLK, :].astype(F32)
            parts.append((part * mask).astype(BF16))
    right[...] = jnp.concatenate(parts, axis=0).T
    for h in range(HALVES):
        order = [a * pairs + q for q in range(pairs) for a in range(h * per, (h + 1) * per)]
        turned = jnp.concatenate([columns[t, 0] for t in order], axis=0).T
        for s in range(2):
            mask = tile_mask([occ_t[pair * 2 + s, t * 2 + side] for t in order])
            part = turned[s * BLK : (s + 1) * BLK, :].astype(F32)
            left[h, s * BLK : (s + 1) * BLK, :] = (part * mask).astype(BF16)


def prepare(matrix, occupancy, pairs, where):
    local_rows, local_cols = matrix.shape
    cycles = local_rows // (pairs * 2 * BLK)
    right = (local_cols, cycles * 2 * BLK)
    left = (HALVES, 2 * BLK, local_rows // 2 // HALVES)
    return call(
        functools.partial(prepare_kernel, pairs, cycles),
        vmem=60 << 20,
        out_shape=[jax.ShapeDtypeStruct(right, BF16), jax.ShapeDtypeStruct(left, BF16)],
        grid_spec=pltpu.PrefetchScalarGridSpec(
            num_scalar_prefetch=2,
            grid=(1,),
            in_specs=[
                pl.BlockSpec(
                    (cycles, 1, 2 * BLK, local_cols), lambda i, where, occ: (0, where[0] // 2, 0, 0)
                ),
                pl.BlockSpec(
                    (cycles * pairs, 1, BLK, LANES),
                    lambda i, where, occ: (0, lax.rem(where[0], 2), 0, where[0] // 2),
                ),
            ],
            out_specs=[
                pl.BlockSpec(right, lambda i, where, occ: (0, 0)),
                pl.BlockSpec(left, lambda i, where, occ: (0, 0, 0)),
            ],
        ),
    )(
        where,
        occupancy.T,
        matrix.reshape(cycles, pairs, 2 * BLK, local_cols),
        matrix.reshape(cycles * pairs, 2, BLK, local_cols),
    )


def square_terms_kernel(scale, where, *refs):
    *rights, left, out = refs
    span = rights[0].shape[1]
    total = 0.0
    for n, right in enumerate(rights):
        at = pl.multiple_of((where[1] ^ n) * span, span)
        total = total + jnp.dot(right[...], left[pl.ds(at, span), :], preferred_element_type=F32)
    total = scale * total
    lanes = out.shape[2]
    for q in range(out.shape[0]):
        out[q] = total[:, q * lanes : (q + 1) * lanes].astype(BF16)


def square_terms(rights, left, where, scale, pairs):
    cols = rights[0].shape[0]
    depth, lanes = left.shape
    each = lanes // pairs
    return call(
        functools.partial(square_terms_kernel, scale),
        flops=2 * cols * lanes * depth,
        moved=2 * (cols * depth + lanes * depth + cols * lanes),
        out_shape=jax.ShapeDtypeStruct((pairs, cols, each), BF16),
        grid_spec=pltpu.PrefetchScalarGridSpec(
            num_scalar_prefetch=1,
            grid=(pairs // 2,),
            in_specs=[pl.BlockSpec(part.shape, lambda i, where: (0, 0)) for part in rights]
            + [pl.BlockSpec((depth, 2 * each), lambda i, where: (0, i))],
            out_specs=pl.BlockSpec((2, cols, each), lambda i, where: (i, 0, 0)),
        ),
    )(where, *rights, left)


def cube_terms_kernel(places, scale, where, *refs):
    squares, lefts, out, whole = refs[: len(places)], refs[len(places) : -2], refs[-2], refs[-1]
    n_rows = squares[0].shape[0]
    cycles = whole.shape[1] // (n_rows * 2 * BLK)
    span = cycles * BLK

    @pl.when(pl.program_id(0) == 0)
    def _():
        for part, held in zip(squares, places):
            for n, (other, h) in enumerate(held):
                lanes = part.shape[3]
                for row in range(n_rows):
                    side = lax.rem(where[0] + other, 2)
                    at = pl.multiple_of((row * 2 + side) * span + h * lanes, LANES)
                    whole[:, pl.ds(at, lanes)] = part[row, n]

    chunks = [
        ((row * cycles + a) * 2 + s) * BLK for row in range(n_rows) for s in range(2) for a in range(cycles)
    ]
    steps = pl.num_programs(0) // len(lefts)
    for n, left in enumerate(lefts):

        @pl.when(pl.program_id(0) // steps == n)
        def _(left=left):
            ordered = jnp.concatenate([left[at : at + BLK, :] for at in chunks], axis=0)
            total = scale * jnp.dot(whole[...], ordered, preferred_element_type=F32)
            out[...] = total.astype(BF16)


def cube_terms(squares, places, lefts, where, scale, block):
    cols = squares[0].shape[2]
    depth, lanes = lefts[0].shape
    steps = lanes // block

    def left_place(n):
        return lambda i, where: (0, jnp.clip(i - n * steps, 0, steps - 1))

    return call(
        functools.partial(cube_terms_kernel, places, scale),
        flops=2 * cols * lanes * len(lefts) * depth,
        moved=2 * (cols * depth + (lanes * depth + cols * lanes) * len(lefts)),
        out_shape=jax.ShapeDtypeStruct((cols, lanes * len(lefts)), BF16),
        grid_spec=pltpu.PrefetchScalarGridSpec(
            num_scalar_prefetch=1,
            grid=(steps * len(lefts),),
            in_specs=[pl.BlockSpec(part.shape, lambda i, where: (0, 0, 0, 0)) for part in squares]
            + [pl.BlockSpec((depth, block), left_place(n)) for n in range(len(lefts))],
            out_specs=pl.BlockSpec((cols, block), lambda i, where: (0, i)),
            scratch_shapes=[pltpu.VMEM((cols, depth), BF16)],
        ),
    )(where, *squares, *lefts)


def filter_kernel(depths, tile_rows, tile_cols, where, filtering, mask):
    cols, lanes = mask.shape
    tiles = filtering.shape[0]
    row = lax.broadcasted_iota(jnp.int32, (tiles, lanes), 1) // BLK * depths
    rows = lax.broadcasted_iota(jnp.int32, (tiles, lanes), 0) == (
        row + where[1] * tile_rows + where[0]
    )
    col = lax.broadcasted_iota(jnp.int32, (cols, tiles), 0) // BLK + where[2] * tile_cols
    cols_of = lax.broadcasted_iota(jnp.int32, (cols, tiles), 1) == col
    spread = lax.dot_general(
        filtering[...].astype(F32), rows.astype(F32), (((0,), (0,)), ((), ())),
        preferred_element_type=F32,
    )
    mask[...] = jnp.dot(cols_of.astype(F32), spread, preferred_element_type=F32).astype(BF16)


def filter_mask(filtering, where, depths, tile_rows, tile_cols):
    shape = (tile_cols * BLK, tile_rows // depths * BLK)
    return call(
        functools.partial(filter_kernel, depths, tile_rows, tile_cols),
        out_shape=jax.ShapeDtypeStruct(shape, BF16),
        grid_spec=pltpu.PrefetchScalarGridSpec(
            num_scalar_prefetch=1,
            grid=(1,),
            in_specs=[pl.BlockSpec(filtering.shape, lambda i, where: (0, 0))],
            out_specs=pl.BlockSpec(shape, lambda i, where: (0, 0)),
        ),
    )(where, filtering)


def square_kernel(terms, mask, out):
    total = terms[0].astype(F32)
    for q in range(1, terms.shape[0]):
        total = total + terms[q].astype(F32)
    out[...] = (total * mask[...].astype(F32)).astype(BF16)


def square_part(terms, mask, h):
    _, cols, lanes = terms.shape
    return call(
        square_kernel,
        out_shape=jax.ShapeDtypeStruct((cols, lanes), BF16),
        grid=(1,),
        in_specs=[
            pl.BlockSpec(terms.shape, lambda i: (0, 0, 0)),
            pl.BlockSpec((cols, lanes), lambda i: (0, h)),
        ],
        out_specs=pl.BlockSpec((cols, lanes), lambda i: (0, 0)),
    )(terms, mask)


def own_kernel(where, occ_t, columns, own):
    side = lax.rem(where[0], 2)
    tiles, _, width = columns.shape
    turned = jnp.concatenate([columns[t] for t in range(tiles)], axis=0).T
    mine = jnp.where(side == 0, turned[:BLK, :].astype(F32), turned[BLK:, :].astype(F32))
    own[...] = (mine * tile_mask([occ_t[where[0], t] for t in range(tiles)])).astype(BF16)


def own_columns(matrix, occupancy, where):
    local_rows, local_cols = matrix.shape
    tiles = local_rows // BLK
    return call(
        own_kernel,
        out_shape=jax.ShapeDtypeStruct((BLK, local_rows), BF16),
        grid_spec=pltpu.PrefetchScalarGridSpec(
            num_scalar_prefetch=2,
            grid=(1,),
            in_specs=[
                pl.BlockSpec((tiles, BLK, LANES), lambda i, where, occ: (0, 0, where[0] // 2))
            ],
            out_specs=pl.BlockSpec((BLK, local_rows), lambda i, where, occ: (0, 0)),
        ),
    )(where, occupancy.T, matrix.reshape(tiles, BLK, local_cols))


def update_kernel(own, terms, out):
    depths, _, lanes = terms.shape
    pairs = depths // 2
    low = lax.broadcasted_iota(jnp.int32, (BLK, LANES), 1) < BLK
    for block in range(lanes // LANES):
        h, q = block // pairs, block % pairs
        sides = []
        for s in range(2):
            total = 0.0
            for pair in range(pairs):
                part = terms[2 * pair + s, :, block * LANES : (block + 1) * LANES]
                total = total + part.astype(F32)
            sides.append(total)
        one, two = sides
        even = jnp.where(low, one, pltpu.roll(two, BLK, 1))
        odd = jnp.where(low, pltpu.roll(one, BLK, 1), two)
        for a, cube in ((2 * h, even), (2 * h + 1, odd)):
            at = (a * pairs + q) * LANES
            value = 1.5 * own[:, at : at + LANES].astype(F32) - 0.5 * cube
            out[:, at : at + LANES] = value.astype(BF16)


def update(own, terms):
    return call(update_kernel, out_shape=jax.ShapeDtypeStruct(own.shape, BF16))(own, terms)


def shards(matrix, occupancy, filtering):
    rows = lax.axis_size("row")
    depths = lax.axis_size("depth")
    pairs = depths // 2
    row, col, depth = (lax.axis_index(name) for name in ("row", "col", "depth"))
    local_rows, local_cols = matrix.shape
    scale = (local_rows * rows / 2.0) ** (-0.5)
    where = jnp.stack([depth, row, col]).astype(jnp.int32)
    sides = [[2 * q + s for q in range(pairs)] for s in range(2)]

    def trade_over_pairs(terms):
        return lax.all_to_all(terms, "depth", 0, 0, tiled=True, axis_index_groups=sides)

    def to_other_side(value):
        return lax.ppermute(value, "depth", [(d, d ^ 1) for d in range(depths)])

    def gather_col(value, axis, groups):
        return lax.all_gather(value, "col", axis=axis, tiled=True, axis_index_groups=groups)

    def swap_row(value, bit):
        return lax.ppermute(value, "row", [(r, r ^ bit) for r in range(rows)])

    def gather_row(value):
        return lax.all_gather(value, "row", axis=0).astype(BF16)

    right, left = prepare(matrix, occupancy, pairs, where)
    near, across = swap_row(right, 1), swap_row(right, 2)
    along_z = gather_col(left.astype(F16), 1, ALONG_Z)
    across, along_z = lax.optimization_barrier((across, along_z))
    rights = [right, near, across, swap_row(across, 1)]

    one = gather_col(along_z[0], 0, ALONG_X).astype(BF16)
    terms_one = square_terms(rights, one, where, scale, pairs)
    terms_one, along_two = lax.optimization_barrier((terms_one, along_z[1]))
    got_one = trade_over_pairs(terms_one)
    two = gather_col(along_two, 0, ALONG_X).astype(BF16)
    got_one, two = lax.optimization_barrier((got_one, two))
    terms_two = square_terms(rights, two, where, scale, pairs)
    got_one, terms_two, here = lax.optimization_barrier((got_one, terms_two, where))
    got_two = trade_over_pairs(terms_two)

    mask = filter_mask(filtering, here, depths, local_rows // BLK, local_cols // BLK)
    square_one = square_part(got_one, mask, 0).astype(F16)
    other_one = to_other_side(square_one)
    first = gather_row(square_one[None])
    first, other_one, got_two = lax.optimization_barrier((first, other_one, got_two))
    square_two = square_part(got_two, mask, 1).astype(F16)
    rest = gather_row(jnp.stack([square_two, other_one, to_other_side(square_two)]))
    places = (((0, 0),), ((0, 1), (1, 0), (1, 1)))

    terms = cube_terms((first, rest), places, [one, two], where, scale, local_cols // 2)
    terms, here = lax.optimization_barrier((terms, where))
    got = lax.all_to_all(terms.reshape(depths, BLK, -1), "depth", 0, 0, tiled=True)
    return update(own_columns(matrix, occupancy, here), got).T


def solution(mesh):
    placed = (P("row", "col"), P("row", "col"), P())
    return jax.shard_map(
        shards, mesh=mesh, in_specs=placed, out_specs=P("row", ("col", "depth")), check_vma=False
    )
```

```python
import functools

import jax
import jax.numpy as jnp
from jax import lax
from jax.experimental import pallas as pl
from jax.experimental.pallas import tpu as pltpu
from jax.sharding import PartitionSpec as P

BLK = 64
LANES = 128
HALVES = 2
RING = 4
ALONG_Z = [[x * RING + z for z in range(RING)] for x in range(RING)]
ALONG_X = [[x * RING + z for x in range(RING)] for z in range(RING)]
BF16 = jnp.bfloat16
F32 = jnp.float32
F16 = jnp.float16


def call(kernel, flops=0, moved=1 << 20, vmem=20 << 20, **kwargs):
    return pl.pallas_call(
        kernel,
        compiler_params=pltpu.CompilerParams(vmem_limit_bytes=vmem),
        cost_estimate=pl.CostEstimate(flops=flops, bytes_accessed=moved, transcendentals=0),
        **kwargs,
    )


def tile_mask(scalars):
    shape = (1, BLK * len(scalars))
    tile = lax.broadcasted_iota(jnp.int32, shape, 1) // BLK
    mask = jnp.zeros(shape, F32)
    for t, value in enumerate(scalars):
        mask = jnp.where(tile == t, value.astype(F32), mask)
    return mask


def prepare_kernel(pairs, cycles, where, occ_t, rows, columns, right, left):
    per = cycles // HALVES
    pair, side = where[0] // 2, lax.rem(where[0], 2)
    tile_cols = rows.shape[3] // BLK
    parts = []
    for a in range(cycles):
        for s in range(2):
            tile_row = (a * pairs + pair) * 2 + s
            mask = tile_mask([occ_t[t, tile_row] for t in range(tile_cols)])
            part = rows[a, 0, s * BLK : (s + 1) * BLK, :].astype(F32)
            parts.append((part * mask).astype(BF16))
    right[...] = jnp.concatenate(parts, axis=0).T
    for h in range(HALVES):
        order = [a * pairs + q for q in range(pairs) for a in range(h * per, (h + 1) * per)]
        turned = jnp.concatenate([columns[t, 0] for t in order], axis=0).T
        for s in range(2):
            mask = tile_mask([occ_t[pair * 2 + s, t * 2 + side] for t in order])
            part = turned[s * BLK : (s + 1) * BLK, :].astype(F32)
            left[h, s * BLK : (s + 1) * BLK, :] = (part * mask).astype(BF16)


def prepare(matrix, occupancy, pairs, where):
    local_rows, local_cols = matrix.shape
    cycles = local_rows // (pairs * 2 * BLK)
    right = (local_cols, cycles * 2 * BLK)
    left = (HALVES, 2 * BLK, local_rows // 2 // HALVES)
    return call(
        functools.partial(prepare_kernel, pairs, cycles),
        vmem=60 << 20,
        out_shape=[jax.ShapeDtypeStruct(right, BF16), jax.ShapeDtypeStruct(left, BF16)],
        grid_spec=pltpu.PrefetchScalarGridSpec(
            num_scalar_prefetch=2,
            grid=(1,),
            in_specs=[
                pl.BlockSpec(
                    (cycles, 1, 2 * BLK, local_cols), lambda i, where, occ: (0, where[0] // 2, 0, 0)
                ),
                pl.BlockSpec(
                    (cycles * pairs, 1, BLK, LANES),
                    lambda i, where, occ: (0, lax.rem(where[0], 2), 0, where[0] // 2),
                ),
            ],
            out_specs=[
                pl.BlockSpec(right, lambda i, where, occ: (0, 0)),
                pl.BlockSpec(left, lambda i, where, occ: (0, 0, 0)),
            ],
        ),
    )(
        where,
        occupancy.T,
        matrix.reshape(cycles, pairs, 2 * BLK, local_cols),
        matrix.reshape(cycles * pairs, 2, BLK, local_cols),
    )


def square_terms_kernel(scale, where, *refs):
    *rights, left, out = refs
    span = rights[0].shape[1]
    total = 0.0
    for n, right in enumerate(rights):
        at = pl.multiple_of((where[1] ^ n) * span, span)
        total = total + jnp.dot(right[...], left[pl.ds(at, span), :], preferred_element_type=F32)
    total = scale * total
    lanes = out.shape[3]
    for q in range(out.shape[0]):
        for s in range(2):
            out[q, s] = total[:, q * lanes : (q + 1) * lanes].astype(BF16)


def square_terms(rights, left, where, scale, pairs):
    cols = rights[0].shape[0]
    depth, lanes = left.shape
    each = lanes // pairs
    return call(
        functools.partial(square_terms_kernel, scale),
        flops=2 * cols * lanes * depth,
        moved=2 * (cols * depth + lanes * depth + cols * lanes),
        out_shape=jax.ShapeDtypeStruct((pairs, 2, cols, each), BF16),
        grid_spec=pltpu.PrefetchScalarGridSpec(
            num_scalar_prefetch=1,
            grid=(pairs // 2,),
            in_specs=[pl.BlockSpec(part.shape, lambda i, where: (0, 0)) for part in rights]
            + [pl.BlockSpec((depth, 2 * each), lambda i, where: (0, i))],
            out_specs=pl.BlockSpec((2, 2, cols, each), lambda i, where: (i, 0, 0, 0)),
        ),
    )(where, *rights, left)


def cube_terms_kernel(scale, *refs):
    squares, lefts, out, whole = refs[:HALVES], refs[HALVES:-2], refs[-2], refs[-1]
    n_rows = squares[0].shape[0]
    cycles = whole.shape[1] // (n_rows * 2 * BLK)
    span = cycles * BLK

    @pl.when(pl.program_id(0) == 0)
    def _():
        for h, part in enumerate(squares):
            lanes = part.shape[3]
            for row in range(n_rows):
                for side in range(2):
                    at = (row * 2 + side) * span + h * lanes
                    whole[:, at : at + lanes] = part[row, side]

    chunks = [
        ((row * cycles + a) * 2 + s) * BLK for row in range(n_rows) for s in range(2) for a in range(cycles)
    ]
    steps = pl.num_programs(0) // len(lefts)
    for n, left in enumerate(lefts):

        @pl.when(pl.program_id(0) // steps == n)
        def _(left=left):
            ordered = jnp.concatenate([left[at : at + BLK, :] for at in chunks], axis=0)
            total = scale * jnp.dot(whole[...], ordered, preferred_element_type=F32)
            out[...] = total.astype(BF16)


def cube_terms(squares, lefts, scale, block):
    cols = squares[0].shape[2]
    depth, lanes = lefts[0].shape
    steps = lanes // block

    def left_place(n):
        return lambda i: (0, jnp.clip(i - n * steps, 0, steps - 1))

    return call(
        functools.partial(cube_terms_kernel, scale),
        flops=2 * cols * lanes * len(lefts) * depth,
        moved=2 * (cols * depth + (lanes * depth + cols * lanes) * len(lefts)),
        out_shape=jax.ShapeDtypeStruct((cols, lanes * len(lefts)), BF16),
        vmem=28 << 20,
        grid=(steps * len(lefts),),
        in_specs=[pl.BlockSpec(part.shape, lambda i: (0, 0, 0, 0)) for part in squares]
        + [pl.BlockSpec((depth, block), left_place(n)) for n in range(len(lefts))],
        out_specs=pl.BlockSpec((cols, block), lambda i: (0, i)),
        scratch_shapes=[pltpu.VMEM((cols, depth), BF16)],
    )(*squares, *lefts)


def filter_kernel(depths, tile_rows, tile_cols, where, filtering, mask):
    cols, lanes = mask.shape
    tiles = filtering.shape[0]
    lane = lax.broadcasted_iota(jnp.int32, (tiles, lanes), 1)
    row = lax.rem(lane, lanes // 2) // BLK * depths + lane // (lanes // 2)
    rows = lax.broadcasted_iota(jnp.int32, (tiles, lanes), 0) == (
        row + where[1] * tile_rows + where[0] // 2 * 2
    )
    col = lax.broadcasted_iota(jnp.int32, (cols, tiles), 0) // BLK + where[2] * tile_cols
    cols_of = lax.broadcasted_iota(jnp.int32, (cols, tiles), 1) == col
    spread = lax.dot_general(
        filtering[...].astype(F32), rows.astype(F32), (((0,), (0,)), ((), ())),
        preferred_element_type=F32,
    )
    mask[...] = jnp.dot(cols_of.astype(F32), spread, preferred_element_type=F32).astype(BF16)


def filter_mask(filtering, where, depths, tile_rows, tile_cols):
    shape = (tile_cols * BLK, 2 * tile_rows // depths * BLK)
    return call(
        functools.partial(filter_kernel, depths, tile_rows, tile_cols),
        out_shape=jax.ShapeDtypeStruct(shape, BF16),
        grid_spec=pltpu.PrefetchScalarGridSpec(
            num_scalar_prefetch=1,
            grid=(1,),
            in_specs=[pl.BlockSpec(filtering.shape, lambda i, where: (0, 0))],
            out_specs=pl.BlockSpec(shape, lambda i, where: (0, 0)),
        ),
    )(where, filtering)


def square_kernel(h, terms, mask, out):
    lanes = terms.shape[2]
    for s in range(2):
        total = terms[s].astype(F32)
        for q in range(1, terms.shape[0] // 2):
            total = total + terms[2 * q + s].astype(F32)
        at = (s * HALVES + h) * lanes
        out[s] = (total * mask[:, at : at + lanes].astype(F32)).astype(BF16)


def square_part(terms, mask, h):
    return call(
        functools.partial(square_kernel, h),
        out_shape=jax.ShapeDtypeStruct((2,) + terms.shape[1:], BF16),
    )(terms, mask)


def own_kernel(where, occ_t, columns, own):
    side = lax.rem(where[0], 2)
    tiles, _, width = columns.shape
    turned = jnp.concatenate([columns[t] for t in range(tiles)], axis=0).T
    mine = jnp.where(side == 0, turned[:BLK, :].astype(F32), turned[BLK:, :].astype(F32))
    own[...] = (mine * tile_mask([occ_t[where[0], t] for t in range(tiles)])).astype(BF16)


def own_columns(matrix, occupancy, where):
    local_rows, local_cols = matrix.shape
    tiles = local_rows // BLK
    return call(
        own_kernel,
        out_shape=jax.ShapeDtypeStruct((BLK, local_rows), BF16),
        grid_spec=pltpu.PrefetchScalarGridSpec(
            num_scalar_prefetch=2,
            grid=(1,),
            in_specs=[
                pl.BlockSpec((tiles, BLK, LANES), lambda i, where, occ: (0, 0, where[0] // 2))
            ],
            out_specs=pl.BlockSpec((BLK, local_rows), lambda i, where, occ: (0, 0)),
        ),
    )(where, occupancy.T, matrix.reshape(tiles, BLK, local_cols))


def update_kernel(own, terms, out):
    depths, _, lanes = terms.shape
    pairs = depths // 2
    low = lax.broadcasted_iota(jnp.int32, (BLK, LANES), 1) < BLK
    for block in range(lanes // LANES):
        h, q = block // pairs, block % pairs
        sides = []
        for s in range(2):
            total = 0.0
            for pair in range(pairs):
                part = terms[2 * pair + s, :, block * LANES : (block + 1) * LANES]
                total = total + part.astype(F32)
            sides.append(total)
        one, two = sides
        even = jnp.where(low, one, pltpu.roll(two, BLK, 1))
        odd = jnp.where(low, pltpu.roll(one, BLK, 1), two)
        for a, cube in ((2 * h, even), (2 * h + 1, odd)):
            at = (a * pairs + q) * LANES
            value = 1.5 * own[:, at : at + LANES].astype(F32) - 0.5 * cube
            out[:, at : at + LANES] = value.astype(BF16)


def update(own, terms):
    return call(update_kernel, out_shape=jax.ShapeDtypeStruct(own.shape, BF16))(own, terms)


def shards(matrix, occupancy, filtering):
    rows = lax.axis_size("row")
    depths = lax.axis_size("depth")
    pairs = depths // 2
    row, col, depth = (lax.axis_index(name) for name in ("row", "col", "depth"))
    local_rows, local_cols = matrix.shape
    scale = (local_rows * rows / 2.0) ** (-0.5)
    where = jnp.stack([depth, row, col]).astype(jnp.int32)

    def trade_over_depth(terms):
        return lax.all_to_all(terms, "depth", 0, 0, tiled=True)

    def gather_col(value, axis, groups):
        return lax.all_gather(value, "col", axis=axis, tiled=True, axis_index_groups=groups)

    def swap_row(value, bit):
        return lax.ppermute(value, "row", [(r, r ^ bit) for r in range(rows)])

    def gather_row(value):
        return lax.all_gather(value, "row", axis=0).astype(BF16)

    def terms_of(panel):
        terms = square_terms(rights, panel, where, scale, pairs)
        return terms.reshape((depths,) + terms.shape[2:])

    right, left = prepare(matrix, occupancy, pairs, where)
    along_z = gather_col(left.astype(F16), 1, ALONG_Z)
    right, along_z = lax.optimization_barrier((right, along_z))
    across, near = swap_row(right, 2), swap_row(right, 1)
    one = gather_col(along_z[0], 0, ALONG_X)
    across, near, one = lax.optimization_barrier((across, near, one))
    rights = [right, near, across, swap_row(across, 1)]
    one = one.astype(BF16)

    terms_one, along_two = lax.optimization_barrier((terms_of(one), along_z[1]))
    got_one = trade_over_depth(terms_one)
    two = gather_col(along_two, 0, ALONG_X).astype(BF16)
    got_one, two = lax.optimization_barrier((got_one, two))
    got_one, terms_two, here = lax.optimization_barrier((got_one, terms_of(two), where))
    got_two = trade_over_depth(terms_two)

    mask = filter_mask(filtering, here, depths, local_rows // BLK, local_cols // BLK)
    first = gather_row(square_part(got_one, mask, 0).astype(F16))
    first, got_two = lax.optimization_barrier((first, got_two))
    second = gather_row(square_part(got_two, mask, 1).astype(F16))

    terms = cube_terms((first, second), [one, two], scale, local_cols // 2)
    terms, here = lax.optimization_barrier((terms, where))
    got = trade_over_depth(terms.reshape(depths, BLK, -1))
    return update(own_columns(matrix, occupancy, here), got).T


def solution(mesh):
    placed = (P("row", "col"), P("row", "col"), P())
    return jax.shard_map(
        shards, mesh=mesh, in_specs=placed, out_specs=P("row", ("col", "depth")), check_vma=False
    )
```

```python
import functools

import jax
import jax.numpy as jnp
from jax import lax
from jax.experimental import pallas as pl
from jax.experimental.pallas import tpu as pltpu
from jax.sharding import PartitionSpec as P

BLK = 64
LANES = 128
RING = 4
ALONG_Z = [[x * RING + z for z in range(RING)] for x in range(RING)]
ALONG_X = [[x * RING + z for x in range(RING)] for z in range(RING)]
BF16 = jnp.bfloat16
F32 = jnp.float32
F16 = jnp.float16


def call(kernel, flops=0, moved=1 << 20, vmem=24 << 20, **kwargs):
    return pl.pallas_call(
        kernel,
        compiler_params=pltpu.CompilerParams(vmem_limit_bytes=vmem),
        cost_estimate=pl.CostEstimate(flops=flops, bytes_accessed=moved, transcendentals=0),
        **kwargs,
    )


def tile_mask(scalars):
    shape = (1, BLK * len(scalars))
    tile = lax.broadcasted_iota(jnp.int32, shape, 1) // BLK
    mask = jnp.zeros(shape, F32)
    for t, value in enumerate(scalars):
        mask = jnp.where(tile == t, value.astype(F32), mask)
    return mask


def prepare_kernel(pairs, cycles, where, occ_t, rows, columns, right, left):
    pair, side = where[0] // 2, lax.rem(where[0], 2)
    tile_cols = rows.shape[3] // BLK
    parts = []
    for a in range(cycles):
        for s in range(2):
            tile_row = (a * pairs + pair) * 2 + s
            mask = tile_mask([occ_t[t, tile_row] for t in range(tile_cols)])
            part = rows[a, 0, s * BLK : (s + 1) * BLK, :].astype(F32)
            parts.append((part * mask).astype(BF16))
    right[...] = jnp.concatenate(parts, axis=0).T
    order = [a * pairs + q for q in range(pairs) for a in range(cycles)]
    turned = jnp.concatenate([columns[t, 0] for t in order], axis=0).T
    for s in range(2):
        mask = tile_mask([occ_t[pair * 2 + s, t * 2 + side] for t in order])
        part = turned[s * BLK : (s + 1) * BLK, :].astype(F32)
        left[s * BLK : (s + 1) * BLK, :] = (part * mask).astype(BF16)


def prepare(matrix, occupancy, pairs, where):
    local_rows, local_cols = matrix.shape
    cycles = local_rows // (pairs * 2 * BLK)
    right = (local_cols, cycles * 2 * BLK)
    left = (2 * BLK, local_rows // 2)
    return call(
        functools.partial(prepare_kernel, pairs, cycles),
        vmem=60 << 20,
        out_shape=[jax.ShapeDtypeStruct(right, BF16), jax.ShapeDtypeStruct(left, BF16)],
        grid_spec=pltpu.PrefetchScalarGridSpec(
            num_scalar_prefetch=2,
            grid=(1,),
            in_specs=[
                pl.BlockSpec(
                    (cycles, 1, 2 * BLK, local_cols), lambda i, where, occ: (0, where[0] // 2, 0, 0)
                ),
                pl.BlockSpec(
                    (cycles * pairs, 1, BLK, LANES),
                    lambda i, where, occ: (0, lax.rem(where[0], 2), 0, where[0] // 2),
                ),
            ],
            out_specs=[
                pl.BlockSpec(right, lambda i, where, occ: (0, 0)),
                pl.BlockSpec(left, lambda i, where, occ: (0, 0)),
            ],
        ),
    )(
        where,
        occupancy.T,
        matrix.reshape(cycles, pairs, 2 * BLK, local_cols),
        matrix.reshape(cycles * pairs, 2, BLK, local_cols),
    )


ACROSS, BEHIND, AHEAD, HERE = (2, 0), (0, -1), (0, 1), (0, 0)


def pair_at(where, place, pairs):
    fixed, ahead = place
    forward = 1 - 2 * lax.rem(where[1], 2)
    return lax.rem(where[0] // 2 + fixed + ahead * forward + pairs, pairs)


def square_terms_kernel(scale, where, *refs):
    *rights, left, one, two = refs
    span = rights[0].shape[1]
    total = 0.0
    for n, right in enumerate(rights):
        at = pl.multiple_of((where[1] ^ n) * span, span)
        total = total + jnp.dot(right[...], left[pl.ds(at, span), :], preferred_element_type=F32)
    total = (scale * total).astype(BF16)
    for n, out in enumerate((one, two)):

        @pl.when(pl.program_id(0) == n)
        def _(out=out):
            out[...] = total


def square_terms(rights, left, where, scale, pairs, places):
    cols = rights[0].shape[0]
    depth, lanes = left.shape
    each = lanes // pairs

    def left_place(i, where):
        return 0, jnp.where(i == 0, *(pair_at(where, place, pairs) for place in places))

    return call(
        functools.partial(square_terms_kernel, scale),
        flops=4 * cols * each * depth,
        moved=2 * (cols * depth + 2 * each * (depth + cols)),
        out_shape=[jax.ShapeDtypeStruct((cols, each), BF16)] * 2,
        grid_spec=pltpu.PrefetchScalarGridSpec(
            num_scalar_prefetch=1,
            grid=(2,),
            in_specs=[pl.BlockSpec(part.shape, lambda i, where: (0, 0)) for part in rights]
            + [pl.BlockSpec((depth, each), left_place)],
            out_specs=[pl.BlockSpec((cols, each), lambda i, where: (0, 0))] * 2,
        ),
    )(where, *rights, left)


def cube_terms_kernel(scale, pairs, places, where, squares, left, one, two, whole):
    n_rows, _, _, span = squares.shape
    cycles = span // BLK
    each = one.shape[0]

    @pl.when(pl.program_id(0) == 0)
    def _():
        for n, place in enumerate(places):
            start = pl.multiple_of(pair_at(where, place, pairs) * each, each)
            for row in range(n_rows):
                for s in range(2):
                    at = pl.multiple_of((row * 2 + lax.rem(where[0] + s, 2)) * span, span)
                    whole[n * each : (n + 1) * each, pl.ds(at, span)] = squares[
                        row, s, pl.ds(start, each), :
                    ]

    chunks = [
        ((row * cycles + a) * 2 + s) * BLK for row in range(n_rows) for s in range(2) for a in range(cycles)
    ]
    ordered = jnp.concatenate([left[at : at + BLK, :] for at in chunks], axis=0)
    total = (scale * jnp.dot(whole[...], ordered, preferred_element_type=F32)).astype(BF16)
    one[...] = total[:each]
    two[...] = total[each:]


def cube_terms(squares, left, where, scale, pairs, places):
    cols = squares.shape[2]
    depth, lanes = left.shape
    each = cols // pairs
    block = 2 * LANES
    return call(
        functools.partial(cube_terms_kernel, scale, pairs, places),
        flops=4 * each * lanes * depth,
        moved=2 * (cols * depth + lanes * depth + 2 * each * lanes),
        out_shape=[jax.ShapeDtypeStruct((each, lanes), BF16)] * 2,
        grid_spec=pltpu.PrefetchScalarGridSpec(
            num_scalar_prefetch=1,
            grid=(lanes // block,),
            in_specs=[
                pl.BlockSpec(squares.shape, lambda i, where: (0, 0, 0, 0)),
                pl.BlockSpec((depth, block), lambda i, where: (0, i)),
            ],
            out_specs=[pl.BlockSpec((each, block), lambda i, where: (0, i))] * 2,
            scratch_shapes=[pltpu.VMEM((2 * each, depth), BF16)],
        ),
    )(where, squares, left)


def filter_kernel(depths, tile_rows, tile_cols, where, filtering, mask):
    cols, lanes = mask.shape
    tiles = filtering.shape[0]
    row = lax.broadcasted_iota(jnp.int32, (tiles, lanes), 1) // BLK * depths
    rows = lax.broadcasted_iota(jnp.int32, (tiles, lanes), 0) == (
        row + where[1] * tile_rows + where[0]
    )
    col = lax.broadcasted_iota(jnp.int32, (cols, tiles), 0) // BLK + where[2] * tile_cols
    cols_of = lax.broadcasted_iota(jnp.int32, (cols, tiles), 1) == col
    spread = lax.dot_general(
        filtering[...].astype(F32), rows.astype(F32), (((0,), (0,)), ((), ())),
        preferred_element_type=F32,
    )
    mask[...] = jnp.dot(cols_of.astype(F32), spread, preferred_element_type=F32).astype(BF16)


def filter_mask(filtering, where, depths, tile_rows, tile_cols):
    shape = (tile_cols * BLK, tile_rows // depths * BLK)
    return call(
        functools.partial(filter_kernel, depths, tile_rows, tile_cols),
        out_shape=jax.ShapeDtypeStruct(shape, BF16),
        grid_spec=pltpu.PrefetchScalarGridSpec(
            num_scalar_prefetch=1,
            grid=(1,),
            in_specs=[pl.BlockSpec(filtering.shape, lambda i, where: (0, 0))],
            out_specs=pl.BlockSpec(shape, lambda i, where: (0, 0)),
        ),
    )(where, filtering)


def update_kernel(where, left, *refs):
    *terms, keep, send = refs
    cube = 0.0
    for part in terms:
        cube = cube + part[...].astype(F32)
    new = 1.5 * left[...].astype(F32) - 0.5 * cube
    first = lax.rem(where[0], 2) == 0
    low, high = new[:BLK, :], new[BLK:, :]
    keep[...] = jnp.where(first, low, high).astype(BF16)
    send[...] = jnp.where(first, high, low).astype(BF16)


def update(left, terms, where):
    shape = (BLK, left.shape[1])
    whole = pl.BlockSpec(left.shape, lambda i, where: (0, 0))
    half = pl.BlockSpec(shape, lambda i, where: (0, 0))
    return call(
        update_kernel,
        out_shape=[jax.ShapeDtypeStruct(shape, BF16)] * 2,
        grid_spec=pltpu.PrefetchScalarGridSpec(
            num_scalar_prefetch=1, grid=(1,), in_specs=[whole] * (1 + len(terms)), out_specs=[half, half]
        ),
    )(where, left, *terms)


def join_kernel(pairs, cycles, where, keep, got, out):
    first = lax.rem(where[0], 2) == 0
    low = lax.broadcasted_iota(jnp.int32, (BLK, LANES), 1) < BLK
    for q in range(pairs):
        for a in range(0, cycles, 2):
            at = (q * cycles + a) * BLK
            mine = keep[:, at : at + LANES].astype(F32)
            other = got[:, at : at + LANES].astype(F32)
            one, two = jnp.where(first, mine, other), jnp.where(first, other, mine)
            even = jnp.where(low, one, pltpu.roll(two, BLK, 1))
            odd = jnp.where(low, pltpu.roll(one, BLK, 1), two)
            for b, value in ((a, even), (a + 1, odd)):
                to = (b * pairs + q) * LANES
                out[:, to : to + LANES] = value.astype(BF16)


def join(keep, got, where, pairs):
    width, lanes = keep.shape
    half = pl.BlockSpec(keep.shape, lambda i, where: (0, 0))
    return call(
        functools.partial(join_kernel, pairs, lanes // (pairs * BLK)),
        out_shape=jax.ShapeDtypeStruct((width, 2 * lanes), BF16),
        grid_spec=pltpu.PrefetchScalarGridSpec(
            num_scalar_prefetch=1,
            grid=(1,),
            in_specs=[half, half],
            out_specs=pl.BlockSpec((width, 2 * lanes), lambda i, where: (0, 0)),
        ),
    )(where, keep, got)


def shards(matrix, occupancy, filtering):
    rows = lax.axis_size("row")
    depths = lax.axis_size("depth")
    pairs = depths // 2
    row, col, depth = (lax.axis_index(name) for name in ("row", "col", "depth"))
    local_rows, local_cols = matrix.shape
    scale = (local_rows * rows / 2.0) ** (-0.5)
    where = jnp.stack([depth, row, col]).astype(jnp.int32)

    def gather_col(value, groups):
        return lax.all_gather(value, "col", axis=0, tiled=True, axis_index_groups=groups)

    def gather_row(value):
        return lax.all_gather(value, "row", axis=0).astype(BF16)

    def swap_row(value, bit):
        return lax.ppermute(value, "row", [(r, r ^ bit) for r in range(rows)])

    def to_other_side(value):
        return lax.ppermute(value, "depth", [(d, d ^ 1) for d in range(depths)])

    def to_pair(value, ahead):
        def target(r, d):
            return r * depths + (d + 2 * ahead * (1 - 2 * (r % 2))) % depths

        route = [(r * depths + d, target(r, d)) for r in range(rows) for d in range(depths)]
        return lax.ppermute(value, ("row", "depth"), route)

    def terms_here(make):
        across, behind = make((ACROSS, BEHIND))
        across = to_pair(across, 1)
        behind = to_pair(behind, -1)
        ahead, here = make((AHEAD, HERE))
        ahead = to_pair((ahead.astype(F32) + across.astype(F32)).astype(BF16), 1)
        return here, behind, ahead

    right, left = prepare(matrix, occupancy, pairs, where)
    along_z = gather_col(left.astype(F16), ALONG_Z)
    right, along_z = lax.optimization_barrier((right, along_z))
    across, near = swap_row(right, 2), swap_row(right, 1)
    panel = gather_col(along_z, ALONG_X)
    across, near, panel = lax.optimization_barrier((across, near, panel))
    rights = [right, near, across, swap_row(across, 1)]
    panel = panel.astype(BF16)

    terms = terms_here(lambda places: square_terms(rights, panel, where, scale, pairs, places))
    first, later = lax.optimization_barrier((terms[0], where))
    mask = filter_mask(filtering, later, depths, local_rows // BLK, local_cols // BLK)
    square = sum(part.astype(F32) for part in (first,) + terms[1:])
    square = (square * mask.astype(F32)).astype(BF16).astype(F16)
    squares = gather_row(jnp.stack([square, to_other_side(square)]))

    terms = terms_here(lambda places: cube_terms(squares, panel, where, scale, pairs, places))
    keep, send = update(left, terms, where)
    return join(keep, to_other_side(send), where, pairs).T


def solution(mesh):
    placed = (P("row", "col"), P("row", "col"), P())
    return jax.shard_map(
        shards, mesh=mesh, in_specs=placed, out_specs=P("row", ("col", "depth")), check_vma=False
    )
```

```python
import functools

import jax
import jax.numpy as jnp
from jax import lax
from jax.experimental import pallas as pl
from jax.experimental.pallas import tpu as pltpu
from jax.sharding import PartitionSpec as P

BLK = 64
LANES = 128
RING = 4
BF16 = jnp.bfloat16
F32 = jnp.float32


def call(kernel, flops=0, moved=1 << 20, vmem=24 << 20, **kwargs):
    return pl.pallas_call(
        kernel,
        compiler_params=pltpu.CompilerParams(vmem_limit_bytes=vmem),
        cost_estimate=pl.CostEstimate(flops=flops, bytes_accessed=moved, transcendentals=0),
        **kwargs,
    )


def tile_mask(scalars):
    shape = (1, BLK * len(scalars))
    tile = lax.broadcasted_iota(jnp.int32, shape, 1) // BLK
    mask = jnp.zeros(shape, F32)
    for t, value in enumerate(scalars):
        mask = jnp.where(tile == t, value.astype(F32), mask)
    return mask


def right_kernel(pairs, cycles, where, occ_t, rows, right):
    tile_cols = rows.shape[3] // BLK
    parts = []
    for a in range(cycles):
        for s in range(2):
            tile_row = (a * pairs + where[0] // 2) * 2 + s
            mask = tile_mask([occ_t[t, tile_row] for t in range(tile_cols)])
            part = rows[a, 0, s * BLK : (s + 1) * BLK, :].astype(F32)
            parts.append((part * mask).astype(BF16))
    right[...] = jnp.concatenate(parts, axis=0).T


def right_part(matrix, occupancy, pairs, where):
    local_rows, local_cols = matrix.shape
    cycles = local_rows // (pairs * 2 * BLK)
    right = (local_cols, cycles * 2 * BLK)
    return call(
        functools.partial(right_kernel, pairs, cycles),
        vmem=60 << 20,
        out_shape=jax.ShapeDtypeStruct(right, BF16),
        grid_spec=pltpu.PrefetchScalarGridSpec(
            num_scalar_prefetch=2,
            grid=(1,),
            in_specs=[
                pl.BlockSpec(
                    (cycles, 1, 2 * BLK, local_cols), lambda i, where, occ: (0, where[0] // 2, 0, 0)
                )
            ],
            out_specs=pl.BlockSpec(right, lambda i, where, occ: (0, 0)),
        ),
    )(where, occupancy.T, matrix.reshape(cycles, pairs, 2 * BLK, local_cols))


def left_kernel(pairs, cycles, where, occ_t, columns, left):
    pair, side = where[0] // 2, lax.rem(where[0], 2)
    order = [a * pairs + q for q in range(pairs) for a in range(cycles)]
    turned = jnp.concatenate([columns[t, 0] for t in order], axis=0).T
    for s in range(2):
        mask = tile_mask([occ_t[pair * 2 + s, t * 2 + side] for t in order])
        part = turned[s * BLK : (s + 1) * BLK, :].astype(F32)
        left[s * BLK : (s + 1) * BLK, :] = (part * mask).astype(BF16)


def left_part(matrix, occupancy, pairs, where):
    local_rows, local_cols = matrix.shape
    cycles = local_rows // (pairs * 2 * BLK)
    left = (2 * BLK, local_rows // 2)
    return call(
        functools.partial(left_kernel, pairs, cycles),
        vmem=60 << 20,
        out_shape=jax.ShapeDtypeStruct(left, BF16),
        grid_spec=pltpu.PrefetchScalarGridSpec(
            num_scalar_prefetch=2,
            grid=(1,),
            in_specs=[
                pl.BlockSpec(
                    (cycles * pairs, 1, BLK, LANES),
                    lambda i, where, occ: (0, lax.rem(where[0], 2), 0, where[0] // 2),
                )
            ],
            out_specs=pl.BlockSpec(left, lambda i, where, occ: (0, 0)),
        ),
    )(where, occupancy.T, matrix.reshape(cycles * pairs, 2, BLK, local_cols))


def panel_kernel(sources, where, *refs):
    out = refs[-1]
    forward = 1 - 2 * lax.rem(where[1], 2)
    x, z = where[2] // RING, lax.rem(where[2], RING)
    for ref, held in zip(refs, sources):
        for n, (dx, dz) in enumerate(held):
            at = (x - dx * forward) & (RING - 1), (z - dz * forward) & (RING - 1)
            out[at[0] * RING + at[1]] = ref[n] if len(ref.shape) == 3 else ref[...]


def panel_of(pieces, sources, where):
    depth, lanes = pieces[0].shape

    def whole(shape):
        return pl.BlockSpec(shape, lambda i, where: (0,) * len(shape))

    shape = (RING * RING, depth, lanes)
    return call(
        functools.partial(panel_kernel, sources),
        moved=16 << 20,
        vmem=28 << 20,
        out_shape=jax.ShapeDtypeStruct(shape, BF16),
        grid_spec=pltpu.PrefetchScalarGridSpec(
            num_scalar_prefetch=1,
            grid=(1,),
            in_specs=[whole(piece.shape) for piece in pieces],
            out_specs=whole(shape),
        ),
    )(where, *pieces).reshape(RING * RING * depth, lanes)


ACROSS, BEHIND, AHEAD, HERE = (2, 0), (0, -1), (0, 1), (0, 0)


def pair_at(where, place, pairs):
    fixed, ahead = place
    forward = 1 - 2 * lax.rem(where[1], 2)
    return lax.rem(where[0] // 2 + fixed + ahead * forward + pairs, pairs)


def square_terms_kernel(scale, where, *refs):
    *rights, left, one, two = refs
    span = rights[0].shape[1]
    total = 0.0
    for n, right in enumerate(rights):
        at = pl.multiple_of((where[1] ^ n) * span, span)
        total = total + jnp.dot(right[...], left[pl.ds(at, span), :], preferred_element_type=F32)
    total = (scale * total).astype(BF16)
    for n, out in enumerate((one, two)):

        @pl.when(pl.program_id(0) == n)
        def _(out=out):
            out[...] = total


def square_terms(rights, left, where, scale, pairs, places):
    cols = rights[0].shape[0]
    depth, lanes = left.shape
    each = lanes // pairs

    def left_place(i, where):
        return 0, jnp.where(i == 0, *(pair_at(where, place, pairs) for place in places))

    return call(
        functools.partial(square_terms_kernel, scale),
        flops=4 * cols * each * depth,
        moved=2 * (cols * depth + 2 * each * (depth + cols)),
        out_shape=[jax.ShapeDtypeStruct((cols, each), BF16)] * 2,
        grid_spec=pltpu.PrefetchScalarGridSpec(
            num_scalar_prefetch=1,
            grid=(2,),
            in_specs=[pl.BlockSpec(part.shape, lambda i, where: (0, 0)) for part in rights]
            + [pl.BlockSpec((depth, each), left_place)],
            out_specs=[pl.BlockSpec((cols, each), lambda i, where: (0, 0))] * 2,
        ),
    )(where, *rights, left)


def cube_terms_kernel(scale, pairs, places, held, where, *refs):
    *squares, left, one, two, whole = refs
    span = squares[0].shape[1]
    cycles, n_rows = span // BLK, len(squares) // 2
    each = one.shape[0]

    @pl.when(pl.program_id(0) == 0)
    def _():
        for n, place in enumerate(places):
            start = pl.multiple_of(pair_at(where, place, pairs) * each, each)
            for (row, side), square in zip(held, squares):
                at = (where[1] ^ row) * 2 + lax.rem(where[0] + side, 2)
                at = pl.multiple_of(at * span, span)
                whole[n * each : (n + 1) * each, pl.ds(at, span)] = square[pl.ds(start, each), :]

    chunks = [
        ((row * cycles + a) * 2 + s) * BLK for row in range(n_rows) for s in range(2) for a in range(cycles)
    ]
    ordered = jnp.concatenate([left[at : at + BLK, :] for at in chunks], axis=0)
    total = (scale * jnp.dot(whole[...], ordered, preferred_element_type=F32)).astype(BF16)
    one[...] = total[:each]
    two[...] = total[each:]


def cube_terms(squares, held, left, where, scale, pairs, places):
    cols = squares[0].shape[0]
    depth, lanes = left.shape
    each = cols // pairs
    block = 2 * LANES
    return call(
        functools.partial(cube_terms_kernel, scale, pairs, places, held),
        flops=4 * each * lanes * depth,
        moved=2 * (cols * depth + lanes * depth + 2 * each * lanes),
        out_shape=[jax.ShapeDtypeStruct((each, lanes), BF16)] * 2,
        grid_spec=pltpu.PrefetchScalarGridSpec(
            num_scalar_prefetch=1,
            grid=(lanes // block,),
            in_specs=[pl.BlockSpec(part.shape, lambda i, where: (0, 0)) for part in squares]
            + [pl.BlockSpec((depth, block), lambda i, where: (0, i))],
            out_specs=[pl.BlockSpec((each, block), lambda i, where: (0, i))] * 2,
            scratch_shapes=[pltpu.VMEM((2 * each, depth), BF16)],
        ),
    )(where, *squares, left)


def filter_kernel(depths, tile_rows, tile_cols, where, filtering, mask):
    cols, lanes = mask.shape
    tiles = filtering.shape[0]
    row = lax.broadcasted_iota(jnp.int32, (tiles, lanes), 1) // BLK * depths
    rows = lax.broadcasted_iota(jnp.int32, (tiles, lanes), 0) == (
        row + where[1] * tile_rows + where[0]
    )
    col = lax.broadcasted_iota(jnp.int32, (cols, tiles), 0) // BLK + where[2] * tile_cols
    cols_of = lax.broadcasted_iota(jnp.int32, (cols, tiles), 1) == col
    spread = lax.dot_general(
        filtering[...].astype(F32), rows.astype(F32), (((0,), (0,)), ((), ())),
        preferred_element_type=F32,
    )
    mask[...] = jnp.dot(cols_of.astype(F32), spread, preferred_element_type=F32).astype(BF16)


def filter_mask(filtering, where, depths, tile_rows, tile_cols):
    shape = (tile_cols * BLK, tile_rows // depths * BLK)
    return call(
        functools.partial(filter_kernel, depths, tile_rows, tile_cols),
        out_shape=jax.ShapeDtypeStruct(shape, BF16),
        grid_spec=pltpu.PrefetchScalarGridSpec(
            num_scalar_prefetch=1,
            grid=(1,),
            in_specs=[pl.BlockSpec(filtering.shape, lambda i, where: (0, 0))],
            out_specs=pl.BlockSpec(shape, lambda i, where: (0, 0)),
        ),
    )(where, filtering)


def update_kernel(where, left, *refs):
    *terms, keep, send = refs
    cube = 0.0
    for part in terms:
        cube = cube + part[...].astype(F32)
    new = 1.5 * left[...].astype(F32) - 0.5 * cube
    first = lax.rem(where[0], 2) == 0
    low, high = new[:BLK, :], new[BLK:, :]
    keep[...] = jnp.where(first, low, high).astype(BF16)
    send[...] = jnp.where(first, high, low).astype(BF16)


def update(left, terms, where):
    shape = (BLK, left.shape[1])
    whole = pl.BlockSpec(left.shape, lambda i, where: (0, 0))
    half = pl.BlockSpec(shape, lambda i, where: (0, 0))
    return call(
        update_kernel,
        out_shape=[jax.ShapeDtypeStruct(shape, BF16)] * 2,
        grid_spec=pltpu.PrefetchScalarGridSpec(
            num_scalar_prefetch=1, grid=(1,), in_specs=[whole] * (1 + len(terms)), out_specs=[half, half]
        ),
    )(where, left, *terms)


def join_kernel(pairs, cycles, where, keep, got, out):
    first = lax.rem(where[0], 2) == 0
    low = lax.broadcasted_iota(jnp.int32, (BLK, LANES), 1) < BLK
    for q in range(pairs):
        for a in range(0, cycles, 2):
            at = (q * cycles + a) * BLK
            mine = keep[:, at : at + LANES].astype(F32)
            other = got[:, at : at + LANES].astype(F32)
            one, two = jnp.where(first, mine, other), jnp.where(first, other, mine)
            even = jnp.where(low, one, pltpu.roll(two, BLK, 1))
            odd = jnp.where(low, pltpu.roll(one, BLK, 1), two)
            for b, value in ((a, even), (a + 1, odd)):
                to = (b * pairs + q) * LANES
                out[:, to : to + LANES] = value.astype(BF16)


def join(keep, got, where, pairs):
    width, lanes = keep.shape
    half = pl.BlockSpec(keep.shape, lambda i, where: (0, 0))
    return call(
        functools.partial(join_kernel, pairs, lanes // (pairs * BLK)),
        out_shape=jax.ShapeDtypeStruct((width, 2 * lanes), BF16),
        grid_spec=pltpu.PrefetchScalarGridSpec(
            num_scalar_prefetch=1,
            grid=(1,),
            in_specs=[half, half],
            out_specs=pl.BlockSpec((width, 2 * lanes), lambda i, where: (0, 0)),
        ),
    )(where, keep, got)


def shards(matrix, occupancy, filtering):
    rows = lax.axis_size("row")
    depths = lax.axis_size("depth")
    pairs = depths // 2
    row, col, depth = (lax.axis_index(name) for name in ("row", "col", "depth"))
    local_rows, local_cols = matrix.shape
    scale = (local_rows * rows / 2.0) ** (-0.5)
    where = jnp.stack([depth, row, col]).astype(jnp.int32)

    def along_col(value, dx, dz):
        def target(r, c):
            forward = 1 - 2 * (r % 2)
            x, z = (c // RING + dx * forward) % RING, (c + dz * forward) % RING
            return r * RING * RING + x * RING + z

        route = [(r * RING * RING + c, target(r, c)) for r in range(rows) for c in range(RING * RING)]
        return lax.ppermute(value, ("row", "col"), route)

    def chain(value, dx, dz):
        held = [value]
        for _ in range(RING - 1):
            held.append(along_col(held[-1], dx, dz))
        return held

    def swap_row(value, bit):
        return lax.ppermute(value, "row", [(r, r ^ bit) for r in range(rows)])

    def to_other_side(value):
        return lax.ppermute(value, "depth", [(d, d ^ 1) for d in range(depths)])

    def to_pair(value, ahead):
        def target(r, d):
            return r * depths + (d + 2 * ahead * (1 - 2 * (r % 2))) % depths

        route = [(r * depths + d, target(r, d)) for r in range(rows) for d in range(depths)]
        return lax.ppermute(value, ("row", "depth"), route)

    def terms_here(make):
        across, behind = make((ACROSS, BEHIND))
        across = to_pair(across, 1)
        behind = to_pair(behind, -1)
        ahead, here = make((AHEAD, HERE))
        ahead = to_pair((ahead.astype(F32) + across.astype(F32)).astype(BF16), 1)
        return here, behind, ahead

    left = left_part(matrix, occupancy, pairs, where)
    held = chain(left, 0, 1)
    first = chain(jnp.stack(held[:2]), 1, 0)
    last, later, first[3] = lax.optimization_barrier((jnp.stack(held[2:]), where, first[3]))
    last = chain(last, 1, 0)
    right = right_part(matrix, occupancy, pairs, where)
    right, last[1] = lax.optimization_barrier((right, last[1]))
    near, across = swap_row(right, 1), swap_row(right, 2)
    rights = [right, near, across, swap_row(across, 1)]
    pieces = held + first[1:] + last[1:]
    sources = [((0, dz),) for dz in range(RING)]
    sources += [((dx, 0), (dx, 1)) for dx in range(1, RING)]
    sources += [((dx, 2), (dx, 3)) for dx in range(1, RING)]
    panel = panel_of(pieces, sources, where)

    terms = terms_here(lambda places: square_terms(rights, panel, where, scale, pairs, places))
    first, later = lax.optimization_barrier((terms[0], where))
    mask = filter_mask(filtering, later, depths, local_rows // BLK, local_cols // BLK)
    square = sum(part.astype(F32) for part in (first,) + terms[1:])
    square = (square * mask.astype(F32)).astype(BF16)
    other, across, near = to_other_side(square), swap_row(square, 2), swap_row(square, 1)
    other_across = swap_row(other, 2)
    squares = [square, other, across, near, other_across]
    squares += [swap_row(other, 1), swap_row(across, 1), swap_row(other_across, 1)]
    held = ((0, 0), (0, 1), (2, 0), (1, 0), (2, 1), (1, 1), (3, 0), (3, 1))

    terms = terms_here(lambda places: cube_terms(squares, held, panel, where, scale, pairs, places))
    keep, send = update(left, terms, where)
    return join(keep, to_other_side(send), where, pairs).T


def solution(mesh):
    placed = (P("row", "col"), P("row", "col"), P())
    return jax.shard_map(
        shards, mesh=mesh, in_specs=placed, out_specs=P("row", ("col", "depth")), check_vma=False
    )
```

```python
import functools

import jax
import jax.numpy as jnp
from jax import lax
from jax.experimental import pallas as pl
from jax.experimental.pallas import tpu as pltpu
from jax.sharding import PartitionSpec as P

BLK = 64
LANES = 128
RING = 4
ALONG_Z = [[x * RING + z for z in range(RING)] for x in range(RING)]
ALONG_X = [[x * RING + z for x in range(RING)] for z in range(RING)]
BF16 = jnp.bfloat16
F32 = jnp.float32
F16 = jnp.float16


def call(kernel, flops=0, moved=1 << 20, vmem=24 << 20, **kwargs):
    return pl.pallas_call(
        kernel,
        compiler_params=pltpu.CompilerParams(vmem_limit_bytes=vmem),
        cost_estimate=pl.CostEstimate(flops=flops, bytes_accessed=moved, transcendentals=0),
        **kwargs,
    )


def tile_mask(scalars):
    shape = (1, BLK * len(scalars))
    tile = lax.broadcasted_iota(jnp.int32, shape, 1) // BLK
    mask = jnp.zeros(shape, F32)
    for t, value in enumerate(scalars):
        mask = jnp.where(tile == t, value.astype(F32), mask)
    return mask


def left_kernel(where, occ_t, rows, left):
    cycles, _, _, cols = rows.shape
    depths = occ_t.shape[1] // cycles
    for a in range(cycles):
        mask = tile_mask([occ_t[t, a * depths + where[0]] for t in range(cols // BLK)])
        left[a * BLK : (a + 1) * BLK, :] = (rows[a, 0].astype(F32) * mask).astype(BF16)


def left_part(matrix, occupancy, where, depths):
    local_rows, cols = matrix.shape
    cycles = local_rows // (depths * BLK)
    return call(
        left_kernel,
        vmem=60 << 20,
        out_shape=jax.ShapeDtypeStruct((cycles * BLK, cols), BF16),
        grid_spec=pltpu.PrefetchScalarGridSpec(
            num_scalar_prefetch=2,
            grid=(1,),
            in_specs=[pl.BlockSpec((cycles, 1, BLK, cols), lambda i, where, occ: (0, where[0], 0, 0))],
            out_specs=pl.BlockSpec((cycles * BLK, cols), lambda i, where, occ: (0, 0)),
        ),
    )(where, occupancy.T, matrix.reshape(cycles, depths, BLK, cols))


def right_kernel(occ_t, rows, right):
    tiles, cols = rows.shape[0] // BLK, rows.shape[1]
    for u in range(tiles):
        row = pl.program_id(0) * tiles + u
        mask = tile_mask([occ_t[t, row] for t in range(cols // BLK)])
        part = rows[u * BLK : (u + 1) * BLK, :].astype(F32)
        right[u * BLK : (u + 1) * BLK, :] = (part * mask).astype(BF16)


def right_part(matrix, occupancy):
    rows, cols = matrix.shape
    block = pl.BlockSpec((rows // 4, cols), lambda i, occ: (i, 0))
    return call(
        right_kernel,
        vmem=60 << 20,
        out_shape=jax.ShapeDtypeStruct(matrix.shape, BF16),
        grid_spec=pltpu.PrefetchScalarGridSpec(
            num_scalar_prefetch=1, grid=(4,), in_specs=[block], out_specs=block
        ),
    )(occupancy.T, matrix)


def filter_kernel(depths, tile_rows, tile_cols, where, filtering, mask):
    rows, cols = mask.shape
    tiles = filtering.shape[0]
    row = lax.broadcasted_iota(jnp.int32, (rows, tiles), 0) // BLK * depths
    of_row = lax.broadcasted_iota(jnp.int32, (rows, tiles), 1) == (
        row + where[1] * tile_rows + where[0]
    )
    col = lax.broadcasted_iota(jnp.int32, (tiles, cols), 1) // BLK + where[2] * tile_cols
    of_col = lax.broadcasted_iota(jnp.int32, (tiles, cols), 0) == col
    spread = jnp.dot(of_row.astype(F32), filtering[...].astype(F32), preferred_element_type=F32)
    mask[...] = jnp.dot(spread, of_col.astype(F32), preferred_element_type=F32).astype(BF16)


def filter_mask(filtering, where, depths, tile_rows, tile_cols):
    shape = (tile_rows // depths * BLK, tile_cols * BLK)
    return call(
        functools.partial(filter_kernel, depths, tile_rows, tile_cols),
        out_shape=jax.ShapeDtypeStruct(shape, BF16),
        grid_spec=pltpu.PrefetchScalarGridSpec(
            num_scalar_prefetch=1,
            grid=(1,),
            in_specs=[pl.BlockSpec(filtering.shape, lambda i, where: (0, 0))],
            out_specs=pl.BlockSpec(shape, lambda i, where: (0, 0)),
        ),
    )(where, filtering)


def left_at(left, row, a, rows):
    return left[pl.ds(pl.multiple_of((row * RING + a) * rows, rows), rows), :]


def square_kernel(held, scale, where, *refs):
    rights, left, out = refs[: len(held)], refs[len(held)], refs[-1]
    rows, depth = out.shape[0], left.shape[1]
    total = 0.0
    for q, right in zip(held, rights):
        for a in range(RING):
            part = right[a * depth : (a + 1) * depth, :]
            lefts = left_at(left, where[1] ^ q, a, rows)
            total = total + jnp.dot(lefts, part, preferred_element_type=F32)
    if len(refs) == len(held) + 2:
        out[...] = total
    else:
        sofar, mask = refs[len(held) + 1 : -1]
        out[...] = (scale * (total + sofar[...]) * mask[...].astype(F32)).astype(BF16)


def square_rows(rights, held, left, where, rows, scale, last=()):
    depth, cols = rights[0].shape
    half = cols // 2

    def block(height):
        return pl.BlockSpec((height, half), lambda i, where: (0, i))

    return call(
        functools.partial(square_kernel, held, scale),
        flops=2 * rows * depth * len(held) * cols,
        moved=2 * depth * len(held) * cols,
        vmem=30 << 20,
        out_shape=jax.ShapeDtypeStruct((rows, cols), BF16 if last else F32),
        grid_spec=pltpu.PrefetchScalarGridSpec(
            num_scalar_prefetch=1,
            grid=(2,),
            in_specs=[block(depth) for _ in rights]
            + [pl.BlockSpec(left.shape, lambda i, where: (0, 0))]
            + [block(rows) for _ in last],
            out_specs=block(rows),
        ),
    )(where, *rights, left, *last)


def cube_kernel(held, scale, where, *refs):
    *squares, left, own, out = refs
    rows = own.shape[0]
    total = 0.0
    for square, names in zip(squares, held):
        for n, q in enumerate(names):
            for a in range(RING):
                part = [
                    square[y, n, a * BLK : (a + 1) * BLK, :] for y in range(square.shape[0])
                ]
                lefts = left_at(left, where[1] ^ q, a, rows)
                part = jnp.concatenate(part, axis=0)
                total = total + jnp.dot(lefts, part, preferred_element_type=F32)
    new = 1.5 * own[...].astype(F32) - 0.5 * (scale * total)
    out[...] = new.astype(BF16).T


def new_columns(squares, held, left, own, where, scale, h):
    rows, cols = own.shape
    half = cols // 2
    return call(
        functools.partial(cube_kernel, held, scale),
        flops=2 * rows * half * left.shape[0] // rows * cols,
        moved=2 * left.shape[0] * cols,
        vmem=30 << 20,
        out_shape=jax.ShapeDtypeStruct((half, rows), BF16),
        grid_spec=pltpu.PrefetchScalarGridSpec(
            num_scalar_prefetch=1,
            grid=(1,),
            in_specs=[pl.BlockSpec(part.shape, lambda i, where: (0, 0, 0, 0)) for part in squares]
            + [
                pl.BlockSpec(left.shape, lambda i, where: (0, 0)),
                pl.BlockSpec((rows, half), lambda i, where: (0, h)),
            ],
            out_specs=pl.BlockSpec((half, rows), lambda i, where: (0, 0)),
        ),
    )(where, *squares, left, own)


def join_kernel(got, out):
    depths, _, lanes = got.shape
    low = lax.broadcasted_iota(jnp.int32, (BLK, LANES), 1) < BLK
    for d in range(0, depths, 2):
        for b in range(lanes // LANES):
            one, two = (got[d + s, :, b * LANES : (b + 1) * LANES].astype(F32) for s in (0, 1))
            even = jnp.where(low, one, pltpu.roll(two, BLK, 1))
            odd = jnp.where(low, pltpu.roll(one, BLK, 1), two)
            for a, value in ((2 * b, even), (2 * b + 1, odd)):
                at = (a * depths + d) * BLK
                out[:, at : at + LANES] = value.astype(BF16)


def join(got):
    depths, width, lanes = got.shape
    return call(join_kernel, out_shape=jax.ShapeDtypeStruct((width, depths * lanes), BF16))(got)


def shards(matrix, occupancy, filtering):
    rows = lax.axis_size("row")
    depths = lax.axis_size("depth")
    row, col, depth = (lax.axis_index(name) for name in ("row", "col", "depth"))
    local_rows, local_cols = matrix.shape
    half = local_cols // 2
    own_rows = local_rows // depths
    scale = (local_rows * rows / 2.0) ** (-0.5)
    where = jnp.stack([depth, row, col]).astype(jnp.int32)

    def gather_col(value, groups):
        return lax.all_gather(value, "col", axis=0, tiled=True, axis_index_groups=groups)

    def gather_depth(value):
        return lax.all_gather(value, "depth", axis=0)

    def swap_row(value, bit):
        return lax.ppermute(value, "row", [(r, r ^ bit) for r in range(rows)])

    own = left_part(matrix, occupancy, where, depths)
    along_z = gather_col(own.astype(F16), ALONG_Z)
    right, along_z = lax.optimization_barrier((right_part(matrix, occupancy), along_z))
    across, near = swap_row(right, 2), swap_row(right, 1)
    left = gather_col(along_z, ALONG_X)
    across, near, left, later = lax.optimization_barrier((across, near, left, where))
    both = swap_row(across, 1)
    left = left.astype(BF16)
    mask = filter_mask(filtering, later, depths, local_rows // BLK, local_cols // BLK)
    square = square_rows((right, near, across), (0, 1, 2), left, where, own_rows, scale)
    square = square_rows((both,), (3,), left, where, own_rows, scale, (square, mask))

    one, two = square[:, :half].astype(F16), square[:, half:].astype(F16)
    two_across = swap_row(two, 2)
    one = gather_depth(one[None])
    two_across, one = lax.optimization_barrier((two_across, one))
    one = one.astype(BF16)
    one_across, one_near = swap_row(one, 2), swap_row(one, 1)
    two = gather_depth(jnp.stack([two, two_across]))
    one_across, one_near, two = lax.optimization_barrier((one_across, one_near, two))
    two = two.astype(BF16)
    two_near = swap_row(two, 1)
    one_both = swap_row(one_across, 1)

    squares = (one, one_near, one_across, one_both)
    new_one = new_columns(squares, ((0,), (1,), (2,), (3,)), left, own, where, scale, 0)
    new_two = new_columns((two, two_near), ((0, 2), (1, 3)), left, own, where, scale, 1)
    new = jnp.concatenate([new_one, new_two]).reshape(depths, BLK, own_rows)
    return join(lax.all_to_all(new, "depth", 0, 0, tiled=True)).T


def solution(mesh):
    placed = (P("row", "col"), P("row", "col"), P())
    return jax.shard_map(
        shards, mesh=mesh, in_specs=placed, out_specs=P("row", ("col", "depth")), check_vma=False
    )
```

```python
import functools

import jax
import jax.numpy as jnp
from jax import lax
from jax.experimental import pallas as pl
from jax.experimental.pallas import tpu as pltpu
from jax.sharding import PartitionSpec as P

BLK = 64
LANES = 128
RING = 4
ALONG_Z = [[x * RING + z for z in range(RING)] for x in range(RING)]
ALONG_X = [[x * RING + z for x in range(RING)] for z in range(RING)]
BF16 = jnp.bfloat16
F32 = jnp.float32
F16 = jnp.float16


def call(kernel, flops=0, moved=1 << 20, vmem=24 << 20, **kwargs):
    return pl.pallas_call(
        kernel,
        compiler_params=pltpu.CompilerParams(vmem_limit_bytes=vmem),
        cost_estimate=pl.CostEstimate(flops=flops, bytes_accessed=moved, transcendentals=0),
        **kwargs,
    )


def spread_tiles(occ_t, cols):
    tiles = occ_t.shape[0]
    tile = lax.broadcasted_iota(jnp.int32, (tiles, cols), 1) // BLK
    spread = (lax.broadcasted_iota(jnp.int32, (tiles, cols), 0) == tile).astype(F32)
    return lax.dot_general(
        occ_t.astype(F32), spread, (((0,), (0,)), ((), ())), preferred_element_type=F32
    )


def left_kernel(where, occ_t, rows, left, table):
    cycles, _, _, cols = rows.shape
    depths = table.shape[0] // cycles
    table[...] = spread_tiles(occ_t[...], cols)
    for a in range(cycles):
        mask = table[pl.ds(a * depths + where[0], 1), :]
        left[a * BLK : (a + 1) * BLK, :] = (rows[a, 0].astype(F32) * mask).astype(BF16)


def left_part(matrix, occupancy, where, depths):
    local_rows, cols = matrix.shape
    cycles = local_rows // (depths * BLK)
    occ_t = occupancy.T
    return call(
        left_kernel,
        vmem=60 << 20,
        out_shape=jax.ShapeDtypeStruct((cycles * BLK, cols), BF16),
        grid_spec=pltpu.PrefetchScalarGridSpec(
            num_scalar_prefetch=1,
            grid=(1,),
            in_specs=[
                pl.BlockSpec(occ_t.shape, lambda i, where: (0, 0)),
                pl.BlockSpec((cycles, 1, BLK, cols), lambda i, where: (0, where[0], 0, 0)),
            ],
            out_specs=pl.BlockSpec((cycles * BLK, cols), lambda i, where: (0, 0)),
            scratch_shapes=[pltpu.VMEM((cycles * depths, cols), F32)],
        ),
    )(where, occ_t, matrix.reshape(cycles, depths, BLK, cols))


def right_kernel(occ_t, rows, right):
    tiles, cols = rows.shape[0] // BLK, rows.shape[1]
    table = spread_tiles(occ_t[...], cols)
    for u in range(tiles):
        part = rows[u * BLK : (u + 1) * BLK, :].astype(F32)
        right[u * BLK : (u + 1) * BLK, :] = (part * table[u : u + 1, :]).astype(BF16)


def right_part(matrix, occupancy):
    return call(
        right_kernel, vmem=30 << 20, out_shape=jax.ShapeDtypeStruct(matrix.shape, BF16)
    )(occupancy.T, matrix)


def filter_kernel(depths, tile_rows, tile_cols, where, filtering, mask):
    rows, cols = mask.shape
    tiles = filtering.shape[0]
    row = lax.broadcasted_iota(jnp.int32, (rows, tiles), 0) // BLK * depths
    of_row = lax.broadcasted_iota(jnp.int32, (rows, tiles), 1) == (
        row + where[1] * tile_rows + where[0]
    )
    col = lax.broadcasted_iota(jnp.int32, (tiles, cols), 1) // BLK + where[2] * tile_cols
    of_col = lax.broadcasted_iota(jnp.int32, (tiles, cols), 0) == col
    spread = jnp.dot(of_row.astype(F32), filtering[...].astype(F32), preferred_element_type=F32)
    mask[...] = jnp.dot(spread, of_col.astype(F32), preferred_element_type=F32).astype(BF16)


def filter_mask(filtering, where, depths, tile_rows, tile_cols):
    shape = (tile_rows // depths * BLK, tile_cols * BLK)
    return call(
        functools.partial(filter_kernel, depths, tile_rows, tile_cols),
        out_shape=jax.ShapeDtypeStruct(shape, BF16),
        grid_spec=pltpu.PrefetchScalarGridSpec(
            num_scalar_prefetch=1,
            grid=(1,),
            in_specs=[pl.BlockSpec(filtering.shape, lambda i, where: (0, 0))],
            out_specs=pl.BlockSpec(shape, lambda i, where: (0, 0)),
        ),
    )(where, filtering)


def terms_kernel(held, scale, where, right, left, *outs):
    rows, inner = outs[0].shape[-2], left.shape[1]
    total = 0.0
    for a in range(RING):
        lefts = []
        for q in held:
            at = pl.multiple_of(((where[1] ^ q) * RING + a) * rows, rows)
            lefts.append(left[pl.ds(at, rows), :])
        if len(right.shape) == 2:
            part = right[a * inner : (a + 1) * inner, :]
        else:
            part = [right[y, a * BLK : (a + 1) * BLK, :] for y in range(right.shape[0])]
            part = jnp.concatenate(part, axis=0)
        lefts = jnp.concatenate(lefts, axis=0)
        total = total + jnp.dot(lefts, part, preferred_element_type=F32)
    total = (scale * total).astype(BF16)
    for n in range(len(held)):
        part = total[n * rows : (n + 1) * rows]
        if len(outs) == 1:
            outs[0][n] = part
        else:
            outs[n][...] = part


def terms_of(right, left, where, scale, rows, held, together):
    cols = right.shape[-1]
    half = cols // 2
    block = right.shape[:-1] + (half,)
    lead = (0,) * (len(block) - 1)
    if together:
        out_shape = [jax.ShapeDtypeStruct((len(held), rows, cols), BF16)]
        out_specs = [pl.BlockSpec((len(held), rows, half), lambda i, where: (0, 0, i))]
    else:
        out_shape = [jax.ShapeDtypeStruct((rows, cols), BF16)] * len(held)
        out_specs = [pl.BlockSpec((rows, half), lambda i, where: (0, i))] * len(held)
    return call(
        functools.partial(terms_kernel, held, scale),
        flops=2 * rows * len(held) * RING * left.shape[1] * cols,
        moved=2 * (right.size + left.size // 2 + rows * len(held) * cols),
        out_shape=out_shape,
        grid_spec=pltpu.PrefetchScalarGridSpec(
            num_scalar_prefetch=1,
            grid=(2,),
            in_specs=[
                pl.BlockSpec(block, lambda i, where: lead + (i,)),
                pl.BlockSpec(left.shape, lambda i, where: (0, 0)),
            ],
            out_specs=out_specs,
        ),
    )(where, right, left)


def update_kernel(own, *refs):
    *terms, out = refs
    cube = 0.0
    for part in terms:
        cube = cube + part[...].astype(F32)
    out[...] = (1.5 * own[...].astype(F32) - 0.5 * cube).astype(BF16).T


def update(own, terms):
    shape = own.shape[::-1]
    return call(update_kernel, out_shape=jax.ShapeDtypeStruct(shape, BF16))(own, *terms)


def join_kernel(got, out):
    depths, _, lanes = got.shape
    low = lax.broadcasted_iota(jnp.int32, (BLK, LANES), 1) < BLK
    for d in range(0, depths, 2):
        for b in range(lanes // LANES):
            one, two = (got[d + s, :, b * LANES : (b + 1) * LANES].astype(F32) for s in (0, 1))
            even = jnp.where(low, one, pltpu.roll(two, BLK, 1))
            odd = jnp.where(low, pltpu.roll(one, BLK, 1), two)
            for a, value in ((2 * b, even), (2 * b + 1, odd)):
                at = (a * depths + d) * BLK
                out[:, at : at + LANES] = value.astype(BF16)


def join(got):
    depths, width, lanes = got.shape
    return call(join_kernel, out_shape=jax.ShapeDtypeStruct((width, depths * lanes), BF16))(got)


def shards(matrix, occupancy, filtering):
    rows = lax.axis_size("row")
    depths = lax.axis_size("depth")
    row, col, depth = (lax.axis_index(name) for name in ("row", "col", "depth"))
    local_rows, local_cols = matrix.shape
    own_rows = local_rows // depths
    scale = (local_rows * rows / 2.0) ** (-0.5)
    where = jnp.stack([depth, row, col]).astype(jnp.int32)

    def gather_col(value, groups):
        return lax.all_gather(value, "col", axis=0, tiled=True, axis_index_groups=groups)

    def swap_row(value, bit):
        return lax.ppermute(value, "row", [(r, r ^ bit) for r in range(rows)])

    def trade_x_and_row(value):
        places = [(r, x, z) for r in range(rows) for x in range(RING) for z in range(RING)]
        route = [((r * RING + x) * RING + z, (x * RING + r) * RING + z) for r, x, z in places]
        return lax.ppermute(value, ("row", "col"), route)

    def sum_over_row(right):
        [away] = terms_of(right, left, where, scale, own_rows, (1, 3), True)
        near, both = swap_row(away, 1)
        across, here = terms_of(right, left, where, scale, own_rows, (2, 0), False)
        across = swap_row((across.astype(F32) + both.astype(F32)).astype(BF16), 2)
        return here, near, across

    own = left_part(matrix, occupancy, where, depths)
    moved = trade_x_and_row(own.astype(F16))
    right = right_part(matrix, occupancy)
    right, moved = lax.optimization_barrier((right, moved))
    left = gather_col(gather_col(moved, ALONG_Z), ALONG_X).astype(BF16)

    here, near, across = sum_over_row(right)
    here, later = lax.optimization_barrier((here, where))
    mask = filter_mask(filtering, later, depths, local_rows // BLK, local_cols // BLK)
    square = sum(part.astype(F32) for part in (here, near, across)) * mask.astype(F32)
    square = square.astype(BF16).astype(F16)
    squares = lax.all_gather(square, "depth", axis=0).astype(BF16)

    new = update(own, sum_over_row(squares)).reshape(depths, BLK, own_rows)
    return join(lax.all_to_all(new, "depth", 0, 0, tiled=True)).T


def solution(mesh):
    placed = (P("row", "col"), P("row", "col"), P())
    return jax.shard_map(
        shards, mesh=mesh, in_specs=placed, out_specs=P("row", ("col", "depth")), check_vma=False
    )
```

```python
import functools

import jax
import jax.numpy as jnp
from jax import lax
from jax.experimental import pallas as pl
from jax.experimental.pallas import tpu as pltpu
from jax.sharding import PartitionSpec as P

BLK = 64
LANES = 128
RING = 4
ALONG_Z = [[x * RING + z for z in range(RING)] for x in range(RING)]
ALONG_X = [[x * RING + z for x in range(RING)] for z in range(RING)]
BF16 = jnp.bfloat16
F32 = jnp.float32
F16 = jnp.float16


def call(kernel, flops=0, moved=1 << 20, vmem=24 << 20, **kwargs):
    return pl.pallas_call(
        kernel,
        compiler_params=pltpu.CompilerParams(vmem_limit_bytes=vmem),
        cost_estimate=pl.CostEstimate(flops=flops, bytes_accessed=moved, transcendentals=0),
        **kwargs,
    )


def spread_tiles(occ_t, cols):
    tiles = occ_t.shape[0]
    tile = lax.broadcasted_iota(jnp.int32, (tiles, cols), 1) // BLK
    spread = (lax.broadcasted_iota(jnp.int32, (tiles, cols), 0) == tile).astype(F32)
    return lax.dot_general(
        occ_t.astype(F32), spread, (((0,), (0,)), ((), ())), preferred_element_type=F32
    )


def left_kernel(where, occ_t, rows, left, table):
    cycles, _, _, cols = rows.shape
    depths = table.shape[0] // cycles
    table[...] = spread_tiles(occ_t[...], cols)
    for a in range(cycles):
        mask = table[pl.ds(a * depths + where[0], 1), :]
        left[a * BLK : (a + 1) * BLK, :] = (rows[a, 0].astype(F32) * mask).astype(BF16)


def left_part(matrix, occupancy, where, depths):
    local_rows, cols = matrix.shape
    cycles = local_rows // (depths * BLK)
    occ_t = occupancy.T
    return call(
        left_kernel,
        vmem=60 << 20,
        out_shape=jax.ShapeDtypeStruct((cycles * BLK, cols), BF16),
        grid_spec=pltpu.PrefetchScalarGridSpec(
            num_scalar_prefetch=1,
            grid=(1,),
            in_specs=[
                pl.BlockSpec(occ_t.shape, lambda i, where: (0, 0)),
                pl.BlockSpec((cycles, 1, BLK, cols), lambda i, where: (0, where[0], 0, 0)),
            ],
            out_specs=pl.BlockSpec((cycles * BLK, cols), lambda i, where: (0, 0)),
            scratch_shapes=[pltpu.VMEM((cycles * depths, cols), F32)],
        ),
    )(where, occ_t, matrix.reshape(cycles, depths, BLK, cols))


def right_kernel(occ_t, rows, right):
    tiles, cols = rows.shape[0] // BLK, rows.shape[1]
    table = spread_tiles(occ_t[...], cols)
    for u in range(tiles):
        part = rows[u * BLK : (u + 1) * BLK, :].astype(F32)
        right[u * BLK : (u + 1) * BLK, :] = (part * table[u : u + 1, :]).astype(BF16)


def right_part(matrix, occupancy):
    return call(
        right_kernel, vmem=30 << 20, out_shape=jax.ShapeDtypeStruct(matrix.shape, BF16)
    )(occupancy.T, matrix)


def filter_kernel(depths, tile_rows, tile_cols, where, filtering, mask):
    rows, cols = mask.shape
    tiles = filtering.shape[0]
    row = lax.broadcasted_iota(jnp.int32, (rows, tiles), 0) // BLK * depths
    of_row = lax.broadcasted_iota(jnp.int32, (rows, tiles), 1) == (
        row + where[1] * tile_rows + where[0]
    )
    col = lax.broadcasted_iota(jnp.int32, (tiles, cols), 1) // BLK + where[2] * tile_cols
    of_col = lax.broadcasted_iota(jnp.int32, (tiles, cols), 0) == col
    spread = jnp.dot(of_row.astype(F32), filtering[...].astype(F32), preferred_element_type=F32)
    mask[...] = jnp.dot(spread, of_col.astype(F32), preferred_element_type=F32).astype(BF16)


def filter_mask(filtering, where, depths, tile_rows, tile_cols):
    shape = (tile_rows // depths * BLK, tile_cols * BLK)
    return call(
        functools.partial(filter_kernel, depths, tile_rows, tile_cols),
        out_shape=jax.ShapeDtypeStruct(shape, BF16),
        grid_spec=pltpu.PrefetchScalarGridSpec(
            num_scalar_prefetch=1,
            grid=(1,),
            in_specs=[pl.BlockSpec(filtering.shape, lambda i, where: (0, 0))],
            out_specs=pl.BlockSpec(shape, lambda i, where: (0, 0)),
        ),
    )(where, filtering)


def terms_kernel(held, scale, where, right, left, *outs):
    rows, inner = outs[0].shape[-2], left.shape[1]
    total = 0.0
    for a in range(RING):
        lefts = []
        for q in held:
            place = (where[1] + (where[1] ^ q)) & (RING - 1)
            at = pl.multiple_of((place * RING + a) * rows, rows)
            lefts.append(left[pl.ds(at, rows), :])
        if len(right.shape) == 2:
            part = right[a * inner : (a + 1) * inner, :]
        else:
            part = [right[y, a * BLK : (a + 1) * BLK, :] for y in range(right.shape[0])]
            part = jnp.concatenate(part, axis=0)
        lefts = jnp.concatenate(lefts, axis=0)
        total = total + jnp.dot(lefts, part, preferred_element_type=F32)
    total = (scale * total).astype(BF16)
    for n in range(len(held)):
        part = total[n * rows : (n + 1) * rows]
        if len(outs[0].shape) == 3:
            outs[0][n] = part
        else:
            outs[n][...] = part


def terms_of(right, left, where, scale, rows, held, together):
    cols = right.shape[-1]
    half = cols // 2
    block = right.shape[:-1] + (half,)
    lead = (0,) * (len(block) - 1)
    if together:
        out_shape = [jax.ShapeDtypeStruct((len(held), rows, cols), BF16)]
        out_specs = [pl.BlockSpec((len(held), rows, half), lambda i, where: (0, 0, i))]
    else:
        out_shape = [jax.ShapeDtypeStruct((rows, cols), BF16)] * len(held)
        out_specs = [pl.BlockSpec((rows, half), lambda i, where: (0, i))] * len(held)
    return call(
        functools.partial(terms_kernel, held, scale),
        flops=2 * rows * len(held) * RING * left.shape[1] * cols,
        moved=2 * (right.size + left.size // 2 + rows * len(held) * cols),
        out_shape=out_shape,
        grid_spec=pltpu.PrefetchScalarGridSpec(
            num_scalar_prefetch=1,
            grid=(2,),
            in_specs=[
                pl.BlockSpec(block, lambda i, where: lead + (i,)),
                pl.BlockSpec(left.shape, lambda i, where: (0, 0)),
            ],
            out_specs=out_specs,
        ),
    )(where, right, left)


def update_kernel(own, *refs):
    *terms, out = refs
    cube = 0.0
    for part in terms:
        cube = cube + part[...].astype(F32)
    out[...] = (1.5 * own[...].astype(F32) - 0.5 * cube).astype(BF16).T


def update(own, terms):
    shape = own.shape[::-1]
    return call(update_kernel, out_shape=jax.ShapeDtypeStruct(shape, BF16))(own, *terms)


def join_kernel(got, out):
    depths, _, lanes = got.shape
    low = lax.broadcasted_iota(jnp.int32, (BLK, LANES), 1) < BLK
    for d in range(0, depths, 2):
        for b in range(lanes // LANES):
            one, two = (got[d + s, :, b * LANES : (b + 1) * LANES].astype(F32) for s in (0, 1))
            even = jnp.where(low, one, pltpu.roll(two, BLK, 1))
            odd = jnp.where(low, pltpu.roll(one, BLK, 1), two)
            for a, value in ((2 * b, even), (2 * b + 1, odd)):
                at = (a * depths + d) * BLK
                out[:, at : at + LANES] = value.astype(BF16)


def join(got):
    depths, width, lanes = got.shape
    return call(join_kernel, out_shape=jax.ShapeDtypeStruct((width, depths * lanes), BF16))(got)


def shards(matrix, occupancy, filtering):
    rows = lax.axis_size("row")
    depths = lax.axis_size("depth")
    row, col, depth = (lax.axis_index(name) for name in ("row", "col", "depth"))
    local_rows, local_cols = matrix.shape
    own_rows = local_rows // depths
    scale = (local_rows * rows / 2.0) ** (-0.5)
    where = jnp.stack([depth, row, col]).astype(jnp.int32)

    def gather_col(value, groups):
        return lax.all_gather(value, "col", axis=0, tiled=True, axis_index_groups=groups)

    def swap_row(value, bit):
        return lax.ppermute(value, "row", [(r, r ^ bit) for r in range(rows)])

    def trade_x_and_row(value):
        places = [(r, x, z) for r in range(rows) for x in range(RING) for z in range(RING)]
        route = [
            ((r * RING + x) * RING + z, (x * RING + (x + r) % RING) * RING + z) for r, x, z in places
        ]
        return lax.ppermute(value, ("row", "col"), route)

    def sum_over_row(right):
        [away] = terms_of(right, left, where, scale, own_rows, (1, 3), True)
        near, both = swap_row(away, 1)
        [across] = terms_of(right, left, where, scale, own_rows, (2,), False)
        across = swap_row((across.astype(F32) + both.astype(F32)).astype(BF16), 2)
        [here] = terms_of(right, left, where, scale, own_rows, (0,), False)
        return here, near, across

    own = left_part(matrix, occupancy, depth.astype(jnp.int32)[None], depths)
    moved = trade_x_and_row(own.astype(F16))
    right = right_part(matrix, occupancy)
    right, moved = lax.optimization_barrier((right, moved))
    left = gather_col(gather_col(moved, ALONG_Z), ALONG_X).astype(BF16)

    here, near, across = sum_over_row(right)
    here, later = lax.optimization_barrier((here, where))
    mask = filter_mask(filtering, later, depths, local_rows // BLK, local_cols // BLK)
    square = sum(part.astype(F32) for part in (here, near, across)) * mask.astype(F32)
    square = square.astype(BF16).astype(F16)
    squares = lax.all_gather(square, "depth", axis=0).astype(BF16)

    new = update(own, sum_over_row(squares)).reshape(depths, BLK, own_rows)
    return join(lax.all_to_all(new, "depth", 0, 0, tiled=True)).T


def solution(mesh):
    placed = (P("row", "col"), P("row", "col"), P())
    return jax.shard_map(
        shards, mesh=mesh, in_specs=placed, out_specs=P("row", ("col", "depth")), check_vma=False
    )
```

```python
import functools

import jax
import jax.numpy as jnp
from jax import lax
from jax.experimental import pallas as pl
from jax.experimental.pallas import tpu as pltpu
from jax.sharding import PartitionSpec as P

BLK = 64
LANES = 128
RING = 4
ALONG_Z = [[x * RING + z for z in range(RING)] for x in range(RING)]
ALONG_X = [[x * RING + z for x in range(RING)] for z in range(RING)]
BF16 = jnp.bfloat16
F32 = jnp.float32
F16 = jnp.float16


def call(kernel, flops=0, moved=1 << 20, vmem=24 << 20, **kwargs):
    return pl.pallas_call(
        kernel,
        compiler_params=pltpu.CompilerParams(vmem_limit_bytes=vmem),
        cost_estimate=pl.CostEstimate(flops=flops, bytes_accessed=moved, transcendentals=0),
        **kwargs,
    )


def spread_tiles(occ_t, cols):
    tiles = occ_t.shape[0]
    tile = lax.broadcasted_iota(jnp.int32, (tiles, cols), 1) // BLK
    spread = (lax.broadcasted_iota(jnp.int32, (tiles, cols), 0) == tile).astype(F32)
    return lax.dot_general(
        occ_t.astype(F32), spread, (((0,), (0,)), ((), ())), preferred_element_type=F32
    )


def left_kernel(where, occ_t, rows, left, table):
    cycles, _, _, cols = rows.shape
    depths = table.shape[0] // cycles
    table[...] = spread_tiles(occ_t[...], cols)
    for a in range(cycles):
        mask = table[pl.ds(a * depths + where[0], 1), :]
        left[a * BLK : (a + 1) * BLK, :] = (rows[a, 0].astype(F32) * mask).astype(BF16)


def left_part(matrix, occupancy, where, depths):
    local_rows, cols = matrix.shape
    cycles = local_rows // (depths * BLK)
    occ_t = occupancy.T
    return call(
        left_kernel,
        vmem=60 << 20,
        out_shape=jax.ShapeDtypeStruct((cycles * BLK, cols), BF16),
        grid_spec=pltpu.PrefetchScalarGridSpec(
            num_scalar_prefetch=1,
            grid=(1,),
            in_specs=[
                pl.BlockSpec(occ_t.shape, lambda i, where: (0, 0)),
                pl.BlockSpec((cycles, 1, BLK, cols), lambda i, where: (0, where[0], 0, 0)),
            ],
            out_specs=pl.BlockSpec((cycles * BLK, cols), lambda i, where: (0, 0)),
            scratch_shapes=[pltpu.VMEM((cycles * depths, cols), F32)],
        ),
    )(where, occ_t, matrix.reshape(cycles, depths, BLK, cols))


def right_kernel(occ_t, rows, right):
    tiles, cols = rows.shape[0] // BLK, rows.shape[1]
    table = spread_tiles(occ_t[...], cols)
    for u in range(tiles):
        part = rows[u * BLK : (u + 1) * BLK, :].astype(F32)
        right[u * BLK : (u + 1) * BLK, :] = (part * table[u : u + 1, :]).astype(BF16)


def right_part(matrix, occupancy):
    return call(
        right_kernel, vmem=30 << 20, out_shape=jax.ShapeDtypeStruct(matrix.shape, BF16)
    )(occupancy.T, matrix)


def filter_kernel(depths, tile_rows, tile_cols, where, filtering, mask):
    rows, cols = mask.shape
    tiles = filtering.shape[0]
    row = lax.broadcasted_iota(jnp.int32, (rows, tiles), 0) // BLK * depths
    of_row = lax.broadcasted_iota(jnp.int32, (rows, tiles), 1) == (
        row + where[1] * tile_rows + where[0]
    )
    col = lax.broadcasted_iota(jnp.int32, (tiles, cols), 1) // BLK + where[2] * tile_cols
    of_col = lax.broadcasted_iota(jnp.int32, (tiles, cols), 0) == col
    spread = jnp.dot(of_row.astype(F32), filtering[...].astype(F32), preferred_element_type=F32)
    mask[...] = jnp.dot(spread, of_col.astype(F32), preferred_element_type=F32).astype(BF16)


def filter_mask(filtering, where, depths, tile_rows, tile_cols):
    shape = (tile_rows // depths * BLK, tile_cols * BLK)
    return call(
        functools.partial(filter_kernel, depths, tile_rows, tile_cols),
        out_shape=jax.ShapeDtypeStruct(shape, BF16),
        grid_spec=pltpu.PrefetchScalarGridSpec(
            num_scalar_prefetch=1,
            grid=(1,),
            in_specs=[pl.BlockSpec(filtering.shape, lambda i, where: (0, 0))],
            out_specs=pl.BlockSpec(shape, lambda i, where: (0, 0)),
        ),
    )(where, filtering)


def step_along_x(row):
    return (row & 1) * 2 + row // 2


def terms_kernel(held, scale, where, right, left, *outs):
    rows, inner = outs[0].shape[-2], left.shape[1]
    total = 0.0
    for a in range(RING):
        lefts = []
        for q in held:
            place = (where[1] + step_along_x(where[1] ^ q)) & (RING - 1)
            at = pl.multiple_of((place * RING + a) * rows, rows)
            lefts.append(left[pl.ds(at, rows), :])
        if len(right.shape) == 2:
            part = right[a * inner : (a + 1) * inner, :]
        else:
            part = [right[y, a * BLK : (a + 1) * BLK, :] for y in range(right.shape[0])]
            part = jnp.concatenate(part, axis=0)
        lefts = jnp.concatenate(lefts, axis=0)
        total = total + jnp.dot(lefts, part, preferred_element_type=F32)
    total = (scale * total).astype(BF16)
    for n in range(len(held)):
        part = total[n * rows : (n + 1) * rows]
        if len(outs[0].shape) == 3:
            outs[0][n] = part
        else:
            outs[n][...] = part


def terms_of(right, left, where, scale, rows, held, together):
    cols = right.shape[-1]
    vmem = pl.BlockSpec(memory_space=pltpu.VMEM)
    if together:
        out_shape = [jax.ShapeDtypeStruct((len(held), rows, cols), BF16)]
    else:
        out_shape = [jax.ShapeDtypeStruct((rows, cols), BF16)] * len(held)
    return call(
        functools.partial(terms_kernel, held, scale),
        flops=2 * rows * len(held) * RING * left.shape[1] * cols,
        moved=2 * (right.size + left.size // 2 + rows * len(held) * cols),
        out_shape=out_shape,
        in_specs=[pl.BlockSpec(memory_space=pltpu.SMEM), vmem, vmem],
        out_specs=[vmem] * len(out_shape),
    )(where, right, left)


def update_kernel(own, *refs):
    *terms, out = refs
    cube = 0.0
    for part in terms:
        cube = cube + part[...].astype(F32)
    out[...] = (1.5 * own[...].astype(F32) - 0.5 * cube).astype(BF16).T


def update(own, terms):
    shape = own.shape[::-1]
    return call(update_kernel, out_shape=jax.ShapeDtypeStruct(shape, BF16))(own, *terms)


def join_kernel(got, out):
    depths, _, lanes = got.shape
    low = lax.broadcasted_iota(jnp.int32, (BLK, LANES), 1) < BLK
    for d in range(0, depths, 2):
        for b in range(lanes // LANES):
            one, two = (got[d + s, :, b * LANES : (b + 1) * LANES].astype(F32) for s in (0, 1))
            even = jnp.where(low, one, pltpu.roll(two, BLK, 1))
            odd = jnp.where(low, pltpu.roll(one, BLK, 1), two)
            for a, value in ((2 * b, even), (2 * b + 1, odd)):
                at = (a * depths + d) * BLK
                out[:, at : at + LANES] = value.astype(BF16)


def join(got):
    depths, width, lanes = got.shape
    return call(join_kernel, out_shape=jax.ShapeDtypeStruct((width, depths * lanes), BF16))(got)


def shards(matrix, occupancy, filtering):
    rows = lax.axis_size("row")
    depths = lax.axis_size("depth")
    row, col, depth = (lax.axis_index(name) for name in ("row", "col", "depth"))
    local_rows, local_cols = matrix.shape
    own_rows = local_rows // depths
    scale = (local_rows * rows / 2.0) ** (-0.5)
    where = jnp.stack([depth, row, col]).astype(jnp.int32)

    def gather_col(value, groups):
        return lax.all_gather(value, "col", axis=0, tiled=True, axis_index_groups=groups)

    def swap_row(value, bit):
        return lax.ppermute(value, "row", [(r, r ^ bit) for r in range(rows)])

    def trade_x_and_row(value):
        places = [(r, x, z) for r in range(rows) for x in range(RING) for z in range(RING)]
        route = [
            ((r * RING + x) * RING + z, (x * RING + (x + step_along_x(r)) % RING) * RING + z)
            for r, x, z in places
        ]
        return lax.ppermute(value, ("row", "col"), route)

    def sum_over_row(right):
        [away] = terms_of(right, left, where, scale, own_rows, (1, 3), True)
        near, both = swap_row(away, 1)
        [across] = terms_of(right, left, where, scale, own_rows, (2,), False)
        across = swap_row((across.astype(F32) + both.astype(F32)).astype(BF16), 2)
        [here] = terms_of(right, left, where, scale, own_rows, (0,), False)
        return here, near, across

    own = left_part(matrix, occupancy, depth.astype(jnp.int32)[None], depths)
    moved = trade_x_and_row(own.astype(F16))
    right = right_part(matrix, occupancy)
    right, moved = lax.optimization_barrier((right, moved))
    left = gather_col(gather_col(moved, ALONG_Z), ALONG_X).astype(BF16)

    here, near, across = sum_over_row(right)
    here, later = lax.optimization_barrier((here, where))
    mask = filter_mask(filtering, later, depths, local_rows // BLK, local_cols // BLK)
    square = sum(part.astype(F32) for part in (here, near, across)) * mask.astype(F32)
    square = square.astype(BF16).astype(F16)
    squares = lax.all_gather(square, "depth", axis=0).astype(BF16)

    new = update(own, sum_over_row(squares)).reshape(depths, BLK, own_rows)
    return join(lax.all_to_all(new, "depth", 0, 0, tiled=True)).T


def solution(mesh):
    placed = (P("row", "col"), P("row", "col"), P())
    return jax.shard_map(
        shards, mesh=mesh, in_specs=placed, out_specs=P("row", ("col", "depth")), check_vma=False
    )
```

```python
import functools

import jax
import jax.numpy as jnp
from jax import lax
from jax.experimental import pallas as pl
from jax.experimental.pallas import tpu as pltpu
from jax.sharding import PartitionSpec as P

BLK = 64
LANES = 128
RING = 4
ALONG_Z = [[x * RING + z for z in range(RING)] for x in range(RING)]
ALONG_X = [[x * RING + z for x in range(RING)] for z in range(RING)]
BF16 = jnp.bfloat16
F32 = jnp.float32
F16 = jnp.float16


def call(kernel, flops=0, moved=1 << 20, vmem=24 << 20, **kwargs):
    return pl.pallas_call(
        kernel,
        compiler_params=pltpu.CompilerParams(vmem_limit_bytes=vmem),
        cost_estimate=pl.CostEstimate(flops=flops, bytes_accessed=moved, transcendentals=0),
        **kwargs,
    )


def spread_tiles(occ_t, cols):
    tiles = occ_t.shape[0]
    tile = lax.broadcasted_iota(jnp.int32, (tiles, cols), 1) // BLK
    spread = (lax.broadcasted_iota(jnp.int32, (tiles, cols), 0) == tile).astype(F32)
    return lax.dot_general(
        occ_t.astype(F32), spread, (((0,), (0,)), ((), ())), preferred_element_type=F32
    )


def left_kernel(where, occ_t, rows, left, table):
    cycles, _, _, cols = rows.shape
    depths = table.shape[0] // cycles
    table[...] = spread_tiles(occ_t[...], cols)
    for a in range(cycles):
        mask = table[pl.ds(a * depths + where[0], 1), :]
        left[a * BLK : (a + 1) * BLK, :] = (rows[a, 0].astype(F32) * mask).astype(BF16)


def left_part(matrix, occupancy, where, depths):
    local_rows, cols = matrix.shape
    cycles = local_rows // (depths * BLK)
    occ_t = occupancy.T
    return call(
        left_kernel,
        vmem=60 << 20,
        out_shape=jax.ShapeDtypeStruct((cycles * BLK, cols), BF16),
        grid_spec=pltpu.PrefetchScalarGridSpec(
            num_scalar_prefetch=1,
            grid=(1,),
            in_specs=[
                pl.BlockSpec(occ_t.shape, lambda i, where: (0, 0)),
                pl.BlockSpec((cycles, 1, BLK, cols), lambda i, where: (0, where[0], 0, 0)),
            ],
            out_specs=pl.BlockSpec((cycles * BLK, cols), lambda i, where: (0, 0)),
            scratch_shapes=[pltpu.VMEM((cycles * depths, cols), F32)],
        ),
    )(where, occ_t, matrix.reshape(cycles, depths, BLK, cols))


def right_kernel(occ_t, rows, right):
    tiles, cols = rows.shape[0] // BLK, rows.shape[1]
    table = spread_tiles(occ_t[...], cols)
    for u in range(tiles):
        part = rows[u * BLK : (u + 1) * BLK, :].astype(F32)
        right[u * BLK : (u + 1) * BLK, :] = (part * table[u : u + 1, :]).astype(BF16)


def right_part(matrix, occupancy):
    return call(
        right_kernel, vmem=30 << 20, out_shape=jax.ShapeDtypeStruct(matrix.shape, BF16)
    )(occupancy.T, matrix)


def filter_kernel(depths, tile_rows, tile_cols, where, filtering, mask):
    rows, cols = mask.shape
    tiles = filtering.shape[0]
    row = lax.broadcasted_iota(jnp.int32, (rows, tiles), 0) // BLK * depths
    of_row = lax.broadcasted_iota(jnp.int32, (rows, tiles), 1) == (
        row + where[1] * tile_rows + where[0]
    )
    col = lax.broadcasted_iota(jnp.int32, (tiles, cols), 1) // BLK + where[2] * tile_cols
    of_col = lax.broadcasted_iota(jnp.int32, (tiles, cols), 0) == col
    spread = jnp.dot(of_row.astype(F32), filtering[...].astype(F32), preferred_element_type=F32)
    mask[...] = jnp.dot(spread, of_col.astype(F32), preferred_element_type=F32).astype(BF16)


def filter_mask(filtering, where, depths, tile_rows, tile_cols):
    shape = (tile_rows // depths * BLK, tile_cols * BLK)
    return call(
        functools.partial(filter_kernel, depths, tile_rows, tile_cols),
        out_shape=jax.ShapeDtypeStruct(shape, BF16),
        grid_spec=pltpu.PrefetchScalarGridSpec(
            num_scalar_prefetch=1,
            grid=(1,),
            in_specs=[pl.BlockSpec(filtering.shape, lambda i, where: (0, 0))],
            out_specs=pl.BlockSpec(shape, lambda i, where: (0, 0)),
        ),
    )(where, filtering)


def step_along_x(row):
    return (row & 1) * 2 + row // 2


def terms_kernel(held, scale, where, right, left, *outs):
    rows, inner = outs[0].shape[-2], left.shape[1]
    total = 0.0
    for a in range(RING):
        lefts = []
        for q in held:
            place = (where[1] + step_along_x(where[1] ^ q)) & (RING - 1)
            at = pl.multiple_of((place * RING + a) * rows, rows)
            lefts.append(left[pl.ds(at, rows), :])
        if len(right.shape) == 2:
            part = right[a * inner : (a + 1) * inner, :]
        else:
            part = [right[y, a * BLK : (a + 1) * BLK, :] for y in range(right.shape[0])]
            part = jnp.concatenate(part, axis=0)
        lefts = jnp.concatenate(lefts, axis=0)
        total = total + jnp.dot(lefts, part, preferred_element_type=F32)
    total = (scale * total).astype(BF16)
    for n, out in enumerate(outs):
        out[...] = total[n * rows : (n + 1) * rows]


def terms_of(right, left, where, scale, rows, held):
    cols = right.shape[-1]
    vmem = pl.BlockSpec(memory_space=pltpu.VMEM)
    out_shape = [jax.ShapeDtypeStruct((rows, cols), BF16)] * len(held)
    return call(
        functools.partial(terms_kernel, held, scale),
        flops=2 * rows * len(held) * RING * left.shape[1] * cols,
        moved=2 * (right.size + left.size // 2 + rows * len(held) * cols),
        out_shape=out_shape,
        in_specs=[pl.BlockSpec(memory_space=pltpu.SMEM), vmem, vmem],
        out_specs=[vmem] * len(out_shape),
    )(where, right, left)


def update_kernel(own, *refs):
    *terms, out = refs
    cube = 0.0
    for part in terms:
        cube = cube + part[...].astype(F32)
    out[...] = (1.5 * own[...].astype(F32) - 0.5 * cube).astype(BF16).T


def update(own, terms):
    shape = own.shape[::-1]
    return call(update_kernel, out_shape=jax.ShapeDtypeStruct(shape, BF16))(own, *terms)


def join_kernel(got, out):
    depths, _, lanes = got.shape
    low = lax.broadcasted_iota(jnp.int32, (BLK, LANES), 1) < BLK
    for d in range(0, depths, 2):
        for b in range(lanes // LANES):
            one, two = (got[d + s, :, b * LANES : (b + 1) * LANES].astype(F32) for s in (0, 1))
            even = jnp.where(low, one, pltpu.roll(two, BLK, 1))
            odd = jnp.where(low, pltpu.roll(one, BLK, 1), two)
            for a, value in ((2 * b, even), (2 * b + 1, odd)):
                at = (a * depths + d) * BLK
                out[:, at : at + LANES] = value.astype(BF16)


def join(got):
    depths, width, lanes = got.shape
    return call(join_kernel, out_shape=jax.ShapeDtypeStruct((width, depths * lanes), BF16))(got)


def shards(matrix, occupancy, filtering):
    rows = lax.axis_size("row")
    depths = lax.axis_size("depth")
    row, col, depth = (lax.axis_index(name) for name in ("row", "col", "depth"))
    local_rows, local_cols = matrix.shape
    own_rows = local_rows // depths
    scale = (local_rows * rows / 2.0) ** (-0.5)
    where = jnp.stack([depth, row, col]).astype(jnp.int32)

    def gather_col(value, groups):
        return lax.all_gather(value, "col", axis=0, tiled=True, axis_index_groups=groups)

    def swap_row(value, bit):
        return lax.ppermute(value, "row", [(r, r ^ bit) for r in range(rows)])

    def trade_x_and_row(value):
        places = [(r, x, z) for r in range(rows) for x in range(RING) for z in range(RING)]
        route = [
            ((r * RING + x) * RING + z, (x * RING + (x + step_along_x(r)) % RING) * RING + z)
            for r, x, z in places
        ]
        return lax.ppermute(value, ("row", "col"), route)

    def sum_over_row(right):
        [both] = terms_of(right, left, where, scale, own_rows, (3,))
        both = swap_row(both, 1)
        [across] = terms_of(right, left, where, scale, own_rows, (2,))
        across = (across.astype(F32) + both.astype(F32)).astype(BF16)
        across, later = lax.optimization_barrier((across, where))
        across = swap_row(across, 2)
        near, here = terms_of(right, left, later, scale, own_rows, (1, 0))
        across, here = lax.optimization_barrier((across, here))
        return here, across, swap_row(near, 1)

    own = left_part(matrix, occupancy, depth.astype(jnp.int32)[None], depths)
    moved = trade_x_and_row(own.astype(F16))
    right = right_part(matrix, occupancy)
    mask = filter_mask(filtering, where, depths, local_rows // BLK, local_cols // BLK)
    right, mask, moved = lax.optimization_barrier((right, mask, moved))
    left = gather_col(gather_col(moved, ALONG_Z), ALONG_X).astype(BF16)

    here, across, near = sum_over_row(right)
    square = sum(part.astype(F32) for part in (here, across, near)) * mask.astype(F32)
    square = square.astype(BF16).astype(F16)
    squares = lax.all_gather(square, "depth", axis=0).astype(BF16)

    new = update(own, sum_over_row(squares)).reshape(depths, BLK, own_rows)
    return join(lax.all_to_all(new, "depth", 0, 0, tiled=True)).T


def solution(mesh):
    placed = (P("row", "col"), P("row", "col"), P())
    return jax.shard_map(
        shards, mesh=mesh, in_specs=placed, out_specs=P("row", ("col", "depth")), check_vma=False
    )
```

```python
import functools

import jax
import jax.numpy as jnp
from jax import lax
from jax.experimental import pallas as pl
from jax.experimental.pallas import tpu as pltpu
from jax.sharding import PartitionSpec as P

BLK = 64
LANES = 128
RING = 4
ALONG_Z = [[x * RING + z for z in range(RING)] for x in range(RING)]
ALONG_X = [[x * RING + z for x in range(RING)] for z in range(RING)]
BF16 = jnp.bfloat16
F32 = jnp.float32
F16 = jnp.float16


def call(kernel, flops=0, moved=1 << 20, vmem=24 << 20, **kwargs):
    return pl.pallas_call(
        kernel,
        compiler_params=pltpu.CompilerParams(vmem_limit_bytes=vmem),
        cost_estimate=pl.CostEstimate(flops=flops, bytes_accessed=moved, transcendentals=0),
        **kwargs,
    )


def spread_tiles(occ_t, cols):
    tiles = occ_t.shape[0]
    tile = lax.broadcasted_iota(jnp.int32, (tiles, cols), 1) // BLK
    spread = (lax.broadcasted_iota(jnp.int32, (tiles, cols), 0) == tile).astype(F32)
    return lax.dot_general(
        occ_t.astype(F32), spread, (((0,), (0,)), ((), ())), preferred_element_type=F32
    )


def left_kernel(where, occ_t, rows, left, table):
    cycles, _, _, cols = rows.shape
    depths = table.shape[0] // cycles
    table[...] = spread_tiles(occ_t[...], cols)
    for a in range(cycles):
        mask = table[pl.ds(a * depths + where[0], 1), :]
        left[a * BLK : (a + 1) * BLK, :] = (rows[a, 0].astype(F32) * mask).astype(BF16)


def left_part(matrix, occupancy, where, depths):
    local_rows, cols = matrix.shape
    cycles = local_rows // (depths * BLK)
    occ_t = occupancy.T
    return call(
        left_kernel,
        vmem=60 << 20,
        out_shape=jax.ShapeDtypeStruct((cycles * BLK, cols), BF16),
        grid_spec=pltpu.PrefetchScalarGridSpec(
            num_scalar_prefetch=1,
            grid=(1,),
            in_specs=[
                pl.BlockSpec(occ_t.shape, lambda i, where: (0, 0)),
                pl.BlockSpec((cycles, 1, BLK, cols), lambda i, where: (0, where[0], 0, 0)),
            ],
            out_specs=pl.BlockSpec((cycles * BLK, cols), lambda i, where: (0, 0)),
            scratch_shapes=[pltpu.VMEM((cycles * depths, cols), F32)],
        ),
    )(where, occ_t, matrix.reshape(cycles, depths, BLK, cols))


def right_kernel(occ_t, rows, right):
    tiles, cols = rows.shape[0] // BLK, rows.shape[1]
    table = spread_tiles(occ_t[...], cols)
    for u in range(tiles):
        part = rows[u * BLK : (u + 1) * BLK, :].astype(F32)
        right[u * BLK : (u + 1) * BLK, :] = (part * table[u : u + 1, :]).astype(BF16)


def right_part(matrix, occupancy):
    return call(
        right_kernel, vmem=30 << 20, out_shape=jax.ShapeDtypeStruct(matrix.shape, BF16)
    )(occupancy.T, matrix)


def filter_kernel(depths, tile_rows, tile_cols, where, filtering, mask):
    rows, cols = mask.shape
    tiles = filtering.shape[0]
    row = lax.broadcasted_iota(jnp.int32, (rows, tiles), 0) // BLK * depths
    of_row = lax.broadcasted_iota(jnp.int32, (rows, tiles), 1) == (
        row + where[1] * tile_rows + where[0]
    )
    col = lax.broadcasted_iota(jnp.int32, (tiles, cols), 1) // BLK + where[2] * tile_cols
    of_col = lax.broadcasted_iota(jnp.int32, (tiles, cols), 0) == col
    spread = jnp.dot(of_row.astype(F32), filtering[...].astype(F32), preferred_element_type=F32)
    mask[...] = jnp.dot(spread, of_col.astype(F32), preferred_element_type=F32).astype(BF16)


def filter_mask(filtering, where, depths, tile_rows, tile_cols):
    shape = (tile_rows // depths * BLK, tile_cols * BLK)
    return call(
        functools.partial(filter_kernel, depths, tile_rows, tile_cols),
        out_shape=jax.ShapeDtypeStruct(shape, BF16),
        grid_spec=pltpu.PrefetchScalarGridSpec(
            num_scalar_prefetch=1,
            grid=(1,),
            in_specs=[pl.BlockSpec(filtering.shape, lambda i, where: (0, 0))],
            out_specs=pl.BlockSpec(shape, lambda i, where: (0, 0)),
        ),
    )(where, filtering)


def step_along_x(row):
    return (row & 1) * 2 + row // 2


def terms_kernel(held, scale, where, right, left, *outs):
    rows, inner = outs[0].shape[-2], left.shape[1]
    total = 0.0
    for a in range(RING):
        lefts = []
        for q in held:
            place = (where[1] + step_along_x(where[1] ^ q)) & (RING - 1)
            at = pl.multiple_of((place * RING + a) * rows, rows)
            lefts.append(left[pl.ds(at, rows), :])
        if len(right.shape) == 2:
            part = right[a * inner : (a + 1) * inner, :]
        else:
            part = [right[y, a * BLK : (a + 1) * BLK, :] for y in range(right.shape[0])]
            part = jnp.concatenate(part, axis=0)
        lefts = jnp.concatenate(lefts, axis=0)
        total = total + jnp.dot(lefts, part, preferred_element_type=F32)
    total = (scale * total).astype(BF16)
    for n in range(len(held)):
        part = total[n * rows : (n + 1) * rows]
        if len(outs) == len(held):
            outs[n][...] = part
        else:
            outs[0][n] = part


def terms_of(right, left, where, scale, rows, held, together=False):
    cols = right.shape[-1]
    vmem = pl.BlockSpec(memory_space=pltpu.VMEM)
    out_shape = [jax.ShapeDtypeStruct((rows, cols), BF16)] * len(held)
    if together:
        out_shape = [jax.ShapeDtypeStruct((len(held), rows, cols), BF16)]
    return call(
        functools.partial(terms_kernel, held, scale),
        flops=2 * rows * len(held) * RING * left.shape[1] * cols,
        moved=2 * (right.size + left.size // 2 + rows * len(held) * cols),
        out_shape=out_shape,
        in_specs=[pl.BlockSpec(memory_space=pltpu.SMEM), vmem, vmem],
        out_specs=[vmem] * len(out_shape),
    )(where, right, left)


def pack_kernel(where, here, near, across, both, out):
    mine = (here[...].astype(F32) + near[...].astype(F32)).astype(BF16).T
    other = (across[...].astype(F32) + both[...].astype(F32)).astype(BF16).T
    first = where[1] < 2
    out[0] = jnp.where(first, mine, other)
    out[1] = jnp.where(first, other, mine)


def pack(parts, where):
    rows, cols = parts[0].shape
    vmem = pl.BlockSpec(memory_space=pltpu.VMEM)
    return call(
        pack_kernel,
        out_shape=jax.ShapeDtypeStruct((2, cols, rows), BF16),
        in_specs=[pl.BlockSpec(memory_space=pltpu.SMEM)] + [vmem] * len(parts),
        out_specs=vmem,
    )(where, *parts)


def own_kernel(where, occ_t, columns, own):
    tiles, _, _ = columns.shape
    turned = jnp.concatenate([columns[t] for t in range(tiles)], axis=0).T
    low = lax.rem(where[0], 2) == 0
    mine = jnp.where(low, turned[:BLK, :].astype(F32), turned[BLK:, :].astype(F32))
    row = lax.broadcasted_iota(jnp.int32, (1, tiles * BLK), 1) // BLK
    mask = jnp.zeros((1, tiles * BLK), F32)
    for t in range(tiles):
        mask = jnp.where(row == t, occ_t[where[0], t].astype(F32), mask)
    own[...] = (mine * mask).astype(BF16)


def own_columns(matrix, occupancy, where):
    local_rows, local_cols = matrix.shape
    tiles = local_rows // BLK
    return call(
        own_kernel,
        out_shape=jax.ShapeDtypeStruct((BLK, local_rows), BF16),
        grid_spec=pltpu.PrefetchScalarGridSpec(
            num_scalar_prefetch=2,
            grid=(1,),
            in_specs=[
                pl.BlockSpec((tiles, BLK, LANES), lambda i, where, occ: (0, 0, where[0] // 2))
            ],
            out_specs=pl.BlockSpec((BLK, local_rows), lambda i, where, occ: (0, 0)),
        ),
    )(where, occupancy.T, matrix.reshape(tiles, BLK, local_cols))


def update_kernel(own, got, out):
    depths, lanes = got.shape[0] // 2, got.shape[2]
    low = lax.broadcasted_iota(jnp.int32, (BLK, LANES), 1) < BLK
    for d in range(0, depths, 2):
        for b in range(lanes // LANES):
            span = slice(b * LANES, (b + 1) * LANES)
            one, two = (
                got[d + s, :, span].astype(F32) + got[depths + d + s, :, span].astype(F32)
                for s in (0, 1)
            )
            even = jnp.where(low, one, pltpu.roll(two, BLK, 1))
            odd = jnp.where(low, pltpu.roll(one, BLK, 1), two)
            for a, cube in ((2 * b, even), (2 * b + 1, odd)):
                at = (a * depths + d) * BLK
                value = 1.5 * own[:, at : at + LANES].astype(F32) - 0.5 * cube
                out[:, at : at + LANES] = value.astype(BF16)


def update(own, got):
    return call(update_kernel, out_shape=jax.ShapeDtypeStruct(own.shape, BF16))(own, got)


def shards(matrix, occupancy, filtering):
    rows = lax.axis_size("row")
    depths = lax.axis_size("depth")
    row, col, depth = (lax.axis_index(name) for name in ("row", "col", "depth"))
    local_rows, local_cols = matrix.shape
    own_rows = local_rows // depths
    scale = (local_rows * rows / 2.0) ** (-0.5)
    where = jnp.stack([depth, row, col]).astype(jnp.int32)

    def gather_col(value, groups):
        return lax.all_gather(value, "col", axis=0, tiled=True, axis_index_groups=groups)

    def swap_row(value, bit):
        return lax.ppermute(value, "row", [(r, r ^ bit) for r in range(rows)])

    def trade_x_and_row(value):
        places = [(r, x, z) for r in range(rows) for x in range(RING) for z in range(RING)]
        route = [
            ((r * RING + x) * RING + z, (x * RING + (x + step_along_x(r)) % RING) * RING + z)
            for r, x, z in places
        ]
        return lax.ppermute(value, ("row", "col"), route)

    def parts_of(right):
        [away] = terms_of(right, left, where, scale, own_rows, (1, 3), together=True)
        near, both = swap_row(away, 1)
        across, here = terms_of(right, left, where, scale, own_rows, (2, 0))
        return here, near, across, both

    def parts_added(right):
        [both] = terms_of(right, left, where, scale, own_rows, (3,))
        both = swap_row(both, 1)
        [across] = terms_of(right, left, where, scale, own_rows, (2,))
        across = (across.astype(F32) + both.astype(F32)).astype(BF16)
        across, later = lax.optimization_barrier((across, where))
        across = swap_row(across, 2)
        near, here = terms_of(right, left, later, scale, own_rows, (1, 0))
        across, here = lax.optimization_barrier((across, here))
        return here, across, swap_row(near, 1)

    def trade_over_chip_and_depth(value):
        groups = [
            [r * depths + d for r in (core, core + 2) for d in range(depths)] for core in range(2)
        ]
        return lax.all_to_all(
            value, ("row", "depth"), 0, 0, tiled=True, axis_index_groups=groups
        )

    piece = left_part(matrix, occupancy, depth.astype(jnp.int32)[None], depths)
    moved = trade_x_and_row(piece.astype(F16))
    right = right_part(matrix, occupancy)
    mask = filter_mask(filtering, where, depths, local_rows // BLK, local_cols // BLK)
    own = own_columns(matrix, occupancy, where)
    right, mask, own, moved = lax.optimization_barrier((right, mask, own, moved))
    left = gather_col(gather_col(moved, ALONG_Z), ALONG_X).astype(BF16)

    here, across, near = parts_added(right)
    square = sum(part.astype(F32) for part in (here, across, near)) * mask.astype(F32)
    square = square.astype(BF16).astype(F16)
    squares = lax.all_gather(square, "depth", axis=0).astype(BF16)

    parts = pack(parts_of(squares), where).reshape(2 * depths, BLK, own_rows)
    return update(own, trade_over_chip_and_depth(parts)).T


def solution(mesh):
    placed = (P("row", "col"), P("row", "col"), P())
    return jax.shard_map(
        shards, mesh=mesh, in_specs=placed, out_specs=P("row", ("col", "depth")), check_vma=False
    )
```

```python
import functools

import jax
import jax.numpy as jnp
from jax import lax
from jax.experimental import pallas as pl
from jax.experimental.pallas import tpu as pltpu
from jax.sharding import PartitionSpec as P

BLK = 64
LANES = 128
RING = 4
ALONG_Z = [[x * RING + z for z in range(RING)] for x in range(RING)]
ALONG_X = [[x * RING + z for x in range(RING)] for z in range(RING)]


def stage(lower, upper, rows=4):
    return [
        [row * RING * RING + place for place in group]
        for row in range(rows)
        for group in (lower if row < rows // 2 else upper)
    ]


BF16 = jnp.bfloat16
F32 = jnp.float32
F16 = jnp.float16


def call(kernel, flops=0, moved=1 << 20, vmem=24 << 20, **kwargs):
    return pl.pallas_call(
        kernel,
        compiler_params=pltpu.CompilerParams(vmem_limit_bytes=vmem),
        cost_estimate=pl.CostEstimate(flops=flops, bytes_accessed=moved, transcendentals=0),
        **kwargs,
    )


def spread_tiles(occ_t, cols):
    tiles = occ_t.shape[0]
    tile = lax.broadcasted_iota(jnp.int32, (tiles, cols), 1) // BLK
    spread = (lax.broadcasted_iota(jnp.int32, (tiles, cols), 0) == tile).astype(F32)
    return lax.dot_general(
        occ_t.astype(F32), spread, (((0,), (0,)), ((), ())), preferred_element_type=F32
    )


def left_kernel(where, occ_t, rows, left, table):
    cycles, _, _, cols = rows.shape
    depths = table.shape[0] // cycles
    table[...] = spread_tiles(occ_t[...], cols)
    for a in range(cycles):
        mask = table[pl.ds(a * depths + where[0], 1), :]
        left[a * BLK : (a + 1) * BLK, :] = (rows[a, 0].astype(F32) * mask).astype(BF16)


def left_part(matrix, occupancy, where, depths):
    local_rows, cols = matrix.shape
    cycles = local_rows // (depths * BLK)
    occ_t = occupancy.T
    return call(
        left_kernel,
        vmem=60 << 20,
        out_shape=jax.ShapeDtypeStruct((cycles * BLK, cols), BF16),
        grid_spec=pltpu.PrefetchScalarGridSpec(
            num_scalar_prefetch=1,
            grid=(1,),
            in_specs=[
                pl.BlockSpec(occ_t.shape, lambda i, where: (0, 0)),
                pl.BlockSpec((cycles, 1, BLK, cols), lambda i, where: (0, where[0], 0, 0)),
            ],
            out_specs=pl.BlockSpec((cycles * BLK, cols), lambda i, where: (0, 0)),
            scratch_shapes=[pltpu.VMEM((cycles * depths, cols), F32)],
        ),
    )(where, occ_t, matrix.reshape(cycles, depths, BLK, cols))


def right_kernel(occ_t, rows, right):
    tiles, cols = rows.shape[0] // BLK, rows.shape[1]
    table = spread_tiles(occ_t[...], cols)
    for u in range(tiles):
        part = rows[u * BLK : (u + 1) * BLK, :].astype(F32)
        right[u * BLK : (u + 1) * BLK, :] = (part * table[u : u + 1, :]).astype(BF16)


def right_part(matrix, occupancy):
    return call(
        right_kernel, vmem=30 << 20, out_shape=jax.ShapeDtypeStruct(matrix.shape, BF16)
    )(occupancy.T, matrix)


def filter_kernel(depths, tile_rows, tile_cols, where, filtering, mask):
    rows, cols = mask.shape
    tiles = filtering.shape[0]
    row = lax.broadcasted_iota(jnp.int32, (rows, tiles), 0) // BLK * depths
    of_row = lax.broadcasted_iota(jnp.int32, (rows, tiles), 1) == (
        row + where[1] * tile_rows + where[0]
    )
    col = lax.broadcasted_iota(jnp.int32, (tiles, cols), 1) // BLK + where[2] * tile_cols
    of_col = lax.broadcasted_iota(jnp.int32, (tiles, cols), 0) == col
    spread = jnp.dot(of_row.astype(F32), filtering[...].astype(F32), preferred_element_type=F32)
    mask[...] = jnp.dot(spread, of_col.astype(F32), preferred_element_type=F32).astype(BF16)


def filter_mask(filtering, where, depths, tile_rows, tile_cols):
    shape = (tile_rows // depths * BLK, tile_cols * BLK)
    return call(
        functools.partial(filter_kernel, depths, tile_rows, tile_cols),
        out_shape=jax.ShapeDtypeStruct(shape, BF16),
        grid_spec=pltpu.PrefetchScalarGridSpec(
            num_scalar_prefetch=1,
            grid=(1,),
            in_specs=[pl.BlockSpec(filtering.shape, lambda i, where: (0, 0))],
            out_specs=pl.BlockSpec(shape, lambda i, where: (0, 0)),
        ),
    )(where, filtering)


def step_along_x(row):
    return (row & 1) * 2 + row // 2


def terms_kernel(held, scale, where, right, left, *outs):
    rows, inner = outs[0].shape[-2], left.shape[1]
    total = 0.0
    for a in range(RING):
        lefts = []
        for q in held:
            place = (where[1] + step_along_x(where[1] ^ q)) & (RING - 1)
            place = jnp.where(where[1] < 2, place * RING + a, a * RING + place)
            at = pl.multiple_of(place * rows, rows)
            lefts.append(left[pl.ds(at, rows), :])
        if len(right.shape) == 2:
            part = right[a * inner : (a + 1) * inner, :]
        else:
            part = [right[y, a * BLK : (a + 1) * BLK, :] for y in range(right.shape[0])]
            part = jnp.concatenate(part, axis=0)
        lefts = jnp.concatenate(lefts, axis=0)
        total = total + jnp.dot(lefts, part, preferred_element_type=F32)
    total = (scale * total).astype(BF16)
    for n in range(len(held)):
        part = total[n * rows : (n + 1) * rows]
        if len(outs) == len(held):
            outs[n][...] = part
        else:
            outs[0][n] = part


def terms_of(right, left, where, scale, rows, held, together=False):
    cols = right.shape[-1]
    vmem = pl.BlockSpec(memory_space=pltpu.VMEM)
    out_shape = [jax.ShapeDtypeStruct((rows, cols), BF16)] * len(held)
    if together:
        out_shape = [jax.ShapeDtypeStruct((len(held), rows, cols), BF16)]
    return call(
        functools.partial(terms_kernel, held, scale),
        flops=2 * rows * len(held) * RING * left.shape[1] * cols,
        moved=2 * (right.size + left.size // 2 + rows * len(held) * cols),
        out_shape=out_shape,
        in_specs=[pl.BlockSpec(memory_space=pltpu.SMEM), vmem, vmem],
        out_specs=[vmem] * len(out_shape),
    )(where, right, left)


def pack_kernel(where, here, near, across, both, out):
    mine = (here[...].astype(F32) + near[...].astype(F32)).astype(BF16).T
    other = (across[...].astype(F32) + both[...].astype(F32)).astype(BF16).T
    first = where[1] < 2
    out[0] = jnp.where(first, mine, other)
    out[1] = jnp.where(first, other, mine)


def pack(parts, where):
    rows, cols = parts[0].shape
    vmem = pl.BlockSpec(memory_space=pltpu.VMEM)
    return call(
        pack_kernel,
        out_shape=jax.ShapeDtypeStruct((2, cols, rows), BF16),
        in_specs=[pl.BlockSpec(memory_space=pltpu.SMEM)] + [vmem] * len(parts),
        out_specs=vmem,
    )(where, *parts)


def own_kernel(where, occ_t, columns, own):
    tiles, _, _ = columns.shape
    turned = jnp.concatenate([columns[t] for t in range(tiles)], axis=0).T
    low = lax.rem(where[0], 2) == 0
    mine = jnp.where(low, turned[:BLK, :].astype(F32), turned[BLK:, :].astype(F32))
    row = lax.broadcasted_iota(jnp.int32, (1, tiles * BLK), 1) // BLK
    mask = jnp.zeros((1, tiles * BLK), F32)
    for t in range(tiles):
        mask = jnp.where(row == t, occ_t[where[0], t].astype(F32), mask)
    own[...] = (mine * mask).astype(BF16)


def own_columns(matrix, occupancy, where):
    local_rows, local_cols = matrix.shape
    tiles = local_rows // BLK
    return call(
        own_kernel,
        out_shape=jax.ShapeDtypeStruct((BLK, local_rows), BF16),
        grid_spec=pltpu.PrefetchScalarGridSpec(
            num_scalar_prefetch=2,
            grid=(1,),
            in_specs=[
                pl.BlockSpec((tiles, BLK, LANES), lambda i, where, occ: (0, 0, where[0] // 2))
            ],
            out_specs=pl.BlockSpec((BLK, local_rows), lambda i, where, occ: (0, 0)),
        ),
    )(where, occupancy.T, matrix.reshape(tiles, BLK, local_cols))


def update_kernel(own, got, out):
    depths, lanes = got.shape[0] // 2, got.shape[2]
    low = lax.broadcasted_iota(jnp.int32, (BLK, LANES), 1) < BLK
    for d in range(0, depths, 2):
        for b in range(lanes // LANES):
            span = slice(b * LANES, (b + 1) * LANES)
            one, two = (
                got[d + s, :, span].astype(F32) + got[depths + d + s, :, span].astype(F32)
                for s in (0, 1)
            )
            even = jnp.where(low, one, pltpu.roll(two, BLK, 1))
            odd = jnp.where(low, pltpu.roll(one, BLK, 1), two)
            for a, cube in ((2 * b, even), (2 * b + 1, odd)):
                at = (a * depths + d) * BLK
                value = 1.5 * own[:, at : at + LANES].astype(F32) - 0.5 * cube
                out[:, at : at + LANES] = value.astype(BF16)


def update(own, got):
    return call(update_kernel, out_shape=jax.ShapeDtypeStruct(own.shape, BF16))(own, got)


def shards(matrix, occupancy, filtering):
    rows = lax.axis_size("row")
    depths = lax.axis_size("depth")
    row, col, depth = (lax.axis_index(name) for name in ("row", "col", "depth"))
    local_rows, local_cols = matrix.shape
    own_rows = local_rows // depths
    scale = (local_rows * rows / 2.0) ** (-0.5)
    where = jnp.stack([depth, row, col]).astype(jnp.int32)

    def gather_col(value, groups):
        return lax.all_gather(
            value, ("row", "col"), axis=0, tiled=True, axis_index_groups=groups
        )

    def swap_row(value, bit):
        return lax.ppermute(value, "row", [(r, r ^ bit) for r in range(rows)])

    def trade_x_and_row(value):
        places = [(r, x, z) for r in range(rows) for x in range(RING) for z in range(RING)]
        route = [
            ((r * RING + x) * RING + z, (x * RING + (x + step_along_x(r)) % RING) * RING + z)
            for r, x, z in places
        ]
        return lax.ppermute(value, ("row", "col"), route)

    def parts_of(right):
        [away] = terms_of(right, left, where, scale, own_rows, (1, 3), together=True)
        near, both = swap_row(away, 1)
        across, here = terms_of(right, left, where, scale, own_rows, (2, 0))
        return here, near, across, both

    def parts_added(right):
        [both] = terms_of(right, left, where, scale, own_rows, (3,))
        both = swap_row(both, 1)
        [across] = terms_of(right, left, where, scale, own_rows, (2,))
        across = (across.astype(F32) + both.astype(F32)).astype(BF16)
        across, later = lax.optimization_barrier((across, where))
        across = swap_row(across, 2)
        near, here = terms_of(right, left, later, scale, own_rows, (1, 0))
        across, here = lax.optimization_barrier((across, here))
        return here, across, swap_row(near, 1)

    def trade_over_chip_and_depth(value):
        groups = [
            [r * depths + d for r in (core, core + 2) for d in range(depths)] for core in range(2)
        ]
        return lax.all_to_all(
            value, ("row", "depth"), 0, 0, tiled=True, axis_index_groups=groups
        )

    piece = left_part(matrix, occupancy, depth.astype(jnp.int32)[None], depths)
    moved = trade_x_and_row(piece.astype(F16))
    right = right_part(matrix, occupancy)
    mask = filter_mask(filtering, where, depths, local_rows // BLK, local_cols // BLK)
    own = own_columns(matrix, occupancy, where)
    right, mask, own, moved = lax.optimization_barrier((right, mask, own, moved))
    left = gather_col(moved, stage(ALONG_Z, ALONG_X))
    left = gather_col(left, stage(ALONG_X, ALONG_Z)).astype(BF16)

    here, across, near = parts_added(right)
    square = sum(part.astype(F32) for part in (here, across, near)) * mask.astype(F32)
    square = square.astype(BF16).astype(F16)
    squares = lax.all_gather(square, "depth", axis=0).astype(BF16)

    parts = pack(parts_of(squares), where).reshape(2 * depths, BLK, own_rows)
    return update(own, trade_over_chip_and_depth(parts)).T


def solution(mesh):
    placed = (P("row", "col"), P("row", "col"), P())
    return jax.shard_map(
        shards, mesh=mesh, in_specs=placed, out_specs=P("row", ("col", "depth")), check_vma=False
    )
```

```python
import functools

import jax
import jax.numpy as jnp
from jax import lax
from jax.experimental import pallas as pl
from jax.experimental.pallas import tpu as pltpu
from jax.sharding import PartitionSpec as P

BLK = 64
LANES = 128
RING = 4
ALONG_Z = [[x * RING + z for z in range(RING)] for x in range(RING)]
ALONG_X = [[x * RING + z for x in range(RING)] for z in range(RING)]


def stage(first, second, rows=4):
    return [
        [row * RING * RING + place for place in group]
        for row in range(rows)
        for group in (first if row % 2 == 0 else second)
    ]


BF16 = jnp.bfloat16
F32 = jnp.float32
F16 = jnp.float16


def call(kernel, flops=0, moved=1 << 20, vmem=24 << 20, **kwargs):
    return pl.pallas_call(
        kernel,
        compiler_params=pltpu.CompilerParams(vmem_limit_bytes=vmem),
        cost_estimate=pl.CostEstimate(flops=flops, bytes_accessed=moved, transcendentals=0),
        **kwargs,
    )


def spread_tiles(occ_t, cols):
    tiles = occ_t.shape[0]
    tile = lax.broadcasted_iota(jnp.int32, (tiles, cols), 1) // BLK
    spread = (lax.broadcasted_iota(jnp.int32, (tiles, cols), 0) == tile).astype(F32)
    return lax.dot_general(
        occ_t.astype(F32), spread, (((0,), (0,)), ((), ())), preferred_element_type=F32
    )


def left_kernel(where, occ_t, rows, left, table):
    cycles, _, _, cols = rows.shape
    depths = table.shape[0] // cycles
    table[...] = spread_tiles(occ_t[...], cols)
    for a in range(cycles):
        mask = table[pl.ds(a * depths + where[0], 1), :]
        left[a * BLK : (a + 1) * BLK, :] = (rows[a, 0].astype(F32) * mask).astype(BF16)


def left_part(matrix, occupancy, where, depths):
    local_rows, cols = matrix.shape
    cycles = local_rows // (depths * BLK)
    occ_t = occupancy.T
    return call(
        left_kernel,
        vmem=60 << 20,
        out_shape=jax.ShapeDtypeStruct((cycles * BLK, cols), BF16),
        grid_spec=pltpu.PrefetchScalarGridSpec(
            num_scalar_prefetch=1,
            grid=(1,),
            in_specs=[
                pl.BlockSpec(occ_t.shape, lambda i, where: (0, 0)),
                pl.BlockSpec((cycles, 1, BLK, cols), lambda i, where: (0, where[0], 0, 0)),
            ],
            out_specs=pl.BlockSpec((cycles * BLK, cols), lambda i, where: (0, 0)),
            scratch_shapes=[pltpu.VMEM((cycles * depths, cols), F32)],
        ),
    )(where, occ_t, matrix.reshape(cycles, depths, BLK, cols))


def right_kernel(occ_t, rows, right):
    tiles, cols = rows.shape[0] // BLK, rows.shape[1]
    table = spread_tiles(occ_t[...], cols)
    for u in range(tiles):
        part = rows[u * BLK : (u + 1) * BLK, :].astype(F32)
        right[u * BLK : (u + 1) * BLK, :] = (part * table[u : u + 1, :]).astype(BF16)


def right_part(matrix, occupancy):
    return call(
        right_kernel, vmem=30 << 20, out_shape=jax.ShapeDtypeStruct(matrix.shape, BF16)
    )(occupancy.T, matrix)


def filter_kernel(depths, tile_rows, tile_cols, where, filtering, mask):
    rows, cols = mask.shape
    tiles = filtering.shape[0]
    row = lax.broadcasted_iota(jnp.int32, (rows, tiles), 0) // BLK * depths
    of_row = lax.broadcasted_iota(jnp.int32, (rows, tiles), 1) == (
        row + where[1] * tile_rows + where[0]
    )
    col = lax.broadcasted_iota(jnp.int32, (tiles, cols), 1) // BLK + where[2] * tile_cols
    of_col = lax.broadcasted_iota(jnp.int32, (tiles, cols), 0) == col
    spread = jnp.dot(of_row.astype(F32), filtering[...].astype(F32), preferred_element_type=F32)
    mask[...] = jnp.dot(spread, of_col.astype(F32), preferred_element_type=F32).astype(BF16)


def filter_mask(filtering, where, depths, tile_rows, tile_cols):
    shape = (tile_rows // depths * BLK, tile_cols * BLK)
    return call(
        functools.partial(filter_kernel, depths, tile_rows, tile_cols),
        out_shape=jax.ShapeDtypeStruct(shape, BF16),
        grid_spec=pltpu.PrefetchScalarGridSpec(
            num_scalar_prefetch=1,
            grid=(1,),
            in_specs=[pl.BlockSpec(filtering.shape, lambda i, where: (0, 0))],
            out_specs=pl.BlockSpec(shape, lambda i, where: (0, 0)),
        ),
    )(where, filtering)


def step_along_x(row):
    return (row & 1) * 2 + row // 2


def terms_kernel(held, scale, where, right, left, *outs):
    rows, inner = outs[0].shape[-2], left.shape[1]
    total = 0.0
    for a in range(RING):
        lefts = []
        for q in held:
            place = (where[1] + step_along_x(where[1] ^ q)) & (RING - 1)
            place = jnp.where((where[1] & 1) == 0, place * RING + a, a * RING + place)
            at = pl.multiple_of(place * rows, rows)
            lefts.append(left[pl.ds(at, rows), :])
        if len(right.shape) == 2:
            part = right[a * inner : (a + 1) * inner, :]
        else:
            part = [right[y, a * BLK : (a + 1) * BLK, :] for y in range(right.shape[0])]
            part = jnp.concatenate(part, axis=0)
        lefts = jnp.concatenate(lefts, axis=0)
        total = total + jnp.dot(lefts, part, preferred_element_type=F32)
    total = (scale * total).astype(BF16)
    for n in range(len(held)):
        part = total[n * rows : (n + 1) * rows]
        if len(outs) == len(held):
            outs[n][...] = part
        else:
            outs[0][n] = part


def terms_of(right, left, where, scale, rows, held, together=False):
    cols = right.shape[-1]
    vmem = pl.BlockSpec(memory_space=pltpu.VMEM)
    out_shape = [jax.ShapeDtypeStruct((rows, cols), BF16)] * len(held)
    if together:
        out_shape = [jax.ShapeDtypeStruct((len(held), rows, cols), BF16)]
    return call(
        functools.partial(terms_kernel, held, scale),
        flops=2 * rows * len(held) * RING * left.shape[1] * cols,
        moved=2 * (right.size + left.size // 2 + rows * len(held) * cols),
        out_shape=out_shape,
        in_specs=[pl.BlockSpec(memory_space=pltpu.SMEM), vmem, vmem],
        out_specs=[vmem] * len(out_shape),
    )(where, right, left)


def pack_kernel(where, here, near, across, both, out):
    mine = (here[...].astype(F32) + near[...].astype(F32)).astype(BF16).T
    other = (across[...].astype(F32) + both[...].astype(F32)).astype(BF16).T
    first = where[1] < 2
    out[0] = jnp.where(first, mine, other)
    out[1] = jnp.where(first, other, mine)


def pack(parts, where):
    rows, cols = parts[0].shape
    vmem = pl.BlockSpec(memory_space=pltpu.VMEM)
    return call(
        pack_kernel,
        out_shape=jax.ShapeDtypeStruct((2, cols, rows), BF16),
        in_specs=[pl.BlockSpec(memory_space=pltpu.SMEM)] + [vmem] * len(parts),
        out_specs=vmem,
    )(where, *parts)


def own_kernel(where, occ_t, columns, own):
    tiles, _, _ = columns.shape
    turned = jnp.concatenate([columns[t] for t in range(tiles)], axis=0).T
    low = lax.rem(where[0], 2) == 0
    mine = jnp.where(low, turned[:BLK, :].astype(F32), turned[BLK:, :].astype(F32))
    row = lax.broadcasted_iota(jnp.int32, (1, tiles * BLK), 1) // BLK
    mask = jnp.zeros((1, tiles * BLK), F32)
    for t in range(tiles):
        mask = jnp.where(row == t, occ_t[where[0], t].astype(F32), mask)
    own[...] = (mine * mask).astype(BF16)


def own_columns(matrix, occupancy, where):
    local_rows, local_cols = matrix.shape
    tiles = local_rows // BLK
    return call(
        own_kernel,
        out_shape=jax.ShapeDtypeStruct((BLK, local_rows), BF16),
        grid_spec=pltpu.PrefetchScalarGridSpec(
            num_scalar_prefetch=2,
            grid=(1,),
            in_specs=[
                pl.BlockSpec((tiles, BLK, LANES), lambda i, where, occ: (0, 0, where[0] // 2))
            ],
            out_specs=pl.BlockSpec((BLK, local_rows), lambda i, where, occ: (0, 0)),
        ),
    )(where, occupancy.T, matrix.reshape(tiles, BLK, local_cols))


def update_kernel(own, got, out):
    depths, lanes = got.shape[0] // 2, got.shape[2]
    low = lax.broadcasted_iota(jnp.int32, (BLK, LANES), 1) < BLK
    for d in range(0, depths, 2):
        for b in range(lanes // LANES):
            span = slice(b * LANES, (b + 1) * LANES)
            one, two = (
                got[d + s, :, span].astype(F32) + got[depths + d + s, :, span].astype(F32)
                for s in (0, 1)
            )
            even = jnp.where(low, one, pltpu.roll(two, BLK, 1))
            odd = jnp.where(low, pltpu.roll(one, BLK, 1), two)
            for a, cube in ((2 * b, even), (2 * b + 1, odd)):
                at = (a * depths + d) * BLK
                value = 1.5 * own[:, at : at + LANES].astype(F32) - 0.5 * cube
                out[:, at : at + LANES] = value.astype(BF16)


def update(own, got):
    return call(update_kernel, out_shape=jax.ShapeDtypeStruct(own.shape, BF16))(own, got)


def shards(matrix, occupancy, filtering):
    rows = lax.axis_size("row")
    depths = lax.axis_size("depth")
    row, col, depth = (lax.axis_index(name) for name in ("row", "col", "depth"))
    local_rows, local_cols = matrix.shape
    own_rows = local_rows // depths
    scale = (local_rows * rows / 2.0) ** (-0.5)
    where = jnp.stack([depth, row, col]).astype(jnp.int32)

    def gather_col(value, groups):
        return lax.all_gather(
            value, ("row", "col"), axis=0, tiled=True, axis_index_groups=groups
        )

    def swap_row(value, bit):
        return lax.ppermute(value, "row", [(r, r ^ bit) for r in range(rows)])

    def trade_x_and_row(value):
        places = [(r, x, z) for r in range(rows) for x in range(RING) for z in range(RING)]
        route = [
            ((r * RING + x) * RING + z, (x * RING + (x + step_along_x(r)) % RING) * RING + z)
            for r, x, z in places
        ]
        return lax.ppermute(value, ("row", "col"), route)

    def parts_of(right):
        [away] = terms_of(right, left, where, scale, own_rows, (1, 3), together=True)
        near, both = swap_row(away, 1)
        across, here = terms_of(right, left, where, scale, own_rows, (2, 0))
        return here, near, across, both

    def parts_added(right):
        [both] = terms_of(right, left, where, scale, own_rows, (3,))
        both = swap_row(both, 1)
        [across] = terms_of(right, left, where, scale, own_rows, (2,))
        across = (across.astype(F32) + both.astype(F32)).astype(BF16)
        across, later = lax.optimization_barrier((across, where))
        across = swap_row(across, 2)
        near, here = terms_of(right, left, later, scale, own_rows, (1, 0))
        across, here = lax.optimization_barrier((across, here))
        return here, across, swap_row(near, 1)

    def trade_over_chip_and_depth(value):
        groups = [
            [r * depths + d for r in (core, core + 2) for d in range(depths)] for core in range(2)
        ]
        return lax.all_to_all(
            value, ("row", "depth"), 0, 0, tiled=True, axis_index_groups=groups
        )

    piece = left_part(matrix, occupancy, depth.astype(jnp.int32)[None], depths)
    moved = trade_x_and_row(piece.astype(F16))
    right = right_part(matrix, occupancy)
    mask = filter_mask(filtering, where, depths, local_rows // BLK, local_cols // BLK)
    own = own_columns(matrix, occupancy, where)
    right, mask, own, moved = lax.optimization_barrier((right, mask, own, moved))
    left = gather_col(moved, stage(ALONG_Z, ALONG_X))
    left = gather_col(left, stage(ALONG_X, ALONG_Z)).astype(BF16)

    here, across, near = parts_added(right)
    square = sum(part.astype(F32) for part in (here, across, near)) * mask.astype(F32)
    square = square.astype(BF16).astype(F16)
    squares = lax.all_gather(square, "depth", axis=0).astype(BF16)

    parts = pack(parts_of(squares), where).reshape(2 * depths, BLK, own_rows)
    return update(own, trade_over_chip_and_depth(parts)).T


def solution(mesh):
    placed = (P("row", "col"), P("row", "col"), P())
    return jax.shard_map(
        shards, mesh=mesh, in_specs=placed, out_specs=P("row", ("col", "depth")), check_vma=False
    )
```

```python
import functools

import jax
import jax.numpy as jnp
from jax import lax
from jax.experimental import pallas as pl
from jax.experimental.pallas import tpu as pltpu
from jax.sharding import PartitionSpec as P

BLK = 64
LANES = 128
RING = 4
ALONG_Z = [[x * RING + z for z in range(RING)] for x in range(RING)]
ALONG_X = [[x * RING + z for x in range(RING)] for z in range(RING)]


def stage(first, second, rows=4):
    return [
        [row * RING * RING + place for place in group]
        for row in range(rows)
        for group in (first if row % 2 == 0 else second)
    ]


BF16 = jnp.bfloat16
F32 = jnp.float32
F16 = jnp.float16


def call(kernel, flops=0, moved=1 << 20, vmem=24 << 20, **kwargs):
    return pl.pallas_call(
        kernel,
        compiler_params=pltpu.CompilerParams(vmem_limit_bytes=vmem),
        cost_estimate=pl.CostEstimate(flops=flops, bytes_accessed=moved, transcendentals=0),
        **kwargs,
    )


def spread_tiles(occ_t, cols):
    tiles = occ_t.shape[0]
    tile = lax.broadcasted_iota(jnp.int32, (tiles, cols), 1) // BLK
    spread = (lax.broadcasted_iota(jnp.int32, (tiles, cols), 0) == tile).astype(F32)
    return lax.dot_general(
        occ_t.astype(F32), spread, (((0,), (0,)), ((), ())), preferred_element_type=F32
    )


def left_kernel(where, occ_t, rows, left, table):
    cycles, _, _, cols = rows.shape
    depths = table.shape[0] // cycles
    table[...] = spread_tiles(occ_t[...], cols)
    for a in range(cycles):
        mask = table[pl.ds(a * depths + where[0], 1), :]
        left[a * BLK : (a + 1) * BLK, :] = (rows[a, 0].astype(F32) * mask).astype(BF16)


def left_part(matrix, occupancy, where, depths):
    local_rows, cols = matrix.shape
    cycles = local_rows // (depths * BLK)
    occ_t = occupancy.T
    return call(
        left_kernel,
        vmem=60 << 20,
        out_shape=jax.ShapeDtypeStruct((cycles * BLK, cols), BF16),
        grid_spec=pltpu.PrefetchScalarGridSpec(
            num_scalar_prefetch=1,
            grid=(1,),
            in_specs=[
                pl.BlockSpec(occ_t.shape, lambda i, where: (0, 0)),
                pl.BlockSpec((cycles, 1, BLK, cols), lambda i, where: (0, where[0], 0, 0)),
            ],
            out_specs=pl.BlockSpec((cycles * BLK, cols), lambda i, where: (0, 0)),
            scratch_shapes=[pltpu.VMEM((cycles * depths, cols), F32)],
        ),
    )(where, occ_t, matrix.reshape(cycles, depths, BLK, cols))


def right_kernel(occ_t, rows, right):
    tiles, cols = rows.shape[0] // BLK, rows.shape[1]
    table = spread_tiles(occ_t[...], cols)
    for u in range(tiles):
        part = rows[u * BLK : (u + 1) * BLK, :].astype(F32)
        right[u * BLK : (u + 1) * BLK, :] = (part * table[u : u + 1, :]).astype(BF16)


def right_part(matrix, occupancy):
    return call(
        right_kernel, vmem=30 << 20, out_shape=jax.ShapeDtypeStruct(matrix.shape, BF16)
    )(occupancy.T, matrix)


def filter_kernel(depths, tile_rows, tile_cols, where, filtering, mask):
    rows, cols = mask.shape
    tiles = filtering.shape[0]
    row = lax.broadcasted_iota(jnp.int32, (rows, tiles), 0) // BLK * depths
    of_row = lax.broadcasted_iota(jnp.int32, (rows, tiles), 1) == (
        row + where[1] * tile_rows + where[0]
    )
    col = lax.broadcasted_iota(jnp.int32, (tiles, cols), 1) // BLK + where[2] * tile_cols
    of_col = lax.broadcasted_iota(jnp.int32, (tiles, cols), 0) == col
    spread = jnp.dot(of_row.astype(F32), filtering[...].astype(F32), preferred_element_type=F32)
    mask[...] = jnp.dot(spread, of_col.astype(F32), preferred_element_type=F32).astype(BF16)


def filter_mask(filtering, where, depths, tile_rows, tile_cols):
    shape = (tile_rows // depths * BLK, tile_cols * BLK)
    return call(
        functools.partial(filter_kernel, depths, tile_rows, tile_cols),
        out_shape=jax.ShapeDtypeStruct(shape, BF16),
        grid_spec=pltpu.PrefetchScalarGridSpec(
            num_scalar_prefetch=1,
            grid=(1,),
            in_specs=[pl.BlockSpec(filtering.shape, lambda i, where: (0, 0))],
            out_specs=pl.BlockSpec(shape, lambda i, where: (0, 0)),
        ),
    )(where, filtering)


def step_along_x(row):
    return (row & 1) * 2 + row // 2


def terms_kernel(held, scale, where, right, left, *outs):
    rows, inner = outs[0].shape[-2], left.shape[1]
    total = 0.0
    for a in range(RING):
        lefts = []
        for q in held:
            place = (where[1] + step_along_x(where[1] ^ q)) & (RING - 1)
            place = jnp.where((where[1] & 1) == 0, a * RING + place, place * RING + a)
            at = pl.multiple_of(place * rows, rows)
            lefts.append(left[pl.ds(at, rows), :])
        if len(right.shape) == 2:
            part = right[a * inner : (a + 1) * inner, :]
        else:
            part = [right[y, a * BLK : (a + 1) * BLK, :] for y in range(right.shape[0])]
            part = jnp.concatenate(part, axis=0)
        lefts = jnp.concatenate(lefts, axis=0)
        total = total + jnp.dot(lefts, part, preferred_element_type=F32)
    total = (scale * total).astype(BF16)
    for n in range(len(held)):
        part = total[n * rows : (n + 1) * rows]
        if len(outs) == len(held):
            outs[n][...] = part
        else:
            outs[0][n] = part


def terms_of(right, left, where, scale, rows, held, together=False):
    cols = right.shape[-1]
    vmem = pl.BlockSpec(memory_space=pltpu.VMEM)
    out_shape = [jax.ShapeDtypeStruct((rows, cols), BF16)] * len(held)
    if together:
        out_shape = [jax.ShapeDtypeStruct((len(held), rows, cols), BF16)]
    return call(
        functools.partial(terms_kernel, held, scale),
        flops=2 * rows * len(held) * RING * left.shape[1] * cols,
        moved=2 * (right.size + left.size // 2 + rows * len(held) * cols),
        out_shape=out_shape,
        in_specs=[pl.BlockSpec(memory_space=pltpu.SMEM), vmem, vmem],
        out_specs=[vmem] * len(out_shape),
    )(where, right, left)


def pack_kernel(where, here, near, across, both, out):
    mine = (here[...].astype(F32) + near[...].astype(F32)).astype(BF16).T
    other = (across[...].astype(F32) + both[...].astype(F32)).astype(BF16).T
    first = where[1] < 2
    out[0] = jnp.where(first, mine, other)
    out[1] = jnp.where(first, other, mine)


def pack(parts, where):
    rows, cols = parts[0].shape
    vmem = pl.BlockSpec(memory_space=pltpu.VMEM)
    return call(
        pack_kernel,
        out_shape=jax.ShapeDtypeStruct((2, cols, rows), BF16),
        in_specs=[pl.BlockSpec(memory_space=pltpu.SMEM)] + [vmem] * len(parts),
        out_specs=vmem,
    )(where, *parts)


def own_kernel(where, occ_t, columns, own):
    tiles, _, _ = columns.shape
    turned = jnp.concatenate([columns[t] for t in range(tiles)], axis=0).T
    low = lax.rem(where[0], 2) == 0
    mine = jnp.where(low, turned[:BLK, :].astype(F32), turned[BLK:, :].astype(F32))
    row = lax.broadcasted_iota(jnp.int32, (1, tiles * BLK), 1) // BLK
    mask = jnp.zeros((1, tiles * BLK), F32)
    for t in range(tiles):
        mask = jnp.where(row == t, occ_t[where[0], t].astype(F32), mask)
    own[...] = (mine * mask).astype(BF16)


def own_columns(matrix, occupancy, where):
    local_rows, local_cols = matrix.shape
    tiles = local_rows // BLK
    return call(
        own_kernel,
        out_shape=jax.ShapeDtypeStruct((BLK, local_rows), BF16),
        grid_spec=pltpu.PrefetchScalarGridSpec(
            num_scalar_prefetch=2,
            grid=(1,),
            in_specs=[
                pl.BlockSpec((tiles, BLK, LANES), lambda i, where, occ: (0, 0, where[0] // 2))
            ],
            out_specs=pl.BlockSpec((BLK, local_rows), lambda i, where, occ: (0, 0)),
        ),
    )(where, occupancy.T, matrix.reshape(tiles, BLK, local_cols))


def update_kernel(own, got, out):
    depths, lanes = got.shape[0] // 2, got.shape[2]
    low = lax.broadcasted_iota(jnp.int32, (BLK, LANES), 1) < BLK
    for d in range(0, depths, 2):
        for b in range(lanes // LANES):
            span = slice(b * LANES, (b + 1) * LANES)
            one, two = (
                got[d + s, :, span].astype(F32) + got[depths + d + s, :, span].astype(F32)
                for s in (0, 1)
            )
            even = jnp.where(low, one, pltpu.roll(two, BLK, 1))
            odd = jnp.where(low, pltpu.roll(one, BLK, 1), two)
            for a, cube in ((2 * b, even), (2 * b + 1, odd)):
                at = (a * depths + d) * BLK
                value = 1.5 * own[:, at : at + LANES].astype(F32) - 0.5 * cube
                out[:, at : at + LANES] = value.astype(BF16)


def update(own, got):
    return call(update_kernel, out_shape=jax.ShapeDtypeStruct(own.shape, BF16))(own, got)


def shards(matrix, occupancy, filtering):
    rows = lax.axis_size("row")
    depths = lax.axis_size("depth")
    row, col, depth = (lax.axis_index(name) for name in ("row", "col", "depth"))
    local_rows, local_cols = matrix.shape
    own_rows = local_rows // depths
    scale = (local_rows * rows / 2.0) ** (-0.5)
    where = jnp.stack([depth, row, col]).astype(jnp.int32)

    def gather_col(value, groups):
        return lax.all_gather(
            value, ("row", "col"), axis=0, tiled=True, axis_index_groups=groups
        )

    def swap_row(value, bit):
        return lax.ppermute(value, "row", [(r, r ^ bit) for r in range(rows)])

    def trade_x_and_row(value):
        places = [(r, x, z) for r in range(rows) for x in range(RING) for z in range(RING)]
        route = [
            ((r * RING + x) * RING + z, (x * RING + (x + step_along_x(r)) % RING) * RING + z)
            for r, x, z in places
        ]
        return lax.ppermute(value, ("row", "col"), route)

    def parts_of(right):
        [away] = terms_of(right, left, where, scale, own_rows, (1, 3), together=True)
        near, both = swap_row(away, 1)
        across, here = terms_of(right, left, where, scale, own_rows, (2, 0))
        return here, near, across, both

    def parts_added(right):
        [both] = terms_of(right, left, where, scale, own_rows, (3,))
        both = swap_row(both, 1)
        [across] = terms_of(right, left, where, scale, own_rows, (2,))
        across = (across.astype(F32) + both.astype(F32)).astype(BF16)
        across, later = lax.optimization_barrier((across, where))
        across = swap_row(across, 2)
        near, here = terms_of(right, left, later, scale, own_rows, (1, 0))
        across, here = lax.optimization_barrier((across, here))
        return here, across, swap_row(near, 1)

    def trade_over_chip_and_depth(value):
        groups = [
            [r * depths + d for r in (core, core + 2) for d in range(depths)] for core in range(2)
        ]
        return lax.all_to_all(
            value, ("row", "depth"), 0, 0, tiled=True, axis_index_groups=groups
        )

    piece = left_part(matrix, occupancy, depth.astype(jnp.int32)[None], depths)
    moved = trade_x_and_row(piece.astype(F16))
    right = right_part(matrix, occupancy)
    mask = filter_mask(filtering, where, depths, local_rows // BLK, local_cols // BLK)
    own = own_columns(matrix, occupancy, where)
    right, mask, own, moved = lax.optimization_barrier((right, mask, own, moved))
    left = gather_col(moved, stage(ALONG_X, ALONG_Z))
    left = gather_col(left, stage(ALONG_Z, ALONG_X)).astype(BF16)

    here, across, near = parts_added(right)
    square = sum(part.astype(F32) for part in (here, across, near)) * mask.astype(F32)
    square = square.astype(BF16).astype(F16)
    squares = lax.all_gather(square, "depth", axis=0).astype(BF16)

    parts = pack(parts_of(squares), where).reshape(2 * depths, BLK, own_rows)
    return update(own, trade_over_chip_and_depth(parts)).T


def solution(mesh):
    placed = (P("row", "col"), P("row", "col"), P())
    return jax.shard_map(
        shards, mesh=mesh, in_specs=placed, out_specs=P("row", ("col", "depth")), check_vma=False
    )
```

```python
import functools

import jax
import jax.numpy as jnp
from jax import lax
from jax.experimental import pallas as pl
from jax.experimental.pallas import tpu as pltpu
from jax.sharding import PartitionSpec as P

BLK = 64
LANES = 128
RING = 4
ALONG_Z = [[x * RING + z for z in range(RING)] for x in range(RING)]
ALONG_X = [[x * RING + z for x in range(RING)] for z in range(RING)]


def stage(first, second, rows=4):
    return [
        [row * RING * RING + place for place in group]
        for row in range(rows)
        for group in (first if row % 2 == 0 else second)
    ]


BF16 = jnp.bfloat16
F32 = jnp.float32
F16 = jnp.float16


def call(kernel, flops=0, moved=1 << 20, vmem=24 << 20, **kwargs):
    return pl.pallas_call(
        kernel,
        compiler_params=pltpu.CompilerParams(vmem_limit_bytes=vmem),
        cost_estimate=pl.CostEstimate(flops=flops, bytes_accessed=moved, transcendentals=0),
        **kwargs,
    )


def spread_tiles(occ_t, cols):
    tiles = occ_t.shape[0]
    tile = lax.broadcasted_iota(jnp.int32, (tiles, cols), 1) // BLK
    spread = (lax.broadcasted_iota(jnp.int32, (tiles, cols), 0) == tile).astype(F32)
    return lax.dot_general(
        occ_t.astype(F32), spread, (((0,), (0,)), ((), ())), preferred_element_type=F32
    )


def left_kernel(where, occ_t, rows, left, table):
    cycles, _, _, cols = rows.shape
    depths = table.shape[0] // cycles
    table[...] = spread_tiles(occ_t[...], cols)
    for a in range(cycles):
        mask = table[pl.ds(a * depths + where[0], 1), :]
        left[a * BLK : (a + 1) * BLK, :] = (rows[a, 0].astype(F32) * mask).astype(BF16)


def left_part(matrix, occupancy, where, depths):
    local_rows, cols = matrix.shape
    cycles = local_rows // (depths * BLK)
    occ_t = occupancy.T
    return call(
        left_kernel,
        vmem=60 << 20,
        out_shape=jax.ShapeDtypeStruct((cycles * BLK, cols), BF16),
        grid_spec=pltpu.PrefetchScalarGridSpec(
            num_scalar_prefetch=1,
            grid=(1,),
            in_specs=[
                pl.BlockSpec(occ_t.shape, lambda i, where: (0, 0)),
                pl.BlockSpec((cycles, 1, BLK, cols), lambda i, where: (0, where[0], 0, 0)),
            ],
            out_specs=pl.BlockSpec((cycles * BLK, cols), lambda i, where: (0, 0)),
            scratch_shapes=[pltpu.VMEM((cycles * depths, cols), F32)],
        ),
    )(where, occ_t, matrix.reshape(cycles, depths, BLK, cols))


def right_kernel(occ_t, rows, right):
    tiles, cols = rows.shape[0] // BLK, rows.shape[1]
    table = spread_tiles(occ_t[...], cols)
    for u in range(tiles):
        part = rows[u * BLK : (u + 1) * BLK, :].astype(F32)
        right[u * BLK : (u + 1) * BLK, :] = (part * table[u : u + 1, :]).astype(BF16)


def right_part(matrix, occupancy):
    return call(
        right_kernel, vmem=30 << 20, out_shape=jax.ShapeDtypeStruct(matrix.shape, BF16)
    )(occupancy.T, matrix)


def filter_kernel(depths, tile_rows, tile_cols, where, filtering, mask):
    rows, cols = mask.shape
    tiles = filtering.shape[0]
    row = lax.broadcasted_iota(jnp.int32, (rows, tiles), 0) // BLK * depths
    of_row = lax.broadcasted_iota(jnp.int32, (rows, tiles), 1) == (
        row + where[1] * tile_rows + where[0]
    )
    col = lax.broadcasted_iota(jnp.int32, (tiles, cols), 1) // BLK + where[2] * tile_cols
    of_col = lax.broadcasted_iota(jnp.int32, (tiles, cols), 0) == col
    spread = jnp.dot(of_row.astype(F32), filtering[...].astype(F32), preferred_element_type=F32)
    mask[...] = jnp.dot(spread, of_col.astype(F32), preferred_element_type=F32).astype(BF16)


def filter_mask(filtering, where, depths, tile_rows, tile_cols):
    shape = (tile_rows // depths * BLK, tile_cols * BLK)
    return call(
        functools.partial(filter_kernel, depths, tile_rows, tile_cols),
        out_shape=jax.ShapeDtypeStruct(shape, BF16),
        grid_spec=pltpu.PrefetchScalarGridSpec(
            num_scalar_prefetch=1,
            grid=(1,),
            in_specs=[pl.BlockSpec(filtering.shape, lambda i, where: (0, 0))],
            out_specs=pl.BlockSpec(shape, lambda i, where: (0, 0)),
        ),
    )(where, filtering)


def step_along_x(row):
    return (RING - row) & (RING - 1)


def terms_kernel(held, scale, where, right, left, *outs):
    rows, inner = outs[0].shape[-2], left.shape[1]
    total = 0.0
    for a in range(RING):
        lefts = []
        for q in held:
            place = (where[1] + step_along_x(where[1] ^ q)) & (RING - 1)
            place = jnp.where((where[1] & 1) == 0, place * RING + a, a * RING + place)
            at = pl.multiple_of(place * rows, rows)
            lefts.append(left[pl.ds(at, rows), :])
        if len(right.shape) == 2:
            part = right[a * inner : (a + 1) * inner, :]
        else:
            part = [right[y, a * BLK : (a + 1) * BLK, :] for y in range(right.shape[0])]
            part = jnp.concatenate(part, axis=0)
        lefts = jnp.concatenate(lefts, axis=0)
        total = total + jnp.dot(lefts, part, preferred_element_type=F32)
    total = (scale * total).astype(BF16)
    for n in range(len(held)):
        part = total[n * rows : (n + 1) * rows]
        if len(outs) == len(held):
            outs[n][...] = part
        else:
            outs[0][n] = part


def terms_of(right, left, where, scale, rows, held, together=False):
    cols = right.shape[-1]
    vmem = pl.BlockSpec(memory_space=pltpu.VMEM)
    out_shape = [jax.ShapeDtypeStruct((rows, cols), BF16)] * len(held)
    if together:
        out_shape = [jax.ShapeDtypeStruct((len(held), rows, cols), BF16)]
    return call(
        functools.partial(terms_kernel, held, scale),
        flops=2 * rows * len(held) * RING * left.shape[1] * cols,
        moved=2 * (right.size + left.size // 2 + rows * len(held) * cols),
        out_shape=out_shape,
        in_specs=[pl.BlockSpec(memory_space=pltpu.SMEM), vmem, vmem],
        out_specs=[vmem] * len(out_shape),
    )(where, right, left)


def pack_kernel(where, here, near, across, both, out):
    mine = (here[...].astype(F32) + near[...].astype(F32)).astype(BF16).T
    other = (across[...].astype(F32) + both[...].astype(F32)).astype(BF16).T
    first = where[1] < 2
    out[0] = jnp.where(first, mine, other)
    out[1] = jnp.where(first, other, mine)


def pack(parts, where):
    rows, cols = parts[0].shape
    vmem = pl.BlockSpec(memory_space=pltpu.VMEM)
    return call(
        pack_kernel,
        out_shape=jax.ShapeDtypeStruct((2, cols, rows), BF16),
        in_specs=[pl.BlockSpec(memory_space=pltpu.SMEM)] + [vmem] * len(parts),
        out_specs=vmem,
    )(where, *parts)


def own_kernel(where, occ_t, columns, own):
    tiles, _, _ = columns.shape
    turned = jnp.concatenate([columns[t] for t in range(tiles)], axis=0).T
    low = lax.rem(where[0], 2) == 0
    mine = jnp.where(low, turned[:BLK, :].astype(F32), turned[BLK:, :].astype(F32))
    row = lax.broadcasted_iota(jnp.int32, (1, tiles * BLK), 1) // BLK
    mask = jnp.zeros((1, tiles * BLK), F32)
    for t in range(tiles):
        mask = jnp.where(row == t, occ_t[where[0], t].astype(F32), mask)
    own[...] = (mine * mask).astype(BF16)


def own_columns(matrix, occupancy, where):
    local_rows, local_cols = matrix.shape
    tiles = local_rows // BLK
    return call(
        own_kernel,
        out_shape=jax.ShapeDtypeStruct((BLK, local_rows), BF16),
        grid_spec=pltpu.PrefetchScalarGridSpec(
            num_scalar_prefetch=2,
            grid=(1,),
            in_specs=[
                pl.BlockSpec((tiles, BLK, LANES), lambda i, where, occ: (0, 0, where[0] // 2))
            ],
            out_specs=pl.BlockSpec((BLK, local_rows), lambda i, where, occ: (0, 0)),
        ),
    )(where, occupancy.T, matrix.reshape(tiles, BLK, local_cols))


def update_kernel(own, got, out):
    depths, lanes = got.shape[0] // 2, got.shape[2]
    low = lax.broadcasted_iota(jnp.int32, (BLK, LANES), 1) < BLK
    for d in range(0, depths, 2):
        for b in range(lanes // LANES):
            span = slice(b * LANES, (b + 1) * LANES)
            one, two = (
                got[d + s, :, span].astype(F32) + got[depths + d + s, :, span].astype(F32)
                for s in (0, 1)
            )
            even = jnp.where(low, one, pltpu.roll(two, BLK, 1))
            odd = jnp.where(low, pltpu.roll(one, BLK, 1), two)
            for a, cube in ((2 * b, even), (2 * b + 1, odd)):
                at = (a * depths + d) * BLK
                value = 1.5 * own[:, at : at + LANES].astype(F32) - 0.5 * cube
                out[:, at : at + LANES] = value.astype(BF16)


def update(own, got):
    return call(update_kernel, out_shape=jax.ShapeDtypeStruct(own.shape, BF16))(own, got)


def shards(matrix, occupancy, filtering):
    rows = lax.axis_size("row")
    depths = lax.axis_size("depth")
    row, col, depth = (lax.axis_index(name) for name in ("row", "col", "depth"))
    local_rows, local_cols = matrix.shape
    own_rows = local_rows // depths
    scale = (local_rows * rows / 2.0) ** (-0.5)
    where = jnp.stack([depth, row, col]).astype(jnp.int32)

    def gather_col(value, groups):
        return lax.all_gather(
            value, ("row", "col"), axis=0, tiled=True, axis_index_groups=groups
        )

    def swap_row(value, bit):
        return lax.ppermute(value, "row", [(r, r ^ bit) for r in range(rows)])

    def trade_x_and_row(value):
        places = [(r, x, z) for r in range(rows) for x in range(RING) for z in range(RING)]
        route = [
            ((r * RING + x) * RING + z, (x * RING + (x + step_along_x(r)) % RING) * RING + z)
            for r, x, z in places
        ]
        return lax.ppermute(value, ("row", "col"), route)

    def parts_of(right):
        [away] = terms_of(right, left, where, scale, own_rows, (1, 3), together=True)
        near, both = swap_row(away, 1)
        across, here = terms_of(right, left, where, scale, own_rows, (2, 0))
        return here, near, across, both

    def parts_added(right):
        [both] = terms_of(right, left, where, scale, own_rows, (3,))
        both = swap_row(both, 1)
        [across] = terms_of(right, left, where, scale, own_rows, (2,))
        across = (across.astype(F32) + both.astype(F32)).astype(BF16)
        across, later = lax.optimization_barrier((across, where))
        across = swap_row(across, 2)
        near, here = terms_of(right, left, later, scale, own_rows, (1, 0))
        across, here = lax.optimization_barrier((across, here))
        return here, across, swap_row(near, 1)

    def trade_over_chip_and_depth(value):
        groups = [
            [r * depths + d for r in (core, core + 2) for d in range(depths)] for core in range(2)
        ]
        return lax.all_to_all(
            value, ("row", "depth"), 0, 0, tiled=True, axis_index_groups=groups
        )

    piece = left_part(matrix, occupancy, depth.astype(jnp.int32)[None], depths)
    moved = trade_x_and_row(piece.astype(F16))
    right = right_part(matrix, occupancy)
    mask = filter_mask(filtering, where, depths, local_rows // BLK, local_cols // BLK)
    own = own_columns(matrix, occupancy, where)
    right, mask, own, moved = lax.optimization_barrier((right, mask, own, moved))
    left = gather_col(moved, stage(ALONG_Z, ALONG_X))
    left = gather_col(left, stage(ALONG_X, ALONG_Z)).astype(BF16)

    here, across, near = parts_added(right)
    square = sum(part.astype(F32) for part in (here, across, near)) * mask.astype(F32)
    square = square.astype(BF16).astype(F16)
    squares = lax.all_gather(square, "depth", axis=0).astype(BF16)

    parts = pack(parts_of(squares), where).reshape(2 * depths, BLK, own_rows)
    return update(own, trade_over_chip_and_depth(parts)).T


def solution(mesh):
    placed = (P("row", "col"), P("row", "col"), P())
    return jax.shard_map(
        shards, mesh=mesh, in_specs=placed, out_specs=P("row", ("col", "depth")), check_vma=False
    )
```

```python
import functools

import jax
import jax.numpy as jnp
from jax import lax
from jax.experimental import pallas as pl
from jax.experimental.pallas import tpu as pltpu
from jax.sharding import PartitionSpec as P

BLK = 64
LANES = 128
RING = 4
ALONG_Z = [[x * RING + z for z in range(RING)] for x in range(RING)]
ALONG_X = [[x * RING + z for x in range(RING)] for z in range(RING)]


def stage(first, second, rows=4):
    return [
        [row * RING * RING + place for place in group]
        for row in range(rows)
        for group in (first if row % 2 == 0 else second)
    ]


BF16 = jnp.bfloat16
F32 = jnp.float32
F16 = jnp.float16


def call(kernel, flops=0, moved=1 << 20, vmem=24 << 20, **kwargs):
    return pl.pallas_call(
        kernel,
        compiler_params=pltpu.CompilerParams(vmem_limit_bytes=vmem),
        cost_estimate=pl.CostEstimate(flops=flops, bytes_accessed=moved, transcendentals=0),
        **kwargs,
    )


def spread_tiles(occ_t, cols):
    tiles = occ_t.shape[0]
    tile = lax.broadcasted_iota(jnp.int32, (tiles, cols), 1) // BLK
    spread = (lax.broadcasted_iota(jnp.int32, (tiles, cols), 0) == tile).astype(F32)
    return lax.dot_general(
        occ_t.astype(F32), spread, (((0,), (0,)), ((), ())), preferred_element_type=F32
    )


def left_kernel(where, occ_t, rows, left, table):
    cycles, _, _, cols = rows.shape
    depths = table.shape[0] // cycles
    table[...] = spread_tiles(occ_t[...], cols)
    for a in range(cycles):
        mask = table[pl.ds(a * depths + where[0], 1), :]
        left[a * BLK : (a + 1) * BLK, :] = (rows[a, 0].astype(F32) * mask).astype(BF16)


def left_part(matrix, occupancy, where, depths):
    local_rows, cols = matrix.shape
    cycles = local_rows // (depths * BLK)
    occ_t = occupancy.T
    return call(
        left_kernel,
        vmem=60 << 20,
        out_shape=jax.ShapeDtypeStruct((cycles * BLK, cols), BF16),
        grid_spec=pltpu.PrefetchScalarGridSpec(
            num_scalar_prefetch=1,
            grid=(1,),
            in_specs=[
                pl.BlockSpec(occ_t.shape, lambda i, where: (0, 0)),
                pl.BlockSpec((cycles, 1, BLK, cols), lambda i, where: (0, where[0], 0, 0)),
            ],
            out_specs=pl.BlockSpec((cycles * BLK, cols), lambda i, where: (0, 0)),
            scratch_shapes=[pltpu.VMEM((cycles * depths, cols), F32)],
        ),
    )(where, occ_t, matrix.reshape(cycles, depths, BLK, cols))


def right_kernel(occ_t, rows, right):
    tiles, cols = rows.shape[0] // BLK, rows.shape[1]
    table = spread_tiles(occ_t[...], cols)
    for u in range(tiles):
        part = rows[u * BLK : (u + 1) * BLK, :].astype(F32)
        right[u * BLK : (u + 1) * BLK, :] = (part * table[u : u + 1, :]).astype(BF16)


def right_part(matrix, occupancy):
    return call(
        right_kernel, vmem=30 << 20, out_shape=jax.ShapeDtypeStruct(matrix.shape, BF16)
    )(occupancy.T, matrix)


def filter_kernel(depths, tile_rows, tile_cols, where, filtering, mask):
    rows, cols = mask.shape
    tiles = filtering.shape[0]
    row = lax.broadcasted_iota(jnp.int32, (rows, tiles), 0) // BLK * depths
    of_row = lax.broadcasted_iota(jnp.int32, (rows, tiles), 1) == (
        row + where[1] * tile_rows + where[0]
    )
    col = lax.broadcasted_iota(jnp.int32, (tiles, cols), 1) // BLK + where[2] * tile_cols
    of_col = lax.broadcasted_iota(jnp.int32, (tiles, cols), 0) == col
    spread = jnp.dot(of_row.astype(F32), filtering[...].astype(F32), preferred_element_type=F32)
    mask[...] = jnp.dot(spread, of_col.astype(F32), preferred_element_type=F32).astype(BF16)


def filter_mask(filtering, where, depths, tile_rows, tile_cols):
    shape = (tile_rows // depths * BLK, tile_cols * BLK)
    return call(
        functools.partial(filter_kernel, depths, tile_rows, tile_cols),
        out_shape=jax.ShapeDtypeStruct(shape, BF16),
        grid_spec=pltpu.PrefetchScalarGridSpec(
            num_scalar_prefetch=1,
            grid=(1,),
            in_specs=[pl.BlockSpec(filtering.shape, lambda i, where: (0, 0))],
            out_specs=pl.BlockSpec(shape, lambda i, where: (0, 0)),
        ),
    )(where, filtering)


def step_along_x(row):
    return (row & 1) * 2 + row // 2


def terms_kernel(held, scale, where, right, left, *outs):
    rows, inner = outs[0].shape[-2], left.shape[1]
    total = 0.0
    for a in range(RING):
        lefts = []
        for q in held:
            place = (where[1] + step_along_x(where[1] ^ q)) & (RING - 1)
            place = jnp.where((where[1] & 1) == 0, a * RING + place, place * RING + a)
            at = pl.multiple_of(place * rows, rows)
            lefts.append(left[pl.ds(at, rows), :])
        if len(right.shape) == 2:
            part = right[a * inner : (a + 1) * inner, :]
        else:
            last = (right.shape[0] - 1) * (where[1] & 1)
            part = [
                right[jnp.abs(y - last), a * BLK : (a + 1) * BLK, :] for y in range(right.shape[0])
            ]
            part = jnp.concatenate(part, axis=0)
        lefts = jnp.concatenate(lefts, axis=0)
        total = total + jnp.dot(lefts, part, preferred_element_type=F32)
    total = (scale * total).astype(BF16)
    for n in range(len(held)):
        part = total[n * rows : (n + 1) * rows]
        if len(outs) == len(held):
            outs[n][...] = part
        else:
            outs[0][n] = part


def terms_of(right, left, where, scale, rows, held, together=False):
    cols = right.shape[-1]
    vmem = pl.BlockSpec(memory_space=pltpu.VMEM)
    out_shape = [jax.ShapeDtypeStruct((rows, cols), BF16)] * len(held)
    if together:
        out_shape = [jax.ShapeDtypeStruct((len(held), rows, cols), BF16)]
    return call(
        functools.partial(terms_kernel, held, scale),
        flops=2 * rows * len(held) * RING * left.shape[1] * cols,
        moved=2 * (right.size + left.size // 2 + rows * len(held) * cols),
        out_shape=out_shape,
        in_specs=[pl.BlockSpec(memory_space=pltpu.SMEM), vmem, vmem],
        out_specs=[vmem] * len(out_shape),
    )(where, right, left)


def pack_kernel(where, here, near, across, both, out):
    mine = (here[...].astype(F32) + near[...].astype(F32)).astype(BF16).T
    other = (across[...].astype(F32) + both[...].astype(F32)).astype(BF16).T
    first = where[1] < 2
    out[0] = jnp.where(first, mine, other)
    out[1] = jnp.where(first, other, mine)


def pack(parts, where):
    rows, cols = parts[0].shape
    vmem = pl.BlockSpec(memory_space=pltpu.VMEM)
    return call(
        pack_kernel,
        out_shape=jax.ShapeDtypeStruct((2, cols, rows), BF16),
        in_specs=[pl.BlockSpec(memory_space=pltpu.SMEM)] + [vmem] * len(parts),
        out_specs=vmem,
    )(where, *parts)


def own_kernel(where, occ_t, columns, own):
    tiles, _, _ = columns.shape
    turned = jnp.concatenate([columns[t] for t in range(tiles)], axis=0).T
    low = lax.rem(where[0], 2) == 0
    mine = jnp.where(low, turned[:BLK, :].astype(F32), turned[BLK:, :].astype(F32))
    row = lax.broadcasted_iota(jnp.int32, (1, tiles * BLK), 1) // BLK
    mask = jnp.zeros((1, tiles * BLK), F32)
    for t in range(tiles):
        mask = jnp.where(row == t, occ_t[where[0], t].astype(F32), mask)
    own[...] = (mine * mask).astype(BF16)


def own_columns(matrix, occupancy, where):
    local_rows, local_cols = matrix.shape
    tiles = local_rows // BLK
    return call(
        own_kernel,
        out_shape=jax.ShapeDtypeStruct((BLK, local_rows), BF16),
        grid_spec=pltpu.PrefetchScalarGridSpec(
            num_scalar_prefetch=2,
            grid=(1,),
            in_specs=[
                pl.BlockSpec((tiles, BLK, LANES), lambda i, where, occ: (0, 0, where[0] // 2))
            ],
            out_specs=pl.BlockSpec((BLK, local_rows), lambda i, where, occ: (0, 0)),
        ),
    )(where, occupancy.T, matrix.reshape(tiles, BLK, local_cols))


def update_kernel(own, got, out):
    depths, lanes = got.shape[0] // 2, got.shape[2]
    low = lax.broadcasted_iota(jnp.int32, (BLK, LANES), 1) < BLK
    for d in range(0, depths, 2):
        for b in range(lanes // LANES):
            span = slice(b * LANES, (b + 1) * LANES)
            one, two = (
                got[d + s, :, span].astype(F32) + got[depths + d + s, :, span].astype(F32)
                for s in (0, 1)
            )
            even = jnp.where(low, one, pltpu.roll(two, BLK, 1))
            odd = jnp.where(low, pltpu.roll(one, BLK, 1), two)
            for a, cube in ((2 * b, even), (2 * b + 1, odd)):
                at = (a * depths + d) * BLK
                value = 1.5 * own[:, at : at + LANES].astype(F32) - 0.5 * cube
                out[:, at : at + LANES] = value.astype(BF16)


def update(own, got):
    return call(update_kernel, out_shape=jax.ShapeDtypeStruct(own.shape, BF16))(own, got)


def shards(matrix, occupancy, filtering):
    rows = lax.axis_size("row")
    depths = lax.axis_size("depth")
    row, col, depth = (lax.axis_index(name) for name in ("row", "col", "depth"))
    local_rows, local_cols = matrix.shape
    own_rows = local_rows // depths
    scale = (local_rows * rows / 2.0) ** (-0.5)
    where = jnp.stack([depth, row, col]).astype(jnp.int32)

    def gather_col(value, groups):
        return lax.all_gather(
            value, ("row", "col"), axis=0, tiled=True, axis_index_groups=groups
        )

    def swap_row(value, bit):
        return lax.ppermute(value, "row", [(r, r ^ bit) for r in range(rows)])

    def trade_x_and_row(value):
        places = [(r, x, z) for r in range(rows) for x in range(RING) for z in range(RING)]
        route = [
            ((r * RING + x) * RING + z, (x * RING + (x + step_along_x(r)) % RING) * RING + z)
            for r, x, z in places
        ]
        return lax.ppermute(value, ("row", "col"), route)

    def parts_of(right):
        [away] = terms_of(right, left, where, scale, own_rows, (1, 3), together=True)
        near, both = swap_row(away, 1)
        across, here = terms_of(right, left, where, scale, own_rows, (2, 0))
        return here, near, across, both

    def parts_added(right):
        [both] = terms_of(right, left, where, scale, own_rows, (3,))
        both = swap_row(both, 1)
        [across] = terms_of(right, left, where, scale, own_rows, (2,))
        across = (across.astype(F32) + both.astype(F32)).astype(BF16)
        across, later = lax.optimization_barrier((across, where))
        across = swap_row(across, 2)
        near, here = terms_of(right, left, later, scale, own_rows, (1, 0))
        across, here = lax.optimization_barrier((across, here))
        return here, across, swap_row(near, 1)

    def trade_over_chip_and_depth(value):
        groups = [
            [r * depths + d for r in (core, core + 2) for d in range(depths)] for core in range(2)
        ]
        return lax.all_to_all(
            value, ("row", "depth"), 0, 0, tiled=True, axis_index_groups=groups
        )

    piece = left_part(matrix, occupancy, depth.astype(jnp.int32)[None], depths)
    moved = trade_x_and_row(piece.astype(F16))
    right = right_part(matrix, occupancy)
    mask = filter_mask(filtering, where, depths, local_rows // BLK, local_cols // BLK)
    own = own_columns(matrix, occupancy, where)
    right, mask, own, moved = lax.optimization_barrier((right, mask, own, moved))
    left = gather_col(moved, stage(ALONG_X, ALONG_Z))
    left = gather_col(left, stage(ALONG_Z, ALONG_X)).astype(BF16)

    here, across, near = parts_added(right)
    square = sum(part.astype(F32) for part in (here, across, near)) * mask.astype(F32)
    square = square.astype(BF16).astype(F16)
    groups = [
        [r * depths + (d if r % 2 == 0 else depths - 1 - d) for d in range(depths)]
        for r in range(rows)
    ]
    squares = lax.all_gather(square, ("row", "depth"), axis=0, axis_index_groups=groups)
    squares = squares.astype(BF16)

    parts = pack(parts_of(squares), where).reshape(2 * depths, BLK, own_rows)
    return update(own, trade_over_chip_and_depth(parts)).T


def solution(mesh):
    placed = (P("row", "col"), P("row", "col"), P())
    return jax.shard_map(
        shards, mesh=mesh, in_specs=placed, out_specs=P("row", ("col", "depth")), check_vma=False
    )
```

```python
import functools

import jax
import jax.numpy as jnp
from jax import lax
from jax.experimental import pallas as pl
from jax.experimental.pallas import tpu as pltpu
from jax.sharding import PartitionSpec as P

BLK = 64
LANES = 128
RING = 4
ALONG_Z = [[x * RING + z for z in range(RING)] for x in range(RING)]
ALONG_X = [[x * RING + z for x in range(RING)] for z in range(RING)]


def stage(first, second, rows=4):
    return [
        [row * RING * RING + place for place in group]
        for row in range(rows)
        for group in (first if row in (0, 3) else second)
    ]


BF16 = jnp.bfloat16
F32 = jnp.float32
F16 = jnp.float16


def call(kernel, flops=0, moved=1 << 20, vmem=24 << 20, **kwargs):
    return pl.pallas_call(
        kernel,
        compiler_params=pltpu.CompilerParams(vmem_limit_bytes=vmem),
        cost_estimate=pl.CostEstimate(flops=flops, bytes_accessed=moved, transcendentals=0),
        **kwargs,
    )


def spread_tiles(occ_t, cols):
    tiles = occ_t.shape[0]
    tile = lax.broadcasted_iota(jnp.int32, (tiles, cols), 1) // BLK
    spread = (lax.broadcasted_iota(jnp.int32, (tiles, cols), 0) == tile).astype(F32)
    return lax.dot_general(
        occ_t.astype(F32), spread, (((0,), (0,)), ((), ())), preferred_element_type=F32
    )


def left_kernel(where, occ_t, rows, left, table):
    cycles, _, _, cols = rows.shape
    depths = table.shape[0] // cycles
    table[...] = spread_tiles(occ_t[...], cols)
    for a in range(cycles):
        mask = table[pl.ds(a * depths + where[0], 1), :]
        left[a * BLK : (a + 1) * BLK, :] = (rows[a, 0].astype(F32) * mask).astype(BF16)


def left_part(matrix, occupancy, where, depths):
    local_rows, cols = matrix.shape
    cycles = local_rows // (depths * BLK)
    occ_t = occupancy.T
    return call(
        left_kernel,
        vmem=60 << 20,
        out_shape=jax.ShapeDtypeStruct((cycles * BLK, cols), BF16),
        grid_spec=pltpu.PrefetchScalarGridSpec(
            num_scalar_prefetch=1,
            grid=(1,),
            in_specs=[
                pl.BlockSpec(occ_t.shape, lambda i, where: (0, 0)),
                pl.BlockSpec((cycles, 1, BLK, cols), lambda i, where: (0, where[0], 0, 0)),
            ],
            out_specs=pl.BlockSpec((cycles * BLK, cols), lambda i, where: (0, 0)),
            scratch_shapes=[pltpu.VMEM((cycles * depths, cols), F32)],
        ),
    )(where, occ_t, matrix.reshape(cycles, depths, BLK, cols))


def right_kernel(occ_t, rows, right):
    tiles, cols = rows.shape[0] // BLK, rows.shape[1]
    table = spread_tiles(occ_t[...], cols)
    for u in range(tiles):
        part = rows[u * BLK : (u + 1) * BLK, :].astype(F32)
        right[u * BLK : (u + 1) * BLK, :] = (part * table[u : u + 1, :]).astype(BF16)


def right_part(matrix, occupancy):
    return call(
        right_kernel, vmem=30 << 20, out_shape=jax.ShapeDtypeStruct(matrix.shape, BF16)
    )(occupancy.T, matrix)


def filter_kernel(depths, tile_rows, tile_cols, where, filtering, mask):
    rows, cols = mask.shape
    tiles = filtering.shape[0]
    row = lax.broadcasted_iota(jnp.int32, (rows, tiles), 0) // BLK * depths
    of_row = lax.broadcasted_iota(jnp.int32, (rows, tiles), 1) == (
        row + where[1] * tile_rows + where[0]
    )
    col = lax.broadcasted_iota(jnp.int32, (tiles, cols), 1) // BLK + where[2] * tile_cols
    of_col = lax.broadcasted_iota(jnp.int32, (tiles, cols), 0) == col
    spread = jnp.dot(of_row.astype(F32), filtering[...].astype(F32), preferred_element_type=F32)
    mask[...] = jnp.dot(spread, of_col.astype(F32), preferred_element_type=F32).astype(BF16)


def filter_mask(filtering, where, depths, tile_rows, tile_cols):
    shape = (tile_rows // depths * BLK, tile_cols * BLK)
    return call(
        functools.partial(filter_kernel, depths, tile_rows, tile_cols),
        out_shape=jax.ShapeDtypeStruct(shape, BF16),
        grid_spec=pltpu.PrefetchScalarGridSpec(
            num_scalar_prefetch=1,
            grid=(1,),
            in_specs=[pl.BlockSpec(filtering.shape, lambda i, where: (0, 0))],
            out_specs=pl.BlockSpec(shape, lambda i, where: (0, 0)),
        ),
    )(where, filtering)


def step_along_x(row):
    return (row & 1) * 2 + row // 2


def terms_kernel(held, scale, where, right, left, *outs):
    rows, inner = outs[0].shape[-2], left.shape[1]
    total = 0.0
    for a in range(RING):
        lefts = []
        for q in held:
            place = (where[1] + step_along_x(where[1] ^ q)) & (RING - 1)
            place = jnp.where(((where[1] ^ (where[1] // 2)) & 1) == 0, a * RING + place, place * RING + a)
            at = pl.multiple_of(place * rows, rows)
            lefts.append(left[pl.ds(at, rows), :])
        if len(right.shape) == 2:
            part = right[a * inner : (a + 1) * inner, :]
        else:
            part = [right[y, a * BLK : (a + 1) * BLK, :] for y in range(right.shape[0])]
            part = jnp.concatenate(part, axis=0)
        lefts = jnp.concatenate(lefts, axis=0)
        total = total + jnp.dot(lefts, part, preferred_element_type=F32)
    total = (scale * total).astype(BF16)
    for n in range(len(held)):
        part = total[n * rows : (n + 1) * rows]
        if len(outs) == len(held):
            outs[n][...] = part
        else:
            outs[0][n] = part


def terms_of(right, left, where, scale, rows, held, together=False):
    cols = right.shape[-1]
    vmem = pl.BlockSpec(memory_space=pltpu.VMEM)
    out_shape = [jax.ShapeDtypeStruct((rows, cols), BF16)] * len(held)
    if together:
        out_shape = [jax.ShapeDtypeStruct((len(held), rows, cols), BF16)]
    return call(
        functools.partial(terms_kernel, held, scale),
        flops=2 * rows * len(held) * RING * left.shape[1] * cols,
        moved=2 * (right.size + left.size // 2 + rows * len(held) * cols),
        out_shape=out_shape,
        in_specs=[pl.BlockSpec(memory_space=pltpu.SMEM), vmem, vmem],
        out_specs=[vmem] * len(out_shape),
    )(where, right, left)


def pack_kernel(where, here, near, across, both, out):
    mine = (here[...].astype(F32) + near[...].astype(F32)).astype(BF16).T
    other = (across[...].astype(F32) + both[...].astype(F32)).astype(BF16).T
    first = where[1] < 2
    out[0] = jnp.where(first, mine, other)
    out[1] = jnp.where(first, other, mine)


def pack(parts, where):
    rows, cols = parts[0].shape
    vmem = pl.BlockSpec(memory_space=pltpu.VMEM)
    return call(
        pack_kernel,
        out_shape=jax.ShapeDtypeStruct((2, cols, rows), BF16),
        in_specs=[pl.BlockSpec(memory_space=pltpu.SMEM)] + [vmem] * len(parts),
        out_specs=vmem,
    )(where, *parts)


def own_kernel(where, occ_t, columns, own):
    tiles, _, _ = columns.shape
    turned = jnp.concatenate([columns[t] for t in range(tiles)], axis=0).T
    low = lax.rem(where[0], 2) == 0
    mine = jnp.where(low, turned[:BLK, :].astype(F32), turned[BLK:, :].astype(F32))
    row = lax.broadcasted_iota(jnp.int32, (1, tiles * BLK), 1) // BLK
    mask = jnp.zeros((1, tiles * BLK), F32)
    for t in range(tiles):
        mask = jnp.where(row == t, occ_t[where[0], t].astype(F32), mask)
    own[...] = (mine * mask).astype(BF16)


def own_columns(matrix, occupancy, where):
    local_rows, local_cols = matrix.shape
    tiles = local_rows // BLK
    return call(
        own_kernel,
        out_shape=jax.ShapeDtypeStruct((BLK, local_rows), BF16),
        grid_spec=pltpu.PrefetchScalarGridSpec(
            num_scalar_prefetch=2,
            grid=(1,),
            in_specs=[
                pl.BlockSpec((tiles, BLK, LANES), lambda i, where, occ: (0, 0, where[0] // 2))
            ],
            out_specs=pl.BlockSpec((BLK, local_rows), lambda i, where, occ: (0, 0)),
        ),
    )(where, occupancy.T, matrix.reshape(tiles, BLK, local_cols))


def update_kernel(own, got, out):
    depths, lanes = got.shape[0] // 2, got.shape[2]
    low = lax.broadcasted_iota(jnp.int32, (BLK, LANES), 1) < BLK
    for d in range(0, depths, 2):
        for b in range(lanes // LANES):
            span = slice(b * LANES, (b + 1) * LANES)
            one, two = (
                got[d + s, :, span].astype(F32) + got[depths + d + s, :, span].astype(F32)
                for s in (0, 1)
            )
            even = jnp.where(low, one, pltpu.roll(two, BLK, 1))
            odd = jnp.where(low, pltpu.roll(one, BLK, 1), two)
            for a, cube in ((2 * b, even), (2 * b + 1, odd)):
                at = (a * depths + d) * BLK
                value = 1.5 * own[:, at : at + LANES].astype(F32) - 0.5 * cube
                out[:, at : at + LANES] = value.astype(BF16)


def update(own, got):
    return call(update_kernel, out_shape=jax.ShapeDtypeStruct(own.shape, BF16))(own, got)


def shards(matrix, occupancy, filtering):
    rows = lax.axis_size("row")
    depths = lax.axis_size("depth")
    row, col, depth = (lax.axis_index(name) for name in ("row", "col", "depth"))
    local_rows, local_cols = matrix.shape
    own_rows = local_rows // depths
    scale = (local_rows * rows / 2.0) ** (-0.5)
    where = jnp.stack([depth, row, col]).astype(jnp.int32)

    def gather_col(value, groups):
        return lax.all_gather(
            value, ("row", "col"), axis=0, tiled=True, axis_index_groups=groups
        )

    def swap_row(value, bit):
        return lax.ppermute(value, "row", [(r, r ^ bit) for r in range(rows)])

    def trade_x_and_row(value):
        places = [(r, x, z) for r in range(rows) for x in range(RING) for z in range(RING)]
        route = [
            ((r * RING + x) * RING + z, (x * RING + (x + step_along_x(r)) % RING) * RING + z)
            for r, x, z in places
        ]
        return lax.ppermute(value, ("row", "col"), route)

    def parts_of(right):
        [away] = terms_of(right, left, where, scale, own_rows, (1, 3), together=True)
        near, both = swap_row(away, 1)
        across, here = terms_of(right, left, where, scale, own_rows, (2, 0))
        return here, near, across, both

    def parts_added(right):
        [both] = terms_of(right, left, where, scale, own_rows, (3,))
        both = swap_row(both, 1)
        [across] = terms_of(right, left, where, scale, own_rows, (2,))
        across = (across.astype(F32) + both.astype(F32)).astype(BF16)
        across, later = lax.optimization_barrier((across, where))
        across = swap_row(across, 2)
        near, here = terms_of(right, left, later, scale, own_rows, (1, 0))
        across, here = lax.optimization_barrier((across, here))
        return here, across, swap_row(near, 1)

    def trade_over_chip_and_depth(value):
        groups = [
            [r * depths + d for r in (core, core + 2) for d in range(depths)] for core in range(2)
        ]
        return lax.all_to_all(
            value, ("row", "depth"), 0, 0, tiled=True, axis_index_groups=groups
        )

    piece = left_part(matrix, occupancy, depth.astype(jnp.int32)[None], depths)
    moved = trade_x_and_row(piece.astype(F16))
    right = right_part(matrix, occupancy)
    mask = filter_mask(filtering, where, depths, local_rows // BLK, local_cols // BLK)
    own = own_columns(matrix, occupancy, where)
    right, mask, own, moved = lax.optimization_barrier((right, mask, own, moved))
    left = gather_col(moved, stage(ALONG_X, ALONG_Z))
    left = gather_col(left, stage(ALONG_Z, ALONG_X)).astype(BF16)

    here, across, near = parts_added(right)
    square = sum(part.astype(F32) for part in (here, across, near)) * mask.astype(F32)
    square = square.astype(BF16).astype(F16)
    squares = lax.all_gather(square, "depth", axis=0).astype(BF16)

    parts = pack(parts_of(squares), where).reshape(2 * depths, BLK, own_rows)
    return update(own, trade_over_chip_and_depth(parts)).T


def solution(mesh):
    placed = (P("row", "col"), P("row", "col"), P())
    return jax.shard_map(
        shards, mesh=mesh, in_specs=placed, out_specs=P("row", ("col", "depth")), check_vma=False
    )
```
